32 devices in a mesh: pipe: 2 (over x), dp: 4 (over z), et: 4 (over y, core).
Axes of the slice: x: 2, y: 2, z: 4, core: 2. Of those that a mesh axis runs over, the one named last changes fastest.
Arguments:
- tokens: bfloat16 [2, 4, 64, 3072], P('pipe', 'dp', 'et'), may hold values from -6 to 6
- out_grad: bfloat16 [2, 4, 64, 3072], P('pipe', 'dp', 'et'), may hold values from -6 to 6
- top_ids: int32 [2, 4, 64, 4], P('pipe', 'dp', 'et'), may hold values from 0 to 15, as said below
- route_probs: float32 [2, 4, 64, 4], P('pipe', 'dp', 'et'), may hold values from 0.05 to 0.6
- w_gate: bfloat16 [2, 5376, 3072], P('pipe', ('dp', 'et')), may hold values from -0.109375 to 0.109375
- w_up: bfloat16 [2, 5376, 3072], P('pipe', ('dp', 'et')), may hold values from -0.109375 to 0.109375
- w_down: bfloat16 [2, 5376, 3072], P('pipe', ('dp', 'et')), may hold values from -0.078125 to 0.078125
Outputs:
- handed: bfloat16 [2, 4, 64, 3072], P('pipe', 'dp', 'et')
- grad_gate: bfloat16 [2, 5376, 3072], P('pipe', ('dp', 'et'))
- grad_up: bfloat16 [2, 5376, 3072], P('pipe', ('dp', 'et'))
- grad_down: bfloat16 [2, 5376, 3072], P('pipe', ('dp', 'et'))
The draws below stay inside these ranges and needn't reach their ends.
Inputs may be any that keep to these rules, and one draw needn't show every extreme that they name: `top_ids`: each token names 4 distinct experts. In every group (one section's 64 tokens of one index of dp) at most 32 tokens name expert 0, and in every section some group has exactly 32; every group has at least one.
All inputs are finite; a program needn't handle non-finite values.
Results may differ from the reference program's by a relative error of at most 0.02.
Values may be sent and summed in bfloat16 or wider, within the bound.
No kernel may reach another device: no remote copies, remote signals or barrier semaphores. Data moves between devices by JAX's collectives and lax.ppermute only.
A program may use at most 64 MiB of HBM per device.

```python
import jax
import jax.numpy as jnp
from jax import lax

D = 3072
FF = 5376
EXPERTS = 16
TOP = 4
TOKENS = 64
CAP = 32
N_PIPE = 2
N_DP = 4
N_ET = 4


def draw_top_ids(key, part):
    key = jax.random.fold_in(key, 11)
    keys = jax.random.split(key, 5)
    groups = N_PIPE * N_DP
    counts = jax.random.randint(keys[0], (groups,), 1, CAP + 1)
    fullest = jax.random.randint(keys[1], (N_PIPE,), 0, N_DP)
    forced = jnp.arange(groups) % N_DP == jnp.repeat(fullest, N_DP)
    counts = jnp.where(forced, CAP, counts)
    order = jax.vmap(lambda one: jax.random.permutation(one, TOKENS))(jax.random.split(keys[2], groups))
    picked = order < counts[:, None]
    others = jax.vmap(lambda one: jax.random.permutation(one, EXPERTS - 1))(jax.random.split(keys[3], groups * TOKENS)) + 1
    others = others[:, :TOP].reshape(groups, TOKENS, TOP)
    place = jax.random.randint(keys[4], (groups, TOKENS), 0, TOP)
    matches = jnp.arange(TOP)[None, None, :] == place[:, :, None]
    chosen = jnp.where(matches & picked[:, :, None], 0, others)
    return chosen.reshape(N_PIPE, N_DP, TOKENS, TOP).astype(jnp.int32)


def block_levels(own_key, extent, pieces, smallest, largest):
    gain = 1.0
    for axis_at, blocks in pieces:
        steps = jax.random.uniform(jax.random.fold_in(jax.random.fold_in(own_key, 6), axis_at), (blocks,), jnp.float32, smallest / len(pieces), largest / len(pieces))
        gain = gain * jnp.repeat(jnp.exp(steps), extent[axis_at] // blocks).reshape((-1,) + (1,) * (len(extent) - 1 - axis_at))
    return gain


def scatter_about(key, extent, width, reach, cuts=(), kind=jnp.bfloat16):
    drawn = width * jax.random.normal(key, extent, jnp.float32)
    if cuts:
        drawn = drawn * block_levels(key, extent, cuts, -0.22, 0.18)
    return jnp.clip(drawn, -reach, reach).astype(kind)


def setup_inputs(seed: int = 0) -> dict:
    seeds = jax.random.split(jax.random.key(seed), 8)
    return {
        "tokens": scatter_about(seeds[0], (N_PIPE, N_DP, TOKENS, D), 1.0, 6.0, ((0, 2), (1, 4), (2, 4))),
        "out_grad": scatter_about(seeds[1], (N_PIPE, N_DP, TOKENS, D), 1.0, 6.0, ((0, 2), (1, 4), (2, 4))),
        "top_ids": draw_top_ids(jax.random.fold_in(seeds[7], 71), 0),
        "route_probs": jnp.clip(0.05 + 0.55 * jax.random.uniform(seeds[3], (N_PIPE, N_DP, TOKENS, TOP), jnp.float32) ** block_levels(seeds[3], (N_PIPE, N_DP, TOKENS, TOP), ((0, 2), (1, 4), (2, 4)), -0.2, 0.2), 0.05, 0.6),
        "w_gate": scatter_about(seeds[4], (N_PIPE, FF, D), D ** -0.5, 0.109375, ((0, 2), (1, 16))),
        "w_up": scatter_about(seeds[5], (N_PIPE, FF, D), D ** -0.5, 0.109375, ((0, 2), (1, 16))),
        "w_down": scatter_about(seeds[6], (N_PIPE, FF, D), FF ** -0.5, 0.078125, ((0, 2), (1, 16))),
    }


def slot_layout(routed):
    flags = routed.astype(jnp.int32)
    position = jnp.cumsum(flags, axis=-1, dtype=jnp.int32) - 1
    slot_ids = jnp.arange(CAP, dtype=jnp.int32)
    matches = (position[:, None, :] == slot_ids[None, :, None]) & routed[:, None, :]
    token_ids = jnp.arange(TOKENS, dtype=jnp.int32)
    source = jnp.sum(jnp.where(matches, token_ids[None, None, :], 0), axis=-1).astype(jnp.int32)
    filled = jnp.any(matches, axis=-1)
    return source, filled, position


def gather_slots(rows, source, filled):
    picked = jnp.take_along_axis(rows, source[:, :, None], axis=1)
    return jnp.where(filled[:, :, None], picked, jnp.zeros_like(picked))


def section_backward(operands):
    tokens, out_grad, top_ids, route_probs, w_gate, w_up, w_down = operands
    chosen = top_ids == 0
    routed = jnp.any(chosen, axis=-1)
    route_weight = jnp.sum(jnp.where(chosen, route_probs, jnp.float32(0.0)), axis=-1)
    scaled = (route_weight[:, :, None] * out_grad.astype(jnp.float32)).astype(jnp.bfloat16)
    source, filled, position = slot_layout(routed)
    slot_x = gather_slots(tokens, source, filled).reshape(N_DP * CAP, D)
    slot_dz = gather_slots(scaled, source, filled).reshape(N_DP * CAP, D)
    gate = jnp.dot(slot_x, w_gate.T, preferred_element_type=jnp.float32)
    upper = jnp.dot(slot_x, w_up.T, preferred_element_type=jnp.float32)
    sigmoid_gate = jax.nn.sigmoid(gate)
    silu_gate = gate * sigmoid_gate
    act = (silu_gate * upper).astype(jnp.bfloat16)
    act_grad = jnp.dot(slot_dz, w_down.T, preferred_element_type=jnp.float32)
    gate_grad = (act_grad * upper * sigmoid_gate * (1.0 + gate * (1.0 - sigmoid_gate))).astype(jnp.bfloat16)
    up_grad = (act_grad * silu_gate).astype(jnp.bfloat16)
    grad_down = jnp.dot(act.T, slot_dz, preferred_element_type=jnp.float32).astype(jnp.bfloat16)
    grad_gate = jnp.dot(gate_grad.T, slot_x, preferred_element_type=jnp.float32).astype(jnp.bfloat16)
    grad_up = jnp.dot(up_grad.T, slot_x, preferred_element_type=jnp.float32).astype(jnp.bfloat16)
    piece_width = FF // (N_DP * N_ET)

    def add_piece(running, piece):
        start = piece * piece_width
        part_gate = lax.dynamic_slice_in_dim(gate_grad, start, piece_width, 1)
        part_up = lax.dynamic_slice_in_dim(up_grad, start, piece_width, 1)
        gate_rows = lax.dynamic_slice_in_dim(w_gate, start, piece_width, 0)
        up_rows = lax.dynamic_slice_in_dim(w_up, start, piece_width, 0)
        term = jnp.dot(part_gate, gate_rows, preferred_element_type=jnp.float32)
        term = term + jnp.dot(part_up, up_rows, preferred_element_type=jnp.float32)
        term = lax.optimization_barrier(term.astype(jnp.bfloat16)).astype(jnp.float32)
        return running + term, None

    summed, unused = lax.scan(add_piece, jnp.zeros((N_DP * CAP, D), jnp.float32),
                              jnp.arange(N_DP * N_ET, dtype=jnp.int32))
    slot_grad = summed.astype(jnp.bfloat16).reshape(N_DP, CAP, D)
    picked = jnp.take_along_axis(slot_grad, jnp.maximum(position, 0)[:, :, None], axis=1)
    input_grad = jnp.where(routed[:, :, None], picked, jnp.zeros_like(picked))
    return input_grad, grad_gate, grad_up, grad_down


def reference(tokens, out_grad, top_ids, route_probs, w_gate, w_up, w_down):
    input_grad, grad_gate, grad_up, grad_down = lax.map(
        section_backward, (tokens, out_grad, top_ids, route_probs, w_gate, w_up, w_down))
    handed = jnp.roll(input_grad, -1, axis=0)
    return (handed, grad_gate, grad_up, grad_down)
```

```python
import functools

import jax
import jax.numpy as jnp
from jax import lax
from jax.experimental import pallas as pl
from jax.experimental.pallas import tpu as pltpu
from jax.sharding import PartitionSpec as P

FLAG = 128
BF16 = jnp.bfloat16
F32 = jnp.float32
VMEM = pl.BlockSpec(memory_space=pltpu.VMEM)
HBM = pl.BlockSpec(memory_space=pltpu.HBM)


def from_behind(value, axis, steps):
    count = lax.axis_size(axis)
    pairs = [(source, (source + steps) % count) for source in range(count)]
    return lax.ppermute(value, axis, pairs)


def slot_layout(routed, capacity):
    flags = routed.astype(jnp.int32)
    position = jnp.cumsum(flags, axis=-1, dtype=jnp.int32) - 1
    slot_ids = jnp.arange(capacity, dtype=jnp.int32)
    matches = (position[:, None, :] == slot_ids[None, :, None]) & routed[:, None, :]
    token_ids = jnp.arange(routed.shape[-1], dtype=jnp.int32)
    source = jnp.sum(jnp.where(matches, token_ids[None, None, :], 0), axis=-1)
    filled = jnp.any(matches, axis=-1)
    return (source, filled, position)


def gather_slots(rows, source, filled):
    picked = jnp.take_along_axis(rows, source[:, :, None], axis=1)
    return jnp.where(filled[:, :, None], picked, jnp.zeros_like(picked))


def contract(left, right, left_dim, right_dim):
    return lax.dot_general(
        left, right, (((left_dim,), (right_dim,)), ((), ())), preferred_element_type=F32
    )


def on_device_any(tokens, out_grad, top_ids, route_probs, w_gate, w_up, w_down):
    tok_dev = tokens.shape[2]
    model_width = tokens.shape[3]
    et_size = lax.axis_size("et")
    dp_size = lax.axis_size("dp")
    group_tokens = tok_dev * et_size
    capacity = group_tokens // 2
    token_rows = tokens[0, 0]
    chosen = top_ids[0, 0] == 0
    routed_flag = jnp.any(chosen, axis=-1).astype(BF16)
    route_weight = jnp.sum(jnp.where(chosen, route_probs[0, 0], F32(0.0)), axis=-1)
    scaled_rows = (route_weight[:, None] * out_grad[0, 0].astype(F32)).astype(BF16)
    group_x, group_dz, group_flag = (
        lax.all_gather(token_rows, "et", axis=0, tiled=True),
        lax.all_gather(scaled_rows, "et", axis=0, tiled=True),
        lax.all_gather(routed_flag, "et", axis=0, tiled=True),
    )
    routed = group_flag[None, :] > 0
    source, filled, position = slot_layout(routed, capacity)
    own_x = gather_slots(group_x[None], source, filled)
    own_dz = gather_slots(group_dz[None], source, filled)
    all_x, all_dz = (
        lax.all_gather(own_x, "dp", axis=0, tiled=True),
        lax.all_gather(own_dz, "dp", axis=0, tiled=True),
    )
    own_position = position[0]
    own_routed = routed[0]
    slot_x = all_x.reshape(dp_size * capacity, model_width)
    slot_dz = all_dz.reshape(dp_size * capacity, model_width)
    gate_rows = w_gate[0]
    up_rows = w_up[0]
    down_rows = w_down[0]
    gate = contract(slot_x, gate_rows, 1, 1)
    upper = contract(slot_x, up_rows, 1, 1)
    sigmoid_gate = jax.nn.sigmoid(gate)
    silu_gate = gate * sigmoid_gate
    act = (silu_gate * upper).astype(BF16)
    act_grad = contract(slot_dz, down_rows, 1, 1)
    gate_grad = (act_grad * upper * sigmoid_gate * (1.0 + gate * (1.0 - sigmoid_gate))).astype(BF16)
    up_grad = (act_grad * silu_gate).astype(BF16)
    grad_down = contract(act, slot_dz, 0, 0).astype(BF16)
    grad_gate = contract(gate_grad, slot_x, 0, 0).astype(BF16)
    grad_up = contract(up_grad, slot_x, 0, 0).astype(BF16)
    hidden_terms = contract(gate_grad, gate_rows, 1, 0) + contract(up_grad, up_rows, 1, 0)
    rounded = hidden_terms.astype(BF16).reshape(dp_size, capacity, model_width)
    hidden_sum = lax.psum_scatter(rounded, "et", scatter_dimension=1, tiled=True)
    slot_share = lax.psum_scatter(hidden_sum, "dp", scatter_dimension=0, tiled=True)
    slot_grad = lax.all_gather(slot_share, "et", axis=1, tiled=True)[0]
    start = lax.axis_index("et") * tok_dev
    my_position = lax.dynamic_slice_in_dim(own_position, start, tok_dev)
    my_routed = lax.dynamic_slice_in_dim(own_routed, start, tok_dev)
    picked = jnp.take(slot_grad, jnp.maximum(my_position, 0), axis=0)
    input_grad = jnp.where(my_routed[:, None], picked, jnp.zeros_like(picked))
    handed = from_behind(input_grad[None, None], "pipe", -1)
    return (handed, grad_gate[None], grad_up[None], grad_down[None])


def call(kernel, outs, *args, scratch=(), flops=0, vmem=16, space=VMEM):
    moved = sum(a.size * a.dtype.itemsize for a in args)
    moved += sum(o.size * o.dtype.itemsize for o in outs)
    if space is HBM:
        args = [pltpu.with_memory_space_constraint(a, pltpu.HBM) for a in args]
    return pl.pallas_call(
        kernel,
        out_shape=outs,
        in_specs=[space] * len(args),
        out_specs=[VMEM] * len(outs),
        scratch_shapes=list(scratch),
        compiler_params=pltpu.CompilerParams(vmem_limit_bytes=vmem * 2**20),
        cost_estimate=pl.CostEstimate(flops=flops, bytes_accessed=moved, transcendentals=0),
    )(*args)


def like(shape, dtype=BF16):
    return jax.ShapeDtypeStruct(shape, dtype)


def spread(steps):
    return [(e, e ^ steps) for e in range(4)]


def bring(sources, targets, sems):
    copies = [
        pltpu.make_async_copy(source, target, sems.at[i])
        for i, (source, target) in enumerate(zip(sources, targets))
    ]
    for copy in copies:
        copy.start()
    return copies


def stage_kernel(*refs):
    count = len(refs) // 2
    for copy in bring(refs[:count], refs[count : 2 * count], refs[-1]):
        copy.wait()


def pack_kernel(*refs):
    outs, (x_ref, dz_ref, ids_ref, probs_ref, sems) = refs[4:8], refs[8:]
    for copy in bring(refs[:4], refs[8:12], sems):
        copy.wait()
    rows, width = x_ref.shape
    piece = width // 4
    e = lax.axis_index("et")
    chosen = ids_ref[...] == 0
    weight_row = jnp.sum(jnp.where(chosen, probs_ref[...], 0.0), axis=0, keepdims=True)
    flag_row = jnp.max(jnp.where(chosen, 1.0, 0.0), axis=0, keepdims=True)
    on_diagonal = lax.broadcasted_iota(jnp.int32, (rows, rows), 0) == lax.broadcasted_iota(
        jnp.int32, (rows, rows), 1
    )
    weight = jnp.sum(jnp.where(on_diagonal, weight_row, 0.0), axis=1, keepdims=True)
    flag = jnp.sum(jnp.where(on_diagonal, flag_row, 0.0), axis=1, keepdims=True)
    for steps, out in enumerate(outs):
        start = pl.multiple_of((e ^ steps) * piece, 128)
        out[:, :piece] = x_ref[:, pl.ds(start, piece)]
        out[:, piece : 2 * piece] = (weight * dz_ref[:, pl.ds(start, piece)].astype(F32)).astype(BF16)
        out[:, 2 * piece :] = jnp.broadcast_to(flag, (rows, FLAG)).astype(BF16)


def compact_kernel(*refs):
    parts, (slots_ref, pick_ref, all_rows) = refs[:4], refs[4:]
    rows, wide = parts[0].shape
    tokens = 4 * rows
    data = wide - FLAG
    cap = slots_ref.shape[0]
    e = lax.axis_index("et")
    for steps, part in enumerate(parts):
        all_rows[pl.ds(pl.multiple_of((e ^ steps) * rows, 16), rows), :] = part[...]
    flags = all_rows[:, data:]
    before = lax.broadcasted_iota(jnp.int32, (tokens, tokens), 0)
    after = lax.broadcasted_iota(jnp.int32, (tokens, tokens), 1)
    count = contract(flags, (before <= after).astype(F32).astype(BF16), 0, 0)[:cap]
    here = contract(flags, (before == after).astype(F32).astype(BF16), 0, 0)[:cap]
    slot = lax.broadcasted_iota(jnp.int32, (cap, tokens), 0).astype(F32)
    pick = jnp.where((count - 1.0 == slot) & (here > 0.5), 1.0, 0.0).astype(BF16)
    slots_ref[...] = jnp.dot(pick, all_rows[:, :data], preferred_element_type=F32).astype(BF16)
    pick_ref[...] = pick


def expert_kernel(*refs):
    blocks, (wg_ref, wu_ref, wd_ref), outs = refs[:16], refs[16:19], refs[19:]
    x_ref, dz_ref, act_ref, gg_ref, ug_ref, own_ref, other_ref = outs
    cap, wide = blocks[0].shape
    piece = wide // 2
    half = wide
    e = lax.axis_index("et")
    for steps in range(4):
        start = pl.multiple_of((e ^ steps) * piece, 128)
        for k in range(4):
            block = blocks[4 * steps + k]
            rows = pl.ds(k * cap, cap)
            x_ref[rows, pl.ds(start, piece)] = block[:, :piece]
            dz_ref[rows, pl.ds(start, piece)] = block[:, piece:]
    gate = contract(x_ref[...], wg_ref[...], 1, 1)
    upper = contract(x_ref[...], wu_ref[...], 1, 1)
    act_grad = contract(dz_ref[...], wd_ref[...], 1, 1)
    sigmoid_gate = jax.nn.sigmoid(gate)
    silu_gate = gate * sigmoid_gate
    act_ref[...] = (silu_gate * upper).astype(BF16)
    gg_ref[...] = (act_grad * upper * sigmoid_gate * (1.0 + gate * (1.0 - sigmoid_gate))).astype(BF16)
    ug_ref[...] = (act_grad * silu_gate).astype(BF16)
    core = e % 2
    for out, side in ((other_ref, 1 - core), (own_ref, core)):
        start = pl.multiple_of(side * half, 128)
        terms = contract(gg_ref[...], wg_ref[:, pl.ds(start, half)], 1, 0)
        terms += contract(ug_ref[...], wu_ref[:, pl.ds(start, half)], 1, 0)
        out[...] = terms.astype(BF16)


def pair_kernel(own_ref, other_ref, *outs):
    cap = outs[0].shape[0]
    for k, out in enumerate(outs):
        rows = pl.ds(k * cap, cap)
        out[...] = (own_ref[rows, :].astype(F32) + other_ref[rows, :].astype(F32)).astype(BF16)


def add_kernel(left_ref, right_ref, out_ref):
    out_ref[...] = (left_ref[...].astype(F32) + right_ref[...].astype(F32)).astype(BF16)


def expand_kernel(own_ref, near_ref, far_ref, pick_ref, *refs):
    outs, tokens_ref = refs[:4], refs[4]
    rows = outs[0].shape[0]
    e = lax.axis_index("et")
    total = own_ref[...].astype(F32) + near_ref[...].astype(F32) + far_ref[...].astype(F32)
    tokens_ref[...] = contract(pick_ref[...], total.astype(BF16), 0, 0).astype(BF16)
    for steps, out in enumerate(outs):
        out[...] = tokens_ref[pl.ds(pl.multiple_of((e ^ steps) * rows, 16), rows), :]


def finish_kernel(own_ref, core_ref, chip_ref, both_ref, out_ref):
    half = own_ref.shape[1]
    core = lax.axis_index("et") % 2
    mine = own_ref[...].astype(F32) + chip_ref[...].astype(F32)
    out_ref[:, pl.ds(pl.multiple_of(core * half, 128), half)] = mine.astype(BF16)
    theirs = core_ref[...].astype(F32) + both_ref[...].astype(F32)
    out_ref[:, pl.ds(pl.multiple_of((1 - core) * half, 128), half)] = theirs.astype(BF16)


def swap(value, axis, steps):
    return lax.ppermute(value, axis, spread(steps))


def on_device_four(tokens, out_grad, top_ids, route_probs, w_gate, w_up, w_down):
    rows, width = tokens.shape[2:]
    hidden = w_gate.shape[1]
    top = top_ids.shape[3]
    pipe_size = lax.axis_size("pipe")
    cap = 2 * rows
    slots = 4 * cap
    piece, half = width // 4, width // 2

    packed = call(
        pack_kernel,
        [like((rows, 2 * piece + FLAG))] * 4,
        tokens[0, 0],
        out_grad[0, 0],
        top_ids[0, 0].T,
        route_probs[0, 0].T,
        scratch=[
            pltpu.VMEM((rows, width), BF16),
            pltpu.VMEM((rows, width), BF16),
            pltpu.VMEM((top, rows), jnp.int32),
            pltpu.VMEM((top, rows), F32),
            pltpu.SemaphoreType.DMA((4,)),
        ],
        space=HBM,
    )
    arrived = [packed[0]] + [swap(packed[s], "et", s) for s in (1, 2, 3)]
    wg, wu, wd = call(
        stage_kernel,
        [like((hidden, width))] * 3,
        w_gate[0],
        w_up[0],
        w_down[0],
        scratch=[pltpu.SemaphoreType.DMA((3,))],
        space=HBM,
    )
    slot_block, pick = call(
        compact_kernel,
        [like((cap, 2 * piece)), like((cap, 4 * rows))],
        *arrived,
        scratch=[pltpu.VMEM((4 * rows, 2 * piece + FLAG), BF16)],
    )
    near = swap(slot_block, "dp", 1)
    far = swap(slot_block, "dp", 2)
    chip_own = swap(slot_block, "et", 2)
    near, far, chip_own, wg, wu, wd = lax.optimization_barrier((near, far, chip_own, wg, wu, wd))
    last = swap(far, "dp", 1)
    own = [slot_block, near, far, last]
    chip = [chip_own] + [swap(block, "et", 2) for block in own[1:]]
    core = [swap(block, "et", 1) for block in own]
    both = [swap(block, "et", 1) for block in chip]
    x, dz, act, gate_grad, up_grad, terms, away = call(
        expert_kernel,
        [like((slots, width))] * 2 + [like((slots, hidden))] * 3 + [like((slots, half))] * 2,
        *own,
        *core,
        *chip,
        *both,
        wg,
        wu,
        wd,
        flops=10 * slots * hidden * width,
        vmem=32,
    )
    theirs = swap(away, "et", 1)
    home, to_near, to_far, to_last = call(
        pair_kernel, [like((cap, half))] * 4, terms, theirs
    )
    (to_far,) = call(add_kernel, [like((cap, half))], to_far, swap(to_last, "dp", 1))
    by_token = call(
        expand_kernel,
        [like((rows, half))] * 4,
        home,
        swap(to_near, "dp", 1),
        swap(to_far, "dp", 2),
        pick,
        scratch=[pltpu.VMEM((4 * rows, half), BF16)],
    )
    back = []
    for s in range(4):
        pairs = [
            (4 * p + e, 4 * ((p - 1) % pipe_size) + (e ^ s))
            for p in range(pipe_size)
            for e in range(4)
        ]
        back.append(lax.ppermute(by_token[s], ("pipe", "et"), pairs))
    (handed,) = call(finish_kernel, [like((rows, width))], *back)
    grad_down = contract(act, dz, 0, 0).astype(BF16)
    grad_gate = contract(gate_grad, x, 0, 0).astype(BF16)
    grad_up = contract(up_grad, x, 0, 0).astype(BF16)
    return (handed[None, None], grad_gate[None], grad_up[None], grad_down[None])


def solution(mesh):
    placed = (
        P("pipe", "dp", "et", None),
        P("pipe", "dp", "et", None),
        P("pipe", "dp", "et", None),
        P("pipe", "dp", "et", None),
        P("pipe", ("dp", "et"), None),
        P("pipe", ("dp", "et"), None),
        P("pipe", ("dp", "et"), None),
    )
    four = mesh.shape["et"] == 4 and mesh.shape["dp"] == 4
    return jax.shard_map(
        on_device_four if four else on_device_any,
        mesh=mesh,
        in_specs=placed,
        out_specs=(
            P("pipe", "dp", "et", None),
            P("pipe", ("dp", "et"), None),
            P("pipe", ("dp", "et"), None),
            P("pipe", ("dp", "et"), None),
        ),
        check_vma=False,
    )
```

```python
import functools

import jax
import jax.numpy as jnp
from jax import lax
from jax.experimental import pallas as pl
from jax.experimental.pallas import tpu as pltpu
from jax.sharding import PartitionSpec as P

FLAG = 128
BF16 = jnp.bfloat16
F32 = jnp.float32
VMEM = pl.BlockSpec(memory_space=pltpu.VMEM)
HBM = pl.BlockSpec(memory_space=pltpu.HBM)


def from_behind(value, axis, steps):
    count = lax.axis_size(axis)
    pairs = [(source, (source + steps) % count) for source in range(count)]
    return lax.ppermute(value, axis, pairs)


def slot_layout(routed, capacity):
    flags = routed.astype(jnp.int32)
    position = jnp.cumsum(flags, axis=-1, dtype=jnp.int32) - 1
    slot_ids = jnp.arange(capacity, dtype=jnp.int32)
    matches = (position[:, None, :] == slot_ids[None, :, None]) & routed[:, None, :]
    token_ids = jnp.arange(routed.shape[-1], dtype=jnp.int32)
    source = jnp.sum(jnp.where(matches, token_ids[None, None, :], 0), axis=-1)
    filled = jnp.any(matches, axis=-1)
    return (source, filled, position)


def gather_slots(rows, source, filled):
    picked = jnp.take_along_axis(rows, source[:, :, None], axis=1)
    return jnp.where(filled[:, :, None], picked, jnp.zeros_like(picked))


def contract(left, right, left_dim, right_dim):
    return lax.dot_general(
        left, right, (((left_dim,), (right_dim,)), ((), ())), preferred_element_type=F32
    )


def on_device_any(tokens, out_grad, top_ids, route_probs, w_gate, w_up, w_down):
    tok_dev = tokens.shape[2]
    model_width = tokens.shape[3]
    et_size = lax.axis_size("et")
    dp_size = lax.axis_size("dp")
    group_tokens = tok_dev * et_size
    capacity = group_tokens // 2
    token_rows = tokens[0, 0]
    chosen = top_ids[0, 0] == 0
    routed_flag = jnp.any(chosen, axis=-1).astype(BF16)
    route_weight = jnp.sum(jnp.where(chosen, route_probs[0, 0], F32(0.0)), axis=-1)
    scaled_rows = (route_weight[:, None] * out_grad[0, 0].astype(F32)).astype(BF16)
    group_x, group_dz, group_flag = (
        lax.all_gather(token_rows, "et", axis=0, tiled=True),
        lax.all_gather(scaled_rows, "et", axis=0, tiled=True),
        lax.all_gather(routed_flag, "et", axis=0, tiled=True),
    )
    routed = group_flag[None, :] > 0
    source, filled, position = slot_layout(routed, capacity)
    own_x = gather_slots(group_x[None], source, filled)
    own_dz = gather_slots(group_dz[None], source, filled)
    all_x, all_dz = (
        lax.all_gather(own_x, "dp", axis=0, tiled=True),
        lax.all_gather(own_dz, "dp", axis=0, tiled=True),
    )
    own_position = position[0]
    own_routed = routed[0]
    slot_x = all_x.reshape(dp_size * capacity, model_width)
    slot_dz = all_dz.reshape(dp_size * capacity, model_width)
    gate_rows = w_gate[0]
    up_rows = w_up[0]
    down_rows = w_down[0]
    gate = contract(slot_x, gate_rows, 1, 1)
    upper = contract(slot_x, up_rows, 1, 1)
    sigmoid_gate = jax.nn.sigmoid(gate)
    silu_gate = gate * sigmoid_gate
    act = (silu_gate * upper).astype(BF16)
    act_grad = contract(slot_dz, down_rows, 1, 1)
    gate_grad = (act_grad * upper * sigmoid_gate * (1.0 + gate * (1.0 - sigmoid_gate))).astype(BF16)
    up_grad = (act_grad * silu_gate).astype(BF16)
    grad_down = contract(act, slot_dz, 0, 0).astype(BF16)
    grad_gate = contract(gate_grad, slot_x, 0, 0).astype(BF16)
    grad_up = contract(up_grad, slot_x, 0, 0).astype(BF16)
    hidden_terms = contract(gate_grad, gate_rows, 1, 0) + contract(up_grad, up_rows, 1, 0)
    rounded = hidden_terms.astype(BF16).reshape(dp_size, capacity, model_width)
    hidden_sum = lax.psum_scatter(rounded, "et", scatter_dimension=1, tiled=True)
    slot_share = lax.psum_scatter(hidden_sum, "dp", scatter_dimension=0, tiled=True)
    slot_grad = lax.all_gather(slot_share, "et", axis=1, tiled=True)[0]
    start = lax.axis_index("et") * tok_dev
    my_position = lax.dynamic_slice_in_dim(own_position, start, tok_dev)
    my_routed = lax.dynamic_slice_in_dim(own_routed, start, tok_dev)
    picked = jnp.take(slot_grad, jnp.maximum(my_position, 0), axis=0)
    input_grad = jnp.where(my_routed[:, None], picked, jnp.zeros_like(picked))
    handed = from_behind(input_grad[None, None], "pipe", -1)
    return (handed, grad_gate[None], grad_up[None], grad_down[None])


def call(kernel, outs, *args, scratch=(), flops=0, vmem=16, space=VMEM):
    moved = sum(a.size * a.dtype.itemsize for a in args)
    moved += sum(o.size * o.dtype.itemsize for o in outs)
    if space is HBM:
        args = [pltpu.with_memory_space_constraint(a, pltpu.HBM) for a in args]
    return pl.pallas_call(
        kernel,
        out_shape=outs,
        in_specs=[space] * len(args),
        out_specs=[VMEM] * len(outs),
        scratch_shapes=list(scratch),
        compiler_params=pltpu.CompilerParams(vmem_limit_bytes=vmem * 2**20),
        cost_estimate=pl.CostEstimate(flops=flops, bytes_accessed=moved, transcendentals=0),
    )(*args)


def like(shape, dtype=BF16):
    return jax.ShapeDtypeStruct(shape, dtype)


def spread(steps):
    return [(e, e ^ steps) for e in range(4)]


def bring(sources, targets, sems):
    copies = [
        pltpu.make_async_copy(source, target, sems.at[i])
        for i, (source, target) in enumerate(zip(sources, targets))
    ]
    for copy in copies:
        copy.start()
    return copies


def stage_kernel(*refs):
    count = len(refs) // 2
    for copy in bring(refs[:count], refs[count : 2 * count], refs[-1]):
        copy.wait()


def pack_kernel(*refs):
    outs, (x_ref, dz_ref, ids_ref, probs_ref, sems) = refs[4:8], refs[8:]
    for copy in bring(refs[:4], refs[8:12], sems):
        copy.wait()
    rows, width = x_ref.shape
    piece = width // 4
    e = lax.axis_index("et")
    chosen = ids_ref[...] == 0
    weight_row = jnp.sum(jnp.where(chosen, probs_ref[...], 0.0), axis=0, keepdims=True)
    flag_row = jnp.max(jnp.where(chosen, 1.0, 0.0), axis=0, keepdims=True)
    on_diagonal = lax.broadcasted_iota(jnp.int32, (rows, rows), 0) == lax.broadcasted_iota(
        jnp.int32, (rows, rows), 1
    )
    weight = jnp.sum(jnp.where(on_diagonal, weight_row, 0.0), axis=1, keepdims=True)
    flag = jnp.sum(jnp.where(on_diagonal, flag_row, 0.0), axis=1, keepdims=True)
    for steps, out in enumerate(outs):
        start = pl.multiple_of((e ^ steps) * piece, 128)
        out[:, :piece] = x_ref[:, pl.ds(start, piece)]
        out[:, piece : 2 * piece] = (weight * dz_ref[:, pl.ds(start, piece)].astype(F32)).astype(BF16)
        out[:, 2 * piece :] = jnp.broadcast_to(flag, (rows, FLAG)).astype(BF16)


def compact_kernel(*refs):
    parts, (slots_ref, pick_ref, all_rows) = refs[:4], refs[4:]
    rows, wide = parts[0].shape
    tokens = 4 * rows
    data = wide - FLAG
    cap = slots_ref.shape[0]
    e = lax.axis_index("et")
    for steps, part in enumerate(parts):
        all_rows[pl.ds(pl.multiple_of((e ^ steps) * rows, 16), rows), :] = part[...]
    flags = all_rows[:, data:]
    before = lax.broadcasted_iota(jnp.int32, (tokens, tokens), 0)
    after = lax.broadcasted_iota(jnp.int32, (tokens, tokens), 1)
    count = contract(flags, (before <= after).astype(F32).astype(BF16), 0, 0)[:cap]
    here = contract(flags, (before == after).astype(F32).astype(BF16), 0, 0)[:cap]
    slot = lax.broadcasted_iota(jnp.int32, (cap, tokens), 0).astype(F32)
    pick = jnp.where((count - 1.0 == slot) & (here > 0.5), 1.0, 0.0).astype(BF16)
    slots_ref[...] = jnp.dot(pick, all_rows[:, :data], preferred_element_type=F32).astype(BF16)
    pick_ref[...] = jnp.zeros_like(pick_ref)
    pick_ref[:, :tokens] = pick


def expert_kernel(*refs):
    blocks, (wg_ref, wu_ref, wd_ref), outs = refs[:16], refs[16:19], refs[19:]
    x_ref, dz_ref, act_ref, gg_ref, ug_ref, own_ref, other_ref = outs
    cap, wide = blocks[0].shape
    piece = wide // 2
    half = wide
    e = lax.axis_index("et")
    for steps in range(4):
        start = pl.multiple_of((e ^ steps) * piece, 128)
        for k in range(4):
            block = blocks[4 * steps + k]
            rows = pl.ds(k * cap, cap)
            x_ref[rows, pl.ds(start, piece)] = block[:, :piece]
            dz_ref[rows, pl.ds(start, piece)] = block[:, piece:]
    gate = contract(x_ref[...], wg_ref[...], 1, 1)
    upper = contract(x_ref[...], wu_ref[...], 1, 1)
    act_grad = contract(dz_ref[...], wd_ref[...], 1, 1)
    sigmoid_gate = jax.nn.sigmoid(gate)
    silu_gate = gate * sigmoid_gate
    act_ref[...] = (silu_gate * upper).astype(BF16)
    gg_ref[...] = (act_grad * upper * sigmoid_gate * (1.0 + gate * (1.0 - sigmoid_gate))).astype(BF16)
    ug_ref[...] = (act_grad * silu_gate).astype(BF16)
    core = e % 2
    for out, side in ((other_ref, 1 - core), (own_ref, core)):
        start = pl.multiple_of(side * half, 128)
        terms = contract(gg_ref[...], wg_ref[:, pl.ds(start, half)], 1, 0)
        terms += contract(ug_ref[...], wu_ref[:, pl.ds(start, half)], 1, 0)
        out[...] = terms.astype(BF16)


def pair_kernel(own_ref, other_ref, pick_ref, *outs):
    cap, half = outs[1].shape
    for k, out in enumerate(outs):
        rows = pl.ds(k * cap, cap)
        out[:, :half] = (own_ref[rows, :].astype(F32) + other_ref[rows, :].astype(F32)).astype(BF16)
    outs[0][:, half:] = pick_ref[...]


def add_kernel(left_ref, right_ref, out_ref):
    out_ref[...] = (left_ref[...].astype(F32) + right_ref[...].astype(F32)).astype(BF16)


def expand_kernel(own_ref, near_ref, far_ref, *refs):
    outs, tokens_ref = refs[:4], refs[4]
    rows, half = outs[0].shape
    e = lax.axis_index("et")
    total = own_ref[:, :half].astype(F32) + near_ref[...].astype(F32) + far_ref[...].astype(F32)
    tokens_ref[...] = contract(own_ref[:, half:], total.astype(BF16), 0, 0).astype(BF16)
    for steps, out in enumerate(outs):
        out[...] = tokens_ref[pl.ds(pl.multiple_of((e ^ steps) * rows, 16), rows), :]


def finish_kernel(own_ref, core_ref, chip_ref, both_ref, out_ref):
    half = own_ref.shape[1]
    core = lax.axis_index("et") % 2
    mine = own_ref[...].astype(F32) + chip_ref[...].astype(F32)
    out_ref[:, pl.ds(pl.multiple_of(core * half, 128), half)] = mine.astype(BF16)
    theirs = core_ref[...].astype(F32) + both_ref[...].astype(F32)
    out_ref[:, pl.ds(pl.multiple_of((1 - core) * half, 128), half)] = theirs.astype(BF16)


def swap(value, axis, steps):
    return lax.ppermute(value, axis, spread(steps))


def hand(value, pipe_size, steps):
    pairs = [
        (4 * p + z, 4 * ((p - 1) % pipe_size) + (z ^ steps)) for p in range(pipe_size) for z in range(4)
    ]
    return lax.ppermute(value, ("pipe", "dp"), pairs)


def on_device_four(tokens, out_grad, top_ids, route_probs, w_gate, w_up, w_down):
    rows, width = tokens.shape[2:]
    hidden = w_gate.shape[1]
    top = top_ids.shape[3]
    pipe_size = lax.axis_size("pipe")
    cap = 2 * rows
    slots = 4 * cap
    piece, half = width // 4, width // 2

    packed = call(
        pack_kernel,
        [like((rows, 2 * piece + FLAG))] * 4,
        tokens[0, 0],
        out_grad[0, 0],
        top_ids[0, 0].T,
        route_probs[0, 0].T,
        scratch=[
            pltpu.VMEM((rows, width), BF16),
            pltpu.VMEM((rows, width), BF16),
            pltpu.VMEM((top, rows), jnp.int32),
            pltpu.VMEM((top, rows), F32),
            pltpu.SemaphoreType.DMA((4,)),
        ],
        space=HBM,
    )
    arrived = [packed[0]] + [swap(packed[s], "et", s) for s in (1, 2, 3)]
    weights = call(
        stage_kernel,
        [like((hidden, width))] * 3,
        w_gate[0],
        w_up[0],
        w_down[0],
        scratch=[pltpu.SemaphoreType.DMA((3,))],
        space=HBM,
    )
    arrived, (wg, wu, wd) = lax.optimization_barrier((arrived, weights))
    slot_block, pick = call(
        compact_kernel,
        [like((cap, 2 * piece)), like((cap, FLAG))],
        *arrived,
        scratch=[pltpu.VMEM((4 * rows, 2 * piece + FLAG), BF16)],
    )
    near = swap(slot_block, "dp", 1)
    far = swap(slot_block, "dp", 2)
    near, far = lax.optimization_barrier((near, far))
    chip_near = swap(near, "et", 2)
    last = swap(far, "dp", 1)
    own = [slot_block, near, far, last]
    chip = [swap(slot_block, "et", 2), chip_near, swap(far, "et", 2), swap(last, "et", 2)]
    core = [swap(block, "et", 1) for block in own]
    both = [swap(block, "et", 1) for block in chip]
    x, dz, act, gate_grad, up_grad, terms, away = call(
        expert_kernel,
        [like((slots, width))] * 2 + [like((slots, hidden))] * 3 + [like((slots, half))] * 2,
        *own,
        *core,
        *chip,
        *both,
        wg,
        wu,
        wd,
        flops=10 * slots * hidden * width,
        vmem=32,
    )
    theirs = swap(away, "et", 1)
    home, to_near, to_far, to_last = call(
        pair_kernel,
        [like((cap, half + FLAG))] + [like((cap, half))] * 3,
        terms,
        theirs,
        pick,
    )
    from_last = swap(to_last, "dp", 1)
    home = hand(home, pipe_size, 0)
    (to_far,) = call(add_kernel, [like((cap, half))], to_far, from_last)
    to_far, to_near = lax.optimization_barrier((to_far, to_near))
    from_far = hand(to_far, pipe_size, 2)
    from_near = hand(to_near, pipe_size, 1)
    grad_gate = contract(gate_grad, x, 0, 0).astype(BF16)
    grad_up = contract(up_grad, x, 0, 0).astype(BF16)
    from_far, grad_gate, grad_up = lax.optimization_barrier((from_far, grad_gate, grad_up))
    by_token = call(
        expand_kernel,
        [like((rows, half))] * 4,
        home,
        from_near,
        from_far,
        scratch=[pltpu.VMEM((FLAG, half), BF16)],
    )
    back = [by_token[0]] + [swap(by_token[s], "et", s) for s in (1, 2, 3)]
    (handed,) = call(finish_kernel, [like((rows, width))], *back)
    grad_down = contract(act, dz, 0, 0).astype(BF16)
    return (handed[None, None], grad_gate[None], grad_up[None], grad_down[None])


def solution(mesh):
    placed = (
        P("pipe", "dp", "et", None),
        P("pipe", "dp", "et", None),
        P("pipe", "dp", "et", None),
        P("pipe", "dp", "et", None),
        P("pipe", ("dp", "et"), None),
        P("pipe", ("dp", "et"), None),
        P("pipe", ("dp", "et"), None),
    )
    four = mesh.shape["et"] == 4 and mesh.shape["dp"] == 4
    return jax.shard_map(
        on_device_four if four else on_device_any,
        mesh=mesh,
        in_specs=placed,
        out_specs=(
            P("pipe", "dp", "et", None),
            P("pipe", ("dp", "et"), None),
            P("pipe", ("dp", "et"), None),
            P("pipe", ("dp", "et"), None),
        ),
        check_vma=False,
    )
```

```python
import functools

import jax
import jax.numpy as jnp
from jax import lax
from jax.experimental import pallas as pl
from jax.experimental.pallas import tpu as pltpu
from jax.sharding import PartitionSpec as P

FLAG = 128
BF16 = jnp.bfloat16
F32 = jnp.float32
VMEM = pl.BlockSpec(memory_space=pltpu.VMEM)
HBM = pl.BlockSpec(memory_space=pltpu.HBM)


def from_behind(value, axis, steps):
    count = lax.axis_size(axis)
    pairs = [(source, (source + steps) % count) for source in range(count)]
    return lax.ppermute(value, axis, pairs)


def slot_layout(routed, capacity):
    flags = routed.astype(jnp.int32)
    position = jnp.cumsum(flags, axis=-1, dtype=jnp.int32) - 1
    slot_ids = jnp.arange(capacity, dtype=jnp.int32)
    matches = (position[:, None, :] == slot_ids[None, :, None]) & routed[:, None, :]
    token_ids = jnp.arange(routed.shape[-1], dtype=jnp.int32)
    source = jnp.sum(jnp.where(matches, token_ids[None, None, :], 0), axis=-1)
    filled = jnp.any(matches, axis=-1)
    return (source, filled, position)


def gather_slots(rows, source, filled):
    picked = jnp.take_along_axis(rows, source[:, :, None], axis=1)
    return jnp.where(filled[:, :, None], picked, jnp.zeros_like(picked))


def contract(left, right, left_dim, right_dim):
    return lax.dot_general(
        left, right, (((left_dim,), (right_dim,)), ((), ())), preferred_element_type=F32
    )


def on_device_any(tokens, out_grad, top_ids, route_probs, w_gate, w_up, w_down):
    tok_dev = tokens.shape[2]
    model_width = tokens.shape[3]
    et_size = lax.axis_size("et")
    dp_size = lax.axis_size("dp")
    group_tokens = tok_dev * et_size
    capacity = group_tokens // 2
    token_rows = tokens[0, 0]
    chosen = top_ids[0, 0] == 0
    routed_flag = jnp.any(chosen, axis=-1).astype(BF16)
    route_weight = jnp.sum(jnp.where(chosen, route_probs[0, 0], F32(0.0)), axis=-1)
    scaled_rows = (route_weight[:, None] * out_grad[0, 0].astype(F32)).astype(BF16)
    group_x, group_dz, group_flag = (
        lax.all_gather(token_rows, "et", axis=0, tiled=True),
        lax.all_gather(scaled_rows, "et", axis=0, tiled=True),
        lax.all_gather(routed_flag, "et", axis=0, tiled=True),
    )
    routed = group_flag[None, :] > 0
    source, filled, position = slot_layout(routed, capacity)
    own_x = gather_slots(group_x[None], source, filled)
    own_dz = gather_slots(group_dz[None], source, filled)
    all_x, all_dz = (
        lax.all_gather(own_x, "dp", axis=0, tiled=True),
        lax.all_gather(own_dz, "dp", axis=0, tiled=True),
    )
    own_position = position[0]
    own_routed = routed[0]
    slot_x = all_x.reshape(dp_size * capacity, model_width)
    slot_dz = all_dz.reshape(dp_size * capacity, model_width)
    gate_rows = w_gate[0]
    up_rows = w_up[0]
    down_rows = w_down[0]
    gate = contract(slot_x, gate_rows, 1, 1)
    upper = contract(slot_x, up_rows, 1, 1)
    sigmoid_gate = jax.nn.sigmoid(gate)
    silu_gate = gate * sigmoid_gate
    act = (silu_gate * upper).astype(BF16)
    act_grad = contract(slot_dz, down_rows, 1, 1)
    gate_grad = (act_grad * upper * sigmoid_gate * (1.0 + gate * (1.0 - sigmoid_gate))).astype(BF16)
    up_grad = (act_grad * silu_gate).astype(BF16)
    grad_down = contract(act, slot_dz, 0, 0).astype(BF16)
    grad_gate = contract(gate_grad, slot_x, 0, 0).astype(BF16)
    grad_up = contract(up_grad, slot_x, 0, 0).astype(BF16)
    hidden_terms = contract(gate_grad, gate_rows, 1, 0) + contract(up_grad, up_rows, 1, 0)
    rounded = hidden_terms.astype(BF16).reshape(dp_size, capacity, model_width)
    hidden_sum = lax.psum_scatter(rounded, "et", scatter_dimension=1, tiled=True)
    slot_share = lax.psum_scatter(hidden_sum, "dp", scatter_dimension=0, tiled=True)
    slot_grad = lax.all_gather(slot_share, "et", axis=1, tiled=True)[0]
    start = lax.axis_index("et") * tok_dev
    my_position = lax.dynamic_slice_in_dim(own_position, start, tok_dev)
    my_routed = lax.dynamic_slice_in_dim(own_routed, start, tok_dev)
    picked = jnp.take(slot_grad, jnp.maximum(my_position, 0), axis=0)
    input_grad = jnp.where(my_routed[:, None], picked, jnp.zeros_like(picked))
    handed = from_behind(input_grad[None, None], "pipe", -1)
    return (handed, grad_gate[None], grad_up[None], grad_down[None])


def call(kernel, outs, *args, scratch=(), flops=0, vmem=16, space=VMEM, aliases=None):
    moved = sum(a.size * a.dtype.itemsize for a in args)
    moved += sum(o.size * o.dtype.itemsize for o in outs)
    if space is HBM:
        args = [pltpu.with_memory_space_constraint(a, pltpu.HBM) for a in args]
    return pl.pallas_call(
        kernel,
        out_shape=outs,
        in_specs=[space] * len(args),
        out_specs=[VMEM] * len(outs),
        scratch_shapes=list(scratch),
        input_output_aliases=aliases or {},
        compiler_params=pltpu.CompilerParams(vmem_limit_bytes=vmem * 2**20),
        cost_estimate=pl.CostEstimate(flops=flops, bytes_accessed=moved, transcendentals=0),
    )(*args)


def like(shape, dtype=BF16):
    return jax.ShapeDtypeStruct(shape, dtype)


def spread(steps):
    return [(e, e ^ steps) for e in range(4)]


def bring(sources, targets, sems):
    copies = [
        pltpu.make_async_copy(source, target, sems.at[i])
        for i, (source, target) in enumerate(zip(sources, targets))
    ]
    for copy in copies:
        copy.start()
    return copies


def stage_kernel(*refs):
    count = len(refs) // 2
    for copy in bring(refs[:count], refs[count : 2 * count], refs[-1]):
        copy.wait()


def pack_kernel(*refs):
    outs, (x_ref, dz_ref, ids_ref, probs_ref, sems) = refs[4:8], refs[8:]
    for copy in bring(refs[:4], refs[8:12], sems):
        copy.wait()
    rows, width = x_ref.shape
    piece = width // 4
    e = lax.axis_index("et")
    chosen = ids_ref[...] == 0
    weight_row = jnp.sum(jnp.where(chosen, probs_ref[...], 0.0), axis=0, keepdims=True)
    flag_row = jnp.max(jnp.where(chosen, 1.0, 0.0), axis=0, keepdims=True)
    on_diagonal = lax.broadcasted_iota(jnp.int32, (rows, rows), 0) == lax.broadcasted_iota(
        jnp.int32, (rows, rows), 1
    )
    weight = jnp.sum(jnp.where(on_diagonal, weight_row, 0.0), axis=1, keepdims=True)
    flag = jnp.sum(jnp.where(on_diagonal, flag_row, 0.0), axis=1, keepdims=True)
    for steps, out in enumerate(outs):
        start = pl.multiple_of((e ^ steps) * piece, 128)
        out[:, :piece] = x_ref[:, pl.ds(start, piece)]
        out[:, piece : 2 * piece] = (weight * dz_ref[:, pl.ds(start, piece)].astype(F32)).astype(BF16)
        out[:, 2 * piece :] = jnp.broadcast_to(flag, (rows, FLAG)).astype(BF16)


def compact_kernel(*refs):
    parts, (slots_ref, pick_ref, all_rows) = refs[:4], refs[4:]
    rows, wide = parts[0].shape
    tokens = 4 * rows
    data = wide - FLAG
    cap = slots_ref.shape[0]
    e = lax.axis_index("et")
    for steps, part in enumerate(parts):
        all_rows[pl.ds(pl.multiple_of((e ^ steps) * rows, 16), rows), :] = part[...]
    flags = all_rows[:, data:]
    before = lax.broadcasted_iota(jnp.int32, (tokens, tokens), 0)
    after = lax.broadcasted_iota(jnp.int32, (tokens, tokens), 1)
    count = contract(flags, (before <= after).astype(F32).astype(BF16), 0, 0)[:cap]
    here = contract(flags, (before == after).astype(F32).astype(BF16), 0, 0)[:cap]
    slot = lax.broadcasted_iota(jnp.int32, (cap, tokens), 0).astype(F32)
    pick = jnp.where((count - 1.0 == slot) & (here > 0.5), 1.0, 0.0).astype(BF16)
    slots_ref[...] = jnp.dot(pick, all_rows[:, :data], preferred_element_type=F32).astype(BF16)
    pick_ref[...] = jnp.zeros_like(pick_ref)
    pick_ref[:, :tokens] = pick


def expert_kernel(*refs):
    blocks, (wg_ref, wu_ref, wd_ref), outs = refs[:16], refs[16:19], refs[19:]
    x_ref, dz_ref, act_ref, gg_ref, ug_ref, own_ref, other_ref = outs
    cap, wide = blocks[0].shape
    piece = wide // 2
    half = wide
    e = lax.axis_index("et")
    for steps in range(4):
        start = pl.multiple_of((e ^ steps) * piece, 128)
        for k in range(4):
            block = blocks[4 * steps + k]
            rows = pl.ds(k * cap, cap)
            x_ref[rows, pl.ds(start, piece)] = block[:, :piece]
            dz_ref[rows, pl.ds(start, piece)] = block[:, piece:]
    gate = contract(x_ref[...], wg_ref[...], 1, 1)
    upper = contract(x_ref[...], wu_ref[...], 1, 1)
    act_grad = contract(dz_ref[...], wd_ref[...], 1, 1)
    sigmoid_gate = jax.nn.sigmoid(gate)
    silu_gate = gate * sigmoid_gate
    act_ref[...] = (silu_gate * upper).astype(BF16)
    gate_grad = (act_grad * upper * sigmoid_gate * (1.0 + gate * (1.0 - sigmoid_gate))).astype(BF16)
    up_grad = (act_grad * silu_gate).astype(BF16)
    gg_ref[...] = gate_grad
    ug_ref[...] = up_grad
    core = e % 2
    for out, side in ((other_ref, 1 - core), (own_ref, core)):
        start = pl.multiple_of(side * half, 128)
        terms = contract(gate_grad, wg_ref[:, pl.ds(start, half)], 1, 0)
        terms += contract(up_grad, wu_ref[:, pl.ds(start, half)], 1, 0)
        out[...] = terms.astype(BF16)


def pair_kernel(own_ref, other_ref, pick_ref, *outs):
    cap, half = outs[1].shape
    for k, out in enumerate(outs):
        rows = pl.ds(k * cap, cap)
        out[:, :half] = (own_ref[rows, :].astype(F32) + other_ref[rows, :].astype(F32)).astype(BF16)
    outs[0][:, half:] = pick_ref[...]


def expand_kernel(own_ref, *refs):
    others, outs, tokens_ref = refs[:3], refs[3:7], refs[7]
    rows, half = outs[0].shape
    e = lax.axis_index("et")
    total = own_ref[:, :half].astype(F32)
    for other in others:
        total += other[...].astype(F32)
    tokens_ref[...] = contract(own_ref[:, half:], total.astype(BF16), 0, 0).astype(BF16)
    for steps, out in enumerate(outs):
        out[...] = tokens_ref[pl.ds(pl.multiple_of((e ^ steps) * rows, 16), rows), :]


def finish_kernel(own_ref, core_ref, chip_ref, both_ref, out_ref):
    half = own_ref.shape[1]
    core = lax.axis_index("et") % 2
    mine = own_ref[...].astype(F32) + chip_ref[...].astype(F32)
    out_ref[:, pl.ds(pl.multiple_of(core * half, 128), half)] = mine.astype(BF16)
    theirs = core_ref[...].astype(F32) + both_ref[...].astype(F32)
    out_ref[:, pl.ds(pl.multiple_of((1 - core) * half, 128), half)] = theirs.astype(BF16)


def swap(value, axis, steps):
    return lax.ppermute(value, axis, spread(steps))


def hand(value, pipe_size, steps):
    pairs = [
        (4 * p + z, 4 * ((p - 1) % pipe_size) + (z ^ steps)) for p in range(pipe_size) for z in range(4)
    ]
    return lax.ppermute(value, ("pipe", "dp"), pairs)


def on_device_four(tokens, out_grad, top_ids, route_probs, w_gate, w_up, w_down):
    rows, width = tokens.shape[2:]
    hidden = w_gate.shape[1]
    top = top_ids.shape[3]
    pipe_size = lax.axis_size("pipe")
    cap = 2 * rows
    slots = 4 * cap
    piece, half = width // 4, width // 2

    packed = call(
        pack_kernel,
        [like((rows, 2 * piece + FLAG))] * 4,
        tokens[0, 0],
        out_grad[0, 0],
        top_ids[0, 0].T,
        route_probs[0, 0].T,
        scratch=[
            pltpu.VMEM((rows, width), BF16),
            pltpu.VMEM((rows, width), BF16),
            pltpu.VMEM((top, rows), jnp.int32),
            pltpu.VMEM((top, rows), F32),
            pltpu.SemaphoreType.DMA((4,)),
        ],
        space=HBM,
    )
    arrived = [packed[0]] + [swap(packed[s], "et", s) for s in (1, 2, 3)]
    weights = call(
        stage_kernel,
        [like((hidden, width))] * 3,
        w_gate[0],
        w_up[0],
        w_down[0],
        scratch=[pltpu.SemaphoreType.DMA((3,))],
        space=HBM,
    )
    arrived, (wg, wu, wd) = lax.optimization_barrier((arrived, weights))
    slot_block, pick = call(
        compact_kernel,
        [like((cap, 2 * piece)), like((cap, FLAG))],
        *arrived,
        scratch=[pltpu.VMEM((4 * rows, 2 * piece + FLAG), BF16)],
    )
    diag = swap(slot_block, "dp", 3)
    near = swap(slot_block, "dp", 1)
    far = swap(slot_block, "dp", 2)
    own = [slot_block, diag, near, far]
    chip = [swap(block, "et", 2) for block in own]
    core = [swap(block, "et", 1) for block in own]
    both = [swap(block, "et", 1) for block in chip]
    x, dz, act, gate_grad, up_grad, terms, away = call(
        expert_kernel,
        [like((slots, width))] * 2 + [like((slots, hidden))] * 3 + [like((slots, half))] * 2,
        *own,
        *core,
        *chip,
        *both,
        wg,
        wu,
        wd,
        flops=10 * slots * hidden * width,
        vmem=32,
    )
    theirs = swap(away, "et", 1)
    sums = call(
        pair_kernel,
        [like((cap, half + FLAG))] + [like((cap, half))] * 3,
        terms,
        theirs,
        pick,
    )
    home = [hand(sums[k], pipe_size, s) for k, s in ((0, 0), (3, 2), (1, 3), (2, 1))]
    grad_gate = contract(gate_grad, x, 0, 0).astype(BF16)
    grad_up = contract(up_grad, x, 0, 0).astype(BF16)
    home, grad_gate, grad_up = lax.optimization_barrier((home, grad_gate, grad_up))
    by_token = call(
        expand_kernel,
        [like((rows, half))] * 4,
        *home,
        scratch=[pltpu.VMEM((FLAG, half), BF16)],
    )
    back = [by_token[0]] + [swap(by_token[s], "et", s) for s in (1, 2, 3)]
    (handed,) = call(finish_kernel, [like((rows, width))], *back)
    grad_down = contract(act, dz, 0, 0).astype(BF16)
    return (handed[None, None], grad_gate[None], grad_up[None], grad_down[None])


def solution(mesh):
    placed = (
        P("pipe", "dp", "et", None),
        P("pipe", "dp", "et", None),
        P("pipe", "dp", "et", None),
        P("pipe", "dp", "et", None),
        P("pipe", ("dp", "et"), None),
        P("pipe", ("dp", "et"), None),
        P("pipe", ("dp", "et"), None),
    )
    four = mesh.shape["et"] == 4 and mesh.shape["dp"] == 4
    return jax.shard_map(
        on_device_four if four else on_device_any,
        mesh=mesh,
        in_specs=placed,
        out_specs=(
            P("pipe", "dp", "et", None),
            P("pipe", ("dp", "et"), None),
            P("pipe", ("dp", "et"), None),
            P("pipe", ("dp", "et"), None),
        ),
        check_vma=False,
    )
```

```python
import functools

import jax
import jax.numpy as jnp
from jax import lax
from jax.experimental import pallas as pl
from jax.experimental.pallas import tpu as pltpu
from jax.sharding import PartitionSpec as P

FLAG = 128
BF16 = jnp.bfloat16
F32 = jnp.float32
VMEM = pl.BlockSpec(memory_space=pltpu.VMEM)
HBM = pl.BlockSpec(memory_space=pltpu.HBM)


def from_behind(value, axis, steps):
    count = lax.axis_size(axis)
    pairs = [(source, (source + steps) % count) for source in range(count)]
    return lax.ppermute(value, axis, pairs)


def slot_layout(routed, capacity):
    flags = routed.astype(jnp.int32)
    position = jnp.cumsum(flags, axis=-1, dtype=jnp.int32) - 1
    slot_ids = jnp.arange(capacity, dtype=jnp.int32)
    matches = (position[:, None, :] == slot_ids[None, :, None]) & routed[:, None, :]
    token_ids = jnp.arange(routed.shape[-1], dtype=jnp.int32)
    source = jnp.sum(jnp.where(matches, token_ids[None, None, :], 0), axis=-1)
    filled = jnp.any(matches, axis=-1)
    return (source, filled, position)


def gather_slots(rows, source, filled):
    picked = jnp.take_along_axis(rows, source[:, :, None], axis=1)
    return jnp.where(filled[:, :, None], picked, jnp.zeros_like(picked))


def contract(left, right, left_dim, right_dim):
    return lax.dot_general(
        left, right, (((left_dim,), (right_dim,)), ((), ())), preferred_element_type=F32
    )


def on_device_any(tokens, out_grad, top_ids, route_probs, w_gate, w_up, w_down):
    tok_dev = tokens.shape[2]
    model_width = tokens.shape[3]
    et_size = lax.axis_size("et")
    dp_size = lax.axis_size("dp")
    group_tokens = tok_dev * et_size
    capacity = group_tokens // 2
    token_rows = tokens[0, 0]
    chosen = top_ids[0, 0] == 0
    routed_flag = jnp.any(chosen, axis=-1).astype(BF16)
    route_weight = jnp.sum(jnp.where(chosen, route_probs[0, 0], F32(0.0)), axis=-1)
    scaled_rows = (route_weight[:, None] * out_grad[0, 0].astype(F32)).astype(BF16)
    group_x, group_dz, group_flag = (
        lax.all_gather(token_rows, "et", axis=0, tiled=True),
        lax.all_gather(scaled_rows, "et", axis=0, tiled=True),
        lax.all_gather(routed_flag, "et", axis=0, tiled=True),
    )
    routed = group_flag[None, :] > 0
    source, filled, position = slot_layout(routed, capacity)
    own_x = gather_slots(group_x[None], source, filled)
    own_dz = gather_slots(group_dz[None], source, filled)
    all_x, all_dz = (
        lax.all_gather(own_x, "dp", axis=0, tiled=True),
        lax.all_gather(own_dz, "dp", axis=0, tiled=True),
    )
    own_position = position[0]
    own_routed = routed[0]
    slot_x = all_x.reshape(dp_size * capacity, model_width)
    slot_dz = all_dz.reshape(dp_size * capacity, model_width)
    gate_rows = w_gate[0]
    up_rows = w_up[0]
    down_rows = w_down[0]
    gate = contract(slot_x, gate_rows, 1, 1)
    upper = contract(slot_x, up_rows, 1, 1)
    sigmoid_gate = jax.nn.sigmoid(gate)
    silu_gate = gate * sigmoid_gate
    act = (silu_gate * upper).astype(BF16)
    act_grad = contract(slot_dz, down_rows, 1, 1)
    gate_grad = (act_grad * upper * sigmoid_gate * (1.0 + gate * (1.0 - sigmoid_gate))).astype(BF16)
    up_grad = (act_grad * silu_gate).astype(BF16)
    grad_down = contract(act, slot_dz, 0, 0).astype(BF16)
    grad_gate = contract(gate_grad, slot_x, 0, 0).astype(BF16)
    grad_up = contract(up_grad, slot_x, 0, 0).astype(BF16)
    hidden_terms = contract(gate_grad, gate_rows, 1, 0) + contract(up_grad, up_rows, 1, 0)
    rounded = hidden_terms.astype(BF16).reshape(dp_size, capacity, model_width)
    hidden_sum = lax.psum_scatter(rounded, "et", scatter_dimension=1, tiled=True)
    slot_share = lax.psum_scatter(hidden_sum, "dp", scatter_dimension=0, tiled=True)
    slot_grad = lax.all_gather(slot_share, "et", axis=1, tiled=True)[0]
    start = lax.axis_index("et") * tok_dev
    my_position = lax.dynamic_slice_in_dim(own_position, start, tok_dev)
    my_routed = lax.dynamic_slice_in_dim(own_routed, start, tok_dev)
    picked = jnp.take(slot_grad, jnp.maximum(my_position, 0), axis=0)
    input_grad = jnp.where(my_routed[:, None], picked, jnp.zeros_like(picked))
    handed = from_behind(input_grad[None, None], "pipe", -1)
    return (handed, grad_gate[None], grad_up[None], grad_down[None])


def call(kernel, outs, *args, scratch=(), flops=0, vmem=16, space=VMEM, aliases=None):
    moved = 0
    if space is HBM or flops:
        moved = sum(a.size * a.dtype.itemsize for a in args)
        moved += sum(o.size * o.dtype.itemsize for o in outs)
    if space is HBM:
        args = [pltpu.with_memory_space_constraint(a, pltpu.HBM) for a in args]
    return pl.pallas_call(
        kernel,
        out_shape=outs,
        in_specs=[space] * len(args),
        out_specs=[VMEM] * len(outs),
        scratch_shapes=list(scratch),
        input_output_aliases=aliases or {},
        compiler_params=pltpu.CompilerParams(vmem_limit_bytes=vmem * 2**20),
        cost_estimate=pl.CostEstimate(flops=flops, bytes_accessed=moved, transcendentals=0),
    )(*args)


def like(shape, dtype=BF16):
    return jax.ShapeDtypeStruct(shape, dtype)


def spread(steps):
    return [(e, e ^ steps) for e in range(4)]


def bring(sources, targets, sems):
    copies = [
        pltpu.make_async_copy(source, target, sems.at[i])
        for i, (source, target) in enumerate(zip(sources, targets))
    ]
    for copy in copies:
        copy.start()
    return copies


def stage_kernel(*refs):
    weights, outs, sems = refs[:3], refs[3:6], refs[6]
    third = weights[0].shape[0] // 3
    sources, targets = [], []
    for weight, out in zip(weights, outs):
        for part in range(3):
            rows = pl.ds(part * third, third)
            sources.append(weight.at[rows, :])
            targets.append(out.at[rows, :])
    for copy in bring(sources, targets, sems):
        copy.wait()


def pack_kernel(*refs):
    outs, (x_ref, dz_ref, ids_ref, probs_ref, sems) = refs[4:8], refs[8:]
    for copy in bring(refs[:4], refs[8:12], sems):
        copy.wait()
    rows, width = x_ref.shape
    piece = width // 4
    e = lax.axis_index("et")
    chosen = ids_ref[...] == 0
    weight_row = jnp.sum(jnp.where(chosen, probs_ref[...], 0.0), axis=0, keepdims=True)
    flag_row = jnp.max(jnp.where(chosen, 1.0, 0.0), axis=0, keepdims=True)
    on_diagonal = lax.broadcasted_iota(jnp.int32, (rows, rows), 0) == lax.broadcasted_iota(
        jnp.int32, (rows, rows), 1
    )
    weight = jnp.sum(jnp.where(on_diagonal, weight_row, 0.0), axis=1, keepdims=True)
    flag = jnp.sum(jnp.where(on_diagonal, flag_row, 0.0), axis=1, keepdims=True)
    for steps, out in enumerate(outs):
        start = pl.multiple_of((e ^ steps) * piece, 128)
        out[:, :piece] = x_ref[:, pl.ds(start, piece)]
        out[:, piece : 2 * piece] = (weight * dz_ref[:, pl.ds(start, piece)].astype(F32)).astype(BF16)
        out[:, 2 * piece :] = jnp.broadcast_to(flag, (rows, FLAG)).astype(BF16)


def compact_kernel(*refs):
    parts, (slots_ref, pick_ref, all_rows) = refs[:4], refs[4:]
    rows, wide = parts[0].shape
    tokens = 4 * rows
    data = wide - FLAG
    cap = slots_ref.shape[0]
    e = lax.axis_index("et")
    for steps, part in enumerate(parts):
        all_rows[pl.ds(pl.multiple_of((e ^ steps) * rows, 16), rows), :] = part[...]
    flags = all_rows[:, data:]
    before = lax.broadcasted_iota(jnp.int32, (tokens, tokens), 0)
    after = lax.broadcasted_iota(jnp.int32, (tokens, tokens), 1)
    count = contract(flags, (before <= after).astype(F32).astype(BF16), 0, 0)[:cap]
    here = contract(flags, (before == after).astype(F32).astype(BF16), 0, 0)[:cap]
    slot = lax.broadcasted_iota(jnp.int32, (cap, tokens), 0).astype(F32)
    pick = jnp.where((count - 1.0 == slot) & (here > 0.5), 1.0, 0.0).astype(BF16)
    slots_ref[...] = jnp.dot(pick, all_rows[:, :data], preferred_element_type=F32).astype(BF16)
    pick_ref[...] = jnp.zeros_like(pick_ref)
    pick_ref[:, :tokens] = pick


def add_quarter(steps, blocks, x_ref, dz_ref, weights):
    piece = blocks[0].shape[1] // 2
    columns = pl.ds(pl.multiple_of((lax.axis_index("et") ^ steps) * piece, 128), piece)
    start = 0
    for block in blocks:
        rows = pl.ds(start, block.shape[0])
        x_ref[rows, columns] = block[:, :piece]
        dz_ref[rows, columns] = block[:, piece:]
        start += block.shape[0]
    wg_ref, wu_ref, wd_ref = weights
    x, dz = x_ref[:, columns], dz_ref[:, columns]
    return (
        contract(x, wg_ref[:, columns], 1, 1),
        contract(x, wu_ref[:, columns], 1, 1),
        contract(dz, wd_ref[:, columns], 1, 1),
    )


def first_kernel(*refs):
    weights, (x_ref, dz_ref, *sums) = refs[12:15], refs[15:]
    for steps in range(3):
        parts = add_quarter(steps, refs[4 * steps : 4 * steps + 4], x_ref, dz_ref, weights)
        for out, part in zip(sums, parts):
            out[...] = out[...] + part if steps else part


def half_terms(other, gate_grad, up_grad, weights, half):
    side = lax.axis_index("et") % 2 ^ other
    columns = pl.ds(pl.multiple_of(side * half, 128), half)
    terms = contract(gate_grad, weights[0][:, columns], 1, 0)
    return terms + contract(up_grad, weights[1][:, columns], 1, 0)


def third_kernel(*refs):
    both, weights, olds, outs = refs[:4], refs[4:7], refs[9:12], refs[12:]
    x_ref, dz_ref, act_ref, gg_ref, ug_ref, grads_ref, away_ref = outs
    slots = x_ref.shape[0]
    parts = add_quarter(3, both, x_ref, dz_ref, weights)
    gate, upper, act_grad = (old[...] + part for old, part in zip(olds, parts))
    sigmoid_gate = jax.nn.sigmoid(gate)
    silu_gate = gate * sigmoid_gate
    gate_grad = (act_grad * upper * sigmoid_gate * (1.0 + gate * (1.0 - sigmoid_gate))).astype(BF16)
    up_grad = (act_grad * silu_gate).astype(BF16)
    gg_ref[...] = gate_grad
    ug_ref[...] = up_grad
    act_ref[...] = (silu_gate * upper).astype(BF16)
    grads_ref[:slots, :] = gate_grad
    grads_ref[slots:, :] = up_grad
    away_ref[...] = half_terms(1, gate_grad, up_grad, weights, away_ref.shape[1]).astype(BF16)


def own_terms_kernel(grads_ref, wg_ref, wu_ref, out_ref):
    slots, half = out_ref.shape
    grads = grads_ref[:slots, :], grads_ref[slots:, :]
    out_ref[...] = half_terms(0, *grads, (wg_ref, wu_ref), half)


def pair_kernel(own_ref, other_ref, pick_ref, *outs):
    cap, half = outs[0].shape
    for k, out in enumerate(outs):
        rows = pl.ds(k * cap, cap)
        out[:, :half] = (own_ref[rows, :] + other_ref[rows, :].astype(F32)).astype(BF16)
    outs[3][:, half:] = pick_ref[...]


def add_kernel(left_ref, right_ref, near_ref, out_ref, pass_ref, ready_ref):
    out_ref[...] = (left_ref[...].astype(F32) + right_ref[...].astype(F32)).astype(BF16)
    pass_ref[...] = near_ref[...]
    ready_ref[...] = jnp.zeros_like(ready_ref)


def expand_kernel(own_ref, ready_ref, *refs):
    others, outs, tokens_ref = refs[:2], refs[2:6], refs[6]
    rows, half = outs[0].shape
    e = lax.axis_index("et")
    total = own_ref[:, :half].astype(F32)
    for other in others:
        total += other[...].astype(F32)
    tokens_ref[...] = contract(own_ref[:, half:], total.astype(BF16), 0, 0).astype(BF16)
    for steps, out in enumerate(outs):
        out[...] = tokens_ref[pl.ds(pl.multiple_of((e ^ steps) * rows, 16), rows), :]


def finish_kernel(own_ref, core_ref, chip_ref, both_ref, out_ref):
    half = own_ref.shape[1]
    core = lax.axis_index("et") % 2
    mine = own_ref[...].astype(F32) + chip_ref[...].astype(F32)
    out_ref[:, pl.ds(pl.multiple_of(core * half, 128), half)] = mine.astype(BF16)
    theirs = core_ref[...].astype(F32) + both_ref[...].astype(F32)
    out_ref[:, pl.ds(pl.multiple_of((1 - core) * half, 128), half)] = theirs.astype(BF16)


def swap(value, axis, steps):
    return lax.ppermute(value, axis, spread(steps))


def hand(value, pipe_size, steps):
    pairs = [
        (4 * p + z, 4 * ((p - 1) % pipe_size) + (z ^ steps)) for p in range(pipe_size) for z in range(4)
    ]
    return lax.ppermute(value, ("pipe", "dp"), pairs)


def on_device_four(tokens, out_grad, top_ids, route_probs, w_gate, w_up, w_down):
    rows, width = tokens.shape[2:]
    hidden = w_gate.shape[1]
    top = top_ids.shape[3]
    pipe_size = lax.axis_size("pipe")
    cap = 2 * rows
    slots = 4 * cap
    piece, half = width // 4, width // 2

    packed = call(
        pack_kernel,
        [like((rows, 2 * piece + FLAG))] * 4,
        tokens[0, 0],
        out_grad[0, 0],
        top_ids[0, 0].T,
        route_probs[0, 0].T,
        scratch=[
            pltpu.VMEM((rows, width), BF16),
            pltpu.VMEM((rows, width), BF16),
            pltpu.VMEM((top, rows), jnp.int32),
            pltpu.VMEM((top, rows), F32),
            pltpu.SemaphoreType.DMA((4,)),
        ],
        space=HBM,
    )
    arrived = [packed[0]] + [swap(packed[s], "et", s) for s in (1, 2, 3)]
    weights = call(
        stage_kernel,
        [like((hidden, width))] * 3,
        w_gate[0],
        w_up[0],
        w_down[0],
        scratch=[pltpu.SemaphoreType.DMA((9,))],
        space=HBM,
    )
    arrived, weights = lax.optimization_barrier((arrived, weights))
    slot_block, pick = call(
        compact_kernel,
        [like((cap, 2 * piece)), like((cap, FLAG))],
        *arrived,
        scratch=[pltpu.VMEM((4 * rows, 2 * piece + FLAG), BF16)],
    )
    diag = swap(slot_block, "dp", 3)
    near = swap(slot_block, "dp", 1)
    far = swap(slot_block, "dp", 2)
    own = [diag, near, far, slot_block]
    chip = [swap(block, "et", 2) for block in own]
    core = [swap(block, "et", 1) for block in own]
    both = [swap(block, "et", 1) for block in chip]
    wide, sums = [like((slots, width))] * 2, [like((slots, hidden), F32)] * 3
    state = call(first_kernel, wide + sums, *own, *core, *chip, *weights, vmem=32)
    x, dz, act, gate_grad, up_grad, grads, away = call(
        third_kernel,
        wide + [like((slots, hidden))] * 3 + [like((2 * slots, hidden)), like((slots, half))],
        *both,
        *weights,
        *state,
        vmem=32,
        aliases={7: 0, 8: 1},
    )
    theirs = swap(away, "et", 1)
    (own_terms,) = call(
        own_terms_kernel,
        [like((slots, half), F32)],
        grads,
        *weights[:2],
        flops=4 * slots * hidden * half,
        vmem=32,
    )
    to_last, to_near, to_far, home = call(
        pair_kernel,
        [like((cap, half))] * 3 + [like((cap, half + FLAG))],
        own_terms,
        theirs,
        pick,
    )
    from_last = swap(to_last, "dp", 1)
    home = hand(home, pipe_size, 0)
    to_far, to_near, ready = call(
        add_kernel,
        [like((cap, half))] * 2 + [like((8, 128), F32)],
        to_far,
        from_last,
        to_near,
    )
    x, dz, act, gate_grad, up_grad, ready = lax.optimization_barrier(
        (x, dz, act, gate_grad, up_grad, ready)
    )
    grad_gate = contract(gate_grad, x, 0, 0).astype(BF16)
    grad_up = contract(up_grad, x, 0, 0).astype(BF16)
    from_far = hand(to_far, pipe_size, 2)
    from_near = hand(to_near, pipe_size, 1)
    from_far, grad_gate, grad_up = lax.optimization_barrier((from_far, grad_gate, grad_up))
    by_token = call(
        expand_kernel,
        [like((rows, half))] * 4,
        home,
        ready,
        from_far,
        from_near,
        scratch=[pltpu.VMEM((FLAG, half), BF16)],
    )
    back = [by_token[0]] + [swap(by_token[s], "et", s) for s in (1, 2, 3)]
    (handed,) = call(finish_kernel, [like((rows, width))], *back)
    grad_down = contract(act, dz, 0, 0).astype(BF16)
    return (handed[None, None], grad_gate[None], grad_up[None], grad_down[None])


def solution(mesh):
    placed = (
        P("pipe", "dp", "et", None),
        P("pipe", "dp", "et", None),
        P("pipe", "dp", "et", None),
        P("pipe", "dp", "et", None),
        P("pipe", ("dp", "et"), None),
        P("pipe", ("dp", "et"), None),
        P("pipe", ("dp", "et"), None),
    )
    four = mesh.shape["et"] == 4 and mesh.shape["dp"] == 4
    return jax.shard_map(
        on_device_four if four else on_device_any,
        mesh=mesh,
        in_specs=placed,
        out_specs=(
            P("pipe", "dp", "et", None),
            P("pipe", ("dp", "et"), None),
            P("pipe", ("dp", "et"), None),
            P("pipe", ("dp", "et"), None),
        ),
        check_vma=False,
    )
```

```python
import functools

import jax
import jax.numpy as jnp
from jax import lax
from jax.experimental import pallas as pl
from jax.experimental.pallas import tpu as pltpu
from jax.sharding import PartitionSpec as P

FLAG = 128
BF16 = jnp.bfloat16
F32 = jnp.float32
VMEM = pl.BlockSpec(memory_space=pltpu.VMEM)
HBM = pl.BlockSpec(memory_space=pltpu.HBM)


def from_behind(value, axis, steps):
    count = lax.axis_size(axis)
    pairs = [(source, (source + steps) % count) for source in range(count)]
    return lax.ppermute(value, axis, pairs)


def slot_layout(routed, capacity):
    flags = routed.astype(jnp.int32)
    position = jnp.cumsum(flags, axis=-1, dtype=jnp.int32) - 1
    slot_ids = jnp.arange(capacity, dtype=jnp.int32)
    matches = (position[:, None, :] == slot_ids[None, :, None]) & routed[:, None, :]
    token_ids = jnp.arange(routed.shape[-1], dtype=jnp.int32)
    source = jnp.sum(jnp.where(matches, token_ids[None, None, :], 0), axis=-1)
    filled = jnp.any(matches, axis=-1)
    return (source, filled, position)


def gather_slots(rows, source, filled):
    picked = jnp.take_along_axis(rows, source[:, :, None], axis=1)
    return jnp.where(filled[:, :, None], picked, jnp.zeros_like(picked))


def contract(left, right, left_dim, right_dim):
    return lax.dot_general(
        left, right, (((left_dim,), (right_dim,)), ((), ())), preferred_element_type=F32
    )


def on_device_any(tokens, out_grad, top_ids, route_probs, w_gate, w_up, w_down):
    tok_dev = tokens.shape[2]
    model_width = tokens.shape[3]
    et_size = lax.axis_size("et")
    dp_size = lax.axis_size("dp")
    group_tokens = tok_dev * et_size
    capacity = group_tokens // 2
    token_rows = tokens[0, 0]
    chosen = top_ids[0, 0] == 0
    routed_flag = jnp.any(chosen, axis=-1).astype(BF16)
    route_weight = jnp.sum(jnp.where(chosen, route_probs[0, 0], F32(0.0)), axis=-1)
    scaled_rows = (route_weight[:, None] * out_grad[0, 0].astype(F32)).astype(BF16)
    group_x, group_dz, group_flag = (
        lax.all_gather(token_rows, "et", axis=0, tiled=True),
        lax.all_gather(scaled_rows, "et", axis=0, tiled=True),
        lax.all_gather(routed_flag, "et", axis=0, tiled=True),
    )
    routed = group_flag[None, :] > 0
    source, filled, position = slot_layout(routed, capacity)
    own_x = gather_slots(group_x[None], source, filled)
    own_dz = gather_slots(group_dz[None], source, filled)
    all_x, all_dz = (
        lax.all_gather(own_x, "dp", axis=0, tiled=True),
        lax.all_gather(own_dz, "dp", axis=0, tiled=True),
    )
    own_position = position[0]
    own_routed = routed[0]
    slot_x = all_x.reshape(dp_size * capacity, model_width)
    slot_dz = all_dz.reshape(dp_size * capacity, model_width)
    gate_rows = w_gate[0]
    up_rows = w_up[0]
    down_rows = w_down[0]
    gate = contract(slot_x, gate_rows, 1, 1)
    upper = contract(slot_x, up_rows, 1, 1)
    sigmoid_gate = jax.nn.sigmoid(gate)
    silu_gate = gate * sigmoid_gate
    act = (silu_gate * upper).astype(BF16)
    act_grad = contract(slot_dz, down_rows, 1, 1)
    gate_grad = (act_grad * upper * sigmoid_gate * (1.0 + gate * (1.0 - sigmoid_gate))).astype(BF16)
    up_grad = (act_grad * silu_gate).astype(BF16)
    grad_down = contract(act, slot_dz, 0, 0).astype(BF16)
    grad_gate = contract(gate_grad, slot_x, 0, 0).astype(BF16)
    grad_up = contract(up_grad, slot_x, 0, 0).astype(BF16)
    hidden_terms = contract(gate_grad, gate_rows, 1, 0) + contract(up_grad, up_rows, 1, 0)
    rounded = hidden_terms.astype(BF16).reshape(dp_size, capacity, model_width)
    hidden_sum = lax.psum_scatter(rounded, "et", scatter_dimension=1, tiled=True)
    slot_share = lax.psum_scatter(hidden_sum, "dp", scatter_dimension=0, tiled=True)
    slot_grad = lax.all_gather(slot_share, "et", axis=1, tiled=True)[0]
    start = lax.axis_index("et") * tok_dev
    my_position = lax.dynamic_slice_in_dim(own_position, start, tok_dev)
    my_routed = lax.dynamic_slice_in_dim(own_routed, start, tok_dev)
    picked = jnp.take(slot_grad, jnp.maximum(my_position, 0), axis=0)
    input_grad = jnp.where(my_routed[:, None], picked, jnp.zeros_like(picked))
    handed = from_behind(input_grad[None, None], "pipe", -1)
    return (handed, grad_gate[None], grad_up[None], grad_down[None])


def call(kernel, outs, *args, scratch=(), flops=0, vmem=16, space=VMEM, aliases=None):
    moved = 0
    if space is HBM or flops:
        moved = sum(a.size * a.dtype.itemsize for a in args)
        moved += sum(o.size * o.dtype.itemsize for o in outs)
    if space is HBM:
        args = [pltpu.with_memory_space_constraint(a, pltpu.HBM) for a in args]
    return pl.pallas_call(
        kernel,
        out_shape=outs,
        in_specs=[space] * len(args),
        out_specs=[VMEM] * len(outs),
        scratch_shapes=list(scratch),
        input_output_aliases=aliases or {},
        compiler_params=pltpu.CompilerParams(vmem_limit_bytes=vmem * 2**20),
        cost_estimate=pl.CostEstimate(flops=flops, bytes_accessed=moved, transcendentals=0),
    )(*args)


def like(shape, dtype=BF16):
    return jax.ShapeDtypeStruct(shape, dtype)


def spread(steps):
    return [(e, e ^ steps) for e in range(4)]


def bring(sources, targets, sems):
    copies = [
        pltpu.make_async_copy(source, target, sems.at[i])
        for i, (source, target) in enumerate(zip(sources, targets))
    ]
    for copy in copies:
        copy.start()
    return copies


def stage_kernel(*refs):
    weights, outs, sems = refs[:3], refs[3:6], refs[6]
    third = weights[0].shape[0] // 3
    sources, targets = [], []
    for weight, out in zip(weights, outs):
        for part in range(3):
            rows = pl.ds(part * third, third)
            sources.append(weight.at[rows, :])
            targets.append(out.at[rows, :])
    for copy in bring(sources, targets, sems):
        copy.wait()


def pack_kernel(*refs):
    outs, (x_ref, dz_ref, ids_ref, probs_ref, sems) = refs[4:8], refs[8:]
    for copy in bring(refs[:4], refs[8:12], sems):
        copy.wait()
    rows, width = x_ref.shape
    piece = width // 4
    e = lax.axis_index("et")
    chosen = ids_ref[...] == 0
    weight_row = jnp.sum(jnp.where(chosen, probs_ref[...], 0.0), axis=0, keepdims=True)
    flag_row = jnp.max(jnp.where(chosen, 1.0, 0.0), axis=0, keepdims=True)
    on_diagonal = lax.broadcasted_iota(jnp.int32, (rows, rows), 0) == lax.broadcasted_iota(
        jnp.int32, (rows, rows), 1
    )
    weight = jnp.sum(jnp.where(on_diagonal, weight_row, 0.0), axis=1, keepdims=True)
    flag = jnp.sum(jnp.where(on_diagonal, flag_row, 0.0), axis=1, keepdims=True)
    for steps, out in enumerate(outs):
        start = pl.multiple_of((e ^ steps) * piece, 128)
        out[:, :piece] = x_ref[:, pl.ds(start, piece)]
        out[:, piece : 2 * piece] = (weight * dz_ref[:, pl.ds(start, piece)].astype(F32)).astype(BF16)
        out[:, 2 * piece :] = jnp.broadcast_to(flag, (rows, FLAG)).astype(BF16)


def compact_kernel(*refs):
    parts, (slots_ref, pick_ref, all_rows) = refs[:4], refs[4:]
    rows, wide = parts[0].shape
    tokens = 4 * rows
    data = wide - FLAG
    cap = slots_ref.shape[0]
    e = lax.axis_index("et")
    for steps, part in enumerate(parts):
        all_rows[pl.ds(pl.multiple_of((e ^ steps) * rows, 16), rows), :] = part[...]
    flags = all_rows[:, data:]
    before = lax.broadcasted_iota(jnp.int32, (tokens, tokens), 0)
    after = lax.broadcasted_iota(jnp.int32, (tokens, tokens), 1)
    count = contract(flags, (before <= after).astype(F32).astype(BF16), 0, 0)[:cap]
    here = contract(flags, (before == after).astype(F32).astype(BF16), 0, 0)[:cap]
    slot = lax.broadcasted_iota(jnp.int32, (cap, tokens), 0).astype(F32)
    pick = jnp.where((count - 1.0 == slot) & (here > 0.5), 1.0, 0.0).astype(BF16)
    slots_ref[...] = jnp.dot(pick, all_rows[:, :data], preferred_element_type=F32).astype(BF16)
    pick_ref[...] = jnp.zeros_like(pick_ref)
    pick_ref[:, :tokens] = pick


def add_quarter(steps, blocks, x_ref, dz_ref, weights):
    piece = blocks[0].shape[1] // 2
    columns = pl.ds(pl.multiple_of((lax.axis_index("et") ^ steps) * piece, 128), piece)
    start = 0
    for block in blocks:
        rows = pl.ds(start, block.shape[0])
        x_ref[rows, columns] = block[:, :piece]
        dz_ref[rows, columns] = block[:, piece:]
        start += block.shape[0]
    wg_ref, wu_ref, wd_ref = weights
    x, dz = x_ref[:, columns], dz_ref[:, columns]
    return (
        contract(x, wg_ref[:, columns], 1, 1),
        contract(x, wu_ref[:, columns], 1, 1),
        contract(dz, wd_ref[:, columns], 1, 1),
    )


def first_kernel(*refs):
    weights, (x_ref, dz_ref, *sums) = refs[12:15], refs[15:]
    for steps in range(3):
        parts = add_quarter(steps, refs[4 * steps : 4 * steps + 4], x_ref, dz_ref, weights)
        for out, part in zip(sums, parts):
            out[...] = out[...] + part if steps else part


def half_terms(other, gate_grad, up_grad, weights, half):
    side = lax.axis_index("et") % 2 ^ other
    columns = pl.ds(pl.multiple_of(side * half, 128), half)
    terms = contract(gate_grad, weights[0][:, columns], 1, 0)
    return terms + contract(up_grad, weights[1][:, columns], 1, 0)


def third_kernel(*refs):
    both, weights, olds, outs = refs[:4], refs[4:7], refs[9:12], refs[12:]
    x_ref, dz_ref, act_ref, gg_ref, ug_ref, grads_ref, away_ref = outs
    slots = x_ref.shape[0]
    parts = add_quarter(3, both, x_ref, dz_ref, weights)
    gate, upper, act_grad = (old[...] + part for old, part in zip(olds, parts))
    sigmoid_gate = jax.nn.sigmoid(gate)
    silu_gate = gate * sigmoid_gate
    gate_grad = (act_grad * upper * sigmoid_gate * (1.0 + gate * (1.0 - sigmoid_gate))).astype(BF16)
    up_grad = (act_grad * silu_gate).astype(BF16)
    gg_ref[...] = gate_grad
    ug_ref[...] = up_grad
    act_ref[...] = (silu_gate * upper).astype(BF16)
    grads_ref[:slots, :] = gate_grad
    grads_ref[slots:, :] = up_grad
    away_ref[...] = half_terms(1, gate_grad, up_grad, weights, away_ref.shape[1]).astype(BF16)


def own_terms_kernel(grads_ref, wg_ref, wu_ref, out_ref):
    slots, half = out_ref.shape
    grads = grads_ref[:slots, :], grads_ref[slots:, :]
    out_ref[...] = half_terms(0, *grads, (wg_ref, wu_ref), half)


def pair_kernel(own_ref, other_ref, pick_ref, *outs):
    cap, half = outs[0].shape
    for k, out in enumerate(outs):
        rows = pl.ds(k * cap, cap)
        out[:, :half] = (own_ref[rows, :] + other_ref[rows, :].astype(F32)).astype(BF16)
    outs[3][:, half:] = pick_ref[...]


def add_kernel(left_ref, right_ref, near_ref, out_ref, pass_ref, ready_ref):
    out_ref[...] = (left_ref[...].astype(F32) + right_ref[...].astype(F32)).astype(BF16)
    pass_ref[...] = near_ref[...]
    ready_ref[...] = jnp.zeros_like(ready_ref)


def expand_kernel(own_ref, ready_ref, *refs):
    others, outs, tokens_ref = refs[:2], refs[2:6], refs[6]
    rows, half = outs[0].shape
    e = lax.axis_index("et")
    total = own_ref[:, :half].astype(F32)
    for other in others:
        total += other[...].astype(F32)
    tokens_ref[...] = contract(own_ref[:, half:], total.astype(BF16), 0, 0).astype(BF16)
    for steps, out in enumerate(outs):
        out[...] = tokens_ref[pl.ds(pl.multiple_of((e ^ steps) * rows, 16), rows), :]


def finish_kernel(own_ref, core_ref, chip_ref, both_ref, out_ref):
    half = own_ref.shape[1]
    core = lax.axis_index("et") % 2
    mine = own_ref[...].astype(F32) + chip_ref[...].astype(F32)
    out_ref[:, pl.ds(pl.multiple_of(core * half, 128), half)] = mine.astype(BF16)
    theirs = core_ref[...].astype(F32) + both_ref[...].astype(F32)
    out_ref[:, pl.ds(pl.multiple_of((1 - core) * half, 128), half)] = theirs.astype(BF16)


def swap(value, axis, steps):
    return lax.ppermute(value, axis, spread(steps))


def hand(value, pipe_size, steps):
    pairs = [
        (4 * p + z, 4 * ((p - 1) % pipe_size) + (z ^ steps)) for p in range(pipe_size) for z in range(4)
    ]
    return lax.ppermute(value, ("pipe", "dp"), pairs)


def on_device_four(tokens, out_grad, top_ids, route_probs, w_gate, w_up, w_down):
    rows, width = tokens.shape[2:]
    hidden = w_gate.shape[1]
    top = top_ids.shape[3]
    pipe_size = lax.axis_size("pipe")
    cap = 2 * rows
    slots = 4 * cap
    piece, half = width // 4, width // 2

    packed = call(
        pack_kernel,
        [like((rows, 2 * piece + FLAG))] * 4,
        tokens[0, 0],
        out_grad[0, 0],
        top_ids[0, 0].T,
        route_probs[0, 0].T,
        scratch=[
            pltpu.VMEM((rows, width), BF16),
            pltpu.VMEM((rows, width), BF16),
            pltpu.VMEM((top, rows), jnp.int32),
            pltpu.VMEM((top, rows), F32),
            pltpu.SemaphoreType.DMA((4,)),
        ],
        space=HBM,
    )
    arrived = [packed[0]] + [swap(packed[s], "et", s) for s in (1, 2, 3)]
    weights = call(
        stage_kernel,
        [like((hidden, width))] * 3,
        w_gate[0],
        w_up[0],
        w_down[0],
        scratch=[pltpu.SemaphoreType.DMA((9,))],
        space=HBM,
    )
    arrived, weights = lax.optimization_barrier((arrived, weights))
    slot_block, pick = call(
        compact_kernel,
        [like((cap, 2 * piece)), like((cap, FLAG))],
        *arrived,
        scratch=[pltpu.VMEM((4 * rows, 2 * piece + FLAG), BF16)],
    )
    diag = swap(slot_block, "dp", 3)
    near = swap(slot_block, "dp", 1)
    far = swap(slot_block, "dp", 2)
    beside = swap(slot_block, "et", 2)
    own = [diag, near, far, slot_block]
    chip = [swap(diag, "et", 2), swap(beside, "dp", 1), swap(far, "et", 2), beside]
    core = [swap(block, "et", 1) for block in own]
    both = [swap(block, "et", 1) for block in chip]
    wide, sums = [like((slots, width))] * 2, [like((slots, hidden), F32)] * 3
    state = call(first_kernel, wide + sums, *own, *core, *chip, *weights, vmem=32)
    x, dz, act, gate_grad, up_grad, grads, away = call(
        third_kernel,
        wide + [like((slots, hidden))] * 3 + [like((2 * slots, hidden)), like((slots, half))],
        *both,
        *weights,
        *state,
        vmem=32,
        aliases={7: 0, 8: 1},
    )
    theirs = swap(away, "et", 1)
    (own_terms,) = call(
        own_terms_kernel,
        [like((slots, half), F32)],
        grads,
        *weights[:2],
        flops=4 * slots * hidden * half,
        vmem=32,
    )
    to_last, to_near, to_far, home = call(
        pair_kernel,
        [like((cap, half))] * 3 + [like((cap, half + FLAG))],
        own_terms,
        theirs,
        pick,
    )
    from_last = swap(to_last, "dp", 1)
    home = hand(home, pipe_size, 0)
    to_far, to_near, ready = call(
        add_kernel,
        [like((cap, half))] * 2 + [like((8, 128), F32)],
        to_far,
        from_last,
        to_near,
    )
    x, dz, act, gate_grad, up_grad, ready = lax.optimization_barrier(
        (x, dz, act, gate_grad, up_grad, ready)
    )
    grad_gate = contract(gate_grad, x, 0, 0).astype(BF16)
    grad_up = contract(up_grad, x, 0, 0).astype(BF16)
    from_far = hand(to_far, pipe_size, 2)
    from_near = hand(to_near, pipe_size, 1)
    from_far, grad_gate, grad_up = lax.optimization_barrier((from_far, grad_gate, grad_up))
    by_token = call(
        expand_kernel,
        [like((rows, half))] * 4,
        home,
        ready,
        from_far,
        from_near,
        scratch=[pltpu.VMEM((FLAG, half), BF16)],
    )
    back = [by_token[0]] + [swap(by_token[s], "et", s) for s in (1, 2, 3)]
    (handed,) = call(finish_kernel, [like((rows, width))], *back)
    grad_down = contract(act, dz, 0, 0).astype(BF16)
    return (handed[None, None], grad_gate[None], grad_up[None], grad_down[None])


def solution(mesh):
    placed = (
        P("pipe", "dp", "et", None),
        P("pipe", "dp", "et", None),
        P("pipe", "dp", "et", None),
        P("pipe", "dp", "et", None),
        P("pipe", ("dp", "et"), None),
        P("pipe", ("dp", "et"), None),
        P("pipe", ("dp", "et"), None),
    )
    four = mesh.shape["et"] == 4 and mesh.shape["dp"] == 4
    return jax.shard_map(
        on_device_four if four else on_device_any,
        mesh=mesh,
        in_specs=placed,
        out_specs=(
            P("pipe", "dp", "et", None),
            P("pipe", ("dp", "et"), None),
            P("pipe", ("dp", "et"), None),
            P("pipe", ("dp", "et"), None),
        ),
        check_vma=False,
    )
```

```python
import functools

import jax
import jax.numpy as jnp
from jax import lax
from jax.experimental import pallas as pl
from jax.experimental.pallas import tpu as pltpu
from jax.sharding import PartitionSpec as P

FLAG = 128
BF16 = jnp.bfloat16
F32 = jnp.float32
VMEM = pl.BlockSpec(memory_space=pltpu.VMEM)
HBM = pl.BlockSpec(memory_space=pltpu.HBM)


def from_behind(value, axis, steps):
    count = lax.axis_size(axis)
    pairs = [(source, (source + steps) % count) for source in range(count)]
    return lax.ppermute(value, axis, pairs)


def slot_layout(routed, capacity):
    flags = routed.astype(jnp.int32)
    position = jnp.cumsum(flags, axis=-1, dtype=jnp.int32) - 1
    slot_ids = jnp.arange(capacity, dtype=jnp.int32)
    matches = (position[:, None, :] == slot_ids[None, :, None]) & routed[:, None, :]
    token_ids = jnp.arange(routed.shape[-1], dtype=jnp.int32)
    source = jnp.sum(jnp.where(matches, token_ids[None, None, :], 0), axis=-1)
    filled = jnp.any(matches, axis=-1)
    return (source, filled, position)


def gather_slots(rows, source, filled):
    picked = jnp.take_along_axis(rows, source[:, :, None], axis=1)
    return jnp.where(filled[:, :, None], picked, jnp.zeros_like(picked))


def contract(left, right, left_dim, right_dim):
    return lax.dot_general(
        left, right, (((left_dim,), (right_dim,)), ((), ())), preferred_element_type=F32
    )


def on_device_any(tokens, out_grad, top_ids, route_probs, w_gate, w_up, w_down):
    tok_dev = tokens.shape[2]
    model_width = tokens.shape[3]
    et_size = lax.axis_size("et")
    dp_size = lax.axis_size("dp")
    group_tokens = tok_dev * et_size
    capacity = group_tokens // 2
    token_rows = tokens[0, 0]
    chosen = top_ids[0, 0] == 0
    routed_flag = jnp.any(chosen, axis=-1).astype(BF16)
    route_weight = jnp.sum(jnp.where(chosen, route_probs[0, 0], F32(0.0)), axis=-1)
    scaled_rows = (route_weight[:, None] * out_grad[0, 0].astype(F32)).astype(BF16)
    group_x, group_dz, group_flag = (
        lax.all_gather(token_rows, "et", axis=0, tiled=True),
        lax.all_gather(scaled_rows, "et", axis=0, tiled=True),
        lax.all_gather(routed_flag, "et", axis=0, tiled=True),
    )
    routed = group_flag[None, :] > 0
    source, filled, position = slot_layout(routed, capacity)
    own_x = gather_slots(group_x[None], source, filled)
    own_dz = gather_slots(group_dz[None], source, filled)
    all_x, all_dz = (
        lax.all_gather(own_x, "dp", axis=0, tiled=True),
        lax.all_gather(own_dz, "dp", axis=0, tiled=True),
    )
    own_position = position[0]
    own_routed = routed[0]
    slot_x = all_x.reshape(dp_size * capacity, model_width)
    slot_dz = all_dz.reshape(dp_size * capacity, model_width)
    gate_rows = w_gate[0]
    up_rows = w_up[0]
    down_rows = w_down[0]
    gate = contract(slot_x, gate_rows, 1, 1)
    upper = contract(slot_x, up_rows, 1, 1)
    sigmoid_gate = jax.nn.sigmoid(gate)
    silu_gate = gate * sigmoid_gate
    act = (silu_gate * upper).astype(BF16)
    act_grad = contract(slot_dz, down_rows, 1, 1)
    gate_grad = (act_grad * upper * sigmoid_gate * (1.0 + gate * (1.0 - sigmoid_gate))).astype(BF16)
    up_grad = (act_grad * silu_gate).astype(BF16)
    grad_down = contract(act, slot_dz, 0, 0).astype(BF16)
    grad_gate = contract(gate_grad, slot_x, 0, 0).astype(BF16)
    grad_up = contract(up_grad, slot_x, 0, 0).astype(BF16)
    hidden_terms = contract(gate_grad, gate_rows, 1, 0) + contract(up_grad, up_rows, 1, 0)
    rounded = hidden_terms.astype(BF16).reshape(dp_size, capacity, model_width)
    hidden_sum = lax.psum_scatter(rounded, "et", scatter_dimension=1, tiled=True)
    slot_share = lax.psum_scatter(hidden_sum, "dp", scatter_dimension=0, tiled=True)
    slot_grad = lax.all_gather(slot_share, "et", axis=1, tiled=True)[0]
    start = lax.axis_index("et") * tok_dev
    my_position = lax.dynamic_slice_in_dim(own_position, start, tok_dev)
    my_routed = lax.dynamic_slice_in_dim(own_routed, start, tok_dev)
    picked = jnp.take(slot_grad, jnp.maximum(my_position, 0), axis=0)
    input_grad = jnp.where(my_routed[:, None], picked, jnp.zeros_like(picked))
    handed = from_behind(input_grad[None, None], "pipe", -1)
    return (handed, grad_gate[None], grad_up[None], grad_down[None])


def call(kernel, outs, *args, scratch=(), flops=0, vmem=16, space=VMEM, aliases=None):
    moved = 0
    if space is HBM or flops:
        moved = sum(a.size * a.dtype.itemsize for a in args)
        moved += sum(o.size * o.dtype.itemsize for o in outs)
    if space is HBM:
        args = [pltpu.with_memory_space_constraint(a, pltpu.HBM) for a in args]
    return pl.pallas_call(
        kernel,
        out_shape=outs,
        in_specs=[space] * len(args),
        out_specs=[VMEM] * len(outs),
        scratch_shapes=list(scratch),
        input_output_aliases=aliases or {},
        compiler_params=pltpu.CompilerParams(vmem_limit_bytes=vmem * 2**20),
        cost_estimate=pl.CostEstimate(flops=flops, bytes_accessed=moved, transcendentals=0),
    )(*args)


def like(shape, dtype=BF16):
    return jax.ShapeDtypeStruct(shape, dtype)


def spread(steps):
    return [(e, e ^ steps) for e in range(4)]


def bring(sources, targets, sems):
    copies = [
        pltpu.make_async_copy(source, target, sems.at[i])
        for i, (source, target) in enumerate(zip(sources, targets))
    ]
    for copy in copies:
        copy.start()
    return copies


def stage_kernel(*refs):
    weights, outs, sems = refs[:3], refs[3:6], refs[6]
    third = weights[0].shape[0] // 3
    sources, targets = [], []
    for weight, out in zip(weights, outs):
        for part in range(3):
            rows = pl.ds(part * third, third)
            sources.append(weight.at[rows, :])
            targets.append(out.at[rows, :])
    for copy in bring(sources, targets, sems):
        copy.wait()


def pack_kernel(*refs):
    outs, (x_ref, dz_ref, ids_ref, probs_ref, sems) = refs[4:8], refs[8:]
    for copy in bring(refs[:4], refs[8:12], sems):
        copy.wait()
    rows, width = x_ref.shape
    piece = width // 4
    e = lax.axis_index("et")
    chosen = ids_ref[...] == 0
    weight_row = jnp.sum(jnp.where(chosen, probs_ref[...], 0.0), axis=0, keepdims=True)
    flag_row = jnp.max(jnp.where(chosen, 1.0, 0.0), axis=0, keepdims=True)
    on_diagonal = lax.broadcasted_iota(jnp.int32, (rows, rows), 0) == lax.broadcasted_iota(
        jnp.int32, (rows, rows), 1
    )
    weight = jnp.sum(jnp.where(on_diagonal, weight_row, 0.0), axis=1, keepdims=True)
    flag = jnp.sum(jnp.where(on_diagonal, flag_row, 0.0), axis=1, keepdims=True)
    for steps, out in enumerate(outs):
        start = pl.multiple_of((e ^ steps) * piece, 128)
        out[:, :piece] = x_ref[:, pl.ds(start, piece)]
        out[:, piece : 2 * piece] = (weight * dz_ref[:, pl.ds(start, piece)].astype(F32)).astype(BF16)
        out[:, 2 * piece :] = jnp.broadcast_to(flag, (rows, FLAG)).astype(BF16)


def compact_kernel(*refs):
    parts, (slots_ref, pick_ref, all_rows) = refs[:4], refs[4:]
    rows, wide = parts[0].shape
    tokens = 4 * rows
    data = wide - FLAG
    cap = slots_ref.shape[0]
    e = lax.axis_index("et")
    for steps, part in enumerate(parts):
        all_rows[pl.ds(pl.multiple_of((e ^ steps) * rows, 16), rows), :] = part[...]
    flags = all_rows[:, data:]
    before = lax.broadcasted_iota(jnp.int32, (tokens, tokens), 0)
    after = lax.broadcasted_iota(jnp.int32, (tokens, tokens), 1)
    count = contract(flags, (before <= after).astype(F32).astype(BF16), 0, 0)[:cap]
    here = contract(flags, (before == after).astype(F32).astype(BF16), 0, 0)[:cap]
    slot = lax.broadcasted_iota(jnp.int32, (cap, tokens), 0).astype(F32)
    pick = jnp.where((count - 1.0 == slot) & (here > 0.5), 1.0, 0.0).astype(BF16)
    slots_ref[...] = jnp.dot(pick, all_rows[:, :data], preferred_element_type=F32).astype(BF16)
    pick_ref[...] = jnp.zeros_like(pick_ref)
    pick_ref[:, :tokens] = pick


def add_quarter(steps, blocks, x_ref, dz_ref, weights):
    piece = blocks[0].shape[1] // 2
    columns = pl.ds(pl.multiple_of((lax.axis_index("et") ^ steps) * piece, 128), piece)
    start = 0
    for block in blocks:
        rows = pl.ds(start, block.shape[0])
        x_ref[rows, columns] = block[:, :piece]
        dz_ref[rows, columns] = block[:, piece:]
        start += block.shape[0]
    wg_ref, wu_ref, wd_ref = weights
    x, dz = x_ref[:, columns], dz_ref[:, columns]
    return (
        contract(x, wg_ref[:, columns], 1, 1),
        contract(x, wu_ref[:, columns], 1, 1),
        contract(dz, wd_ref[:, columns], 1, 1),
    )


def first_kernel(*refs):
    weights, (x_ref, dz_ref, *sums) = refs[12:15], refs[15:]
    for steps in range(3):
        parts = add_quarter(steps, refs[4 * steps : 4 * steps + 4], x_ref, dz_ref, weights)
        for out, part in zip(sums, parts):
            out[...] = out[...] + part if steps else part


def half_terms(other, gate_grad, up_grad, weights, half):
    side = lax.axis_index("et") % 2 ^ other
    columns = pl.ds(pl.multiple_of(side * half, 128), half)
    terms = contract(gate_grad, weights[0][:, columns], 1, 0)
    return terms + contract(up_grad, weights[1][:, columns], 1, 0)


def third_kernel(*refs):
    both, weights, olds, outs = refs[:4], refs[4:7], refs[9:12], refs[12:]
    x_ref, dz_ref, act_ref, gg_ref, ug_ref, grads_ref, away_ref = outs
    slots = x_ref.shape[0]
    parts = add_quarter(3, both, x_ref, dz_ref, weights)
    gate, upper, act_grad = (old[...] + part for old, part in zip(olds, parts))
    sigmoid_gate = jax.nn.sigmoid(gate)
    silu_gate = gate * sigmoid_gate
    gate_grad = (act_grad * upper * sigmoid_gate * (1.0 + gate * (1.0 - sigmoid_gate))).astype(BF16)
    up_grad = (act_grad * silu_gate).astype(BF16)
    gg_ref[...] = gate_grad
    ug_ref[...] = up_grad
    act_ref[...] = (silu_gate * upper).astype(BF16)
    grads_ref[:slots, :] = gate_grad
    grads_ref[slots:, :] = up_grad
    away_ref[...] = half_terms(1, gate_grad, up_grad, weights, away_ref.shape[1]).astype(BF16)


def own_terms_kernel(grads_ref, wg_ref, wu_ref, out_ref):
    slots, half = out_ref.shape
    grads = grads_ref[:slots, :], grads_ref[slots:, :]
    out_ref[...] = half_terms(0, *grads, (wg_ref, wu_ref), half)


def pair_kernel(own_ref, other_ref, pick_ref, *refs):
    outs, ready_ref = refs[:4], refs[4]
    cap, half = outs[0].shape
    for k, out in enumerate(outs):
        rows = pl.ds(k * cap, cap)
        out[:, :half] = (own_ref[rows, :] + other_ref[rows, :].astype(F32)).astype(BF16)
    outs[3][:, half:] = pick_ref[...]
    ready_ref[...] = jnp.zeros_like(ready_ref)


def add_kernel(left_ref, right_ref, near_ref, first_ref, out_ref, pass_ref, ready_ref):
    out_ref[...] = (left_ref[...].astype(F32) + right_ref[...].astype(F32)).astype(BF16)
    pass_ref[...] = near_ref[...]
    ready_ref[...] = first_ref[...]


def expand_kernel(own_ref, ready_ref, *refs):
    others, outs, tokens_ref = refs[:2], refs[2:6], refs[6]
    rows, half = outs[0].shape
    e = lax.axis_index("et")
    total = own_ref[:, :half].astype(F32)
    for other in others:
        total += other[...].astype(F32)
    tokens_ref[...] = contract(own_ref[:, half:], total.astype(BF16), 0, 0).astype(BF16)
    for steps, out in enumerate(outs):
        out[...] = tokens_ref[pl.ds(pl.multiple_of((e ^ steps) * rows, 16), rows), :]


def finish_kernel(own_ref, core_ref, chip_ref, both_ref, out_ref):
    half = own_ref.shape[1]
    core = lax.axis_index("et") % 2
    mine = own_ref[...].astype(F32) + chip_ref[...].astype(F32)
    out_ref[:, pl.ds(pl.multiple_of(core * half, 128), half)] = mine.astype(BF16)
    theirs = core_ref[...].astype(F32) + both_ref[...].astype(F32)
    out_ref[:, pl.ds(pl.multiple_of((1 - core) * half, 128), half)] = theirs.astype(BF16)


def swap(value, axis, steps):
    return lax.ppermute(value, axis, spread(steps))


def hand(value, pipe_size, steps):
    pairs = [
        (4 * p + z, 4 * ((p - 1) % pipe_size) + (z ^ steps)) for p in range(pipe_size) for z in range(4)
    ]
    return lax.ppermute(value, ("pipe", "dp"), pairs)


def on_device_four(tokens, out_grad, top_ids, route_probs, w_gate, w_up, w_down):
    rows, width = tokens.shape[2:]
    hidden = w_gate.shape[1]
    top = top_ids.shape[3]
    pipe_size = lax.axis_size("pipe")
    cap = 2 * rows
    slots = 4 * cap
    piece, half = width // 4, width // 2

    packed = call(
        pack_kernel,
        [like((rows, 2 * piece + FLAG))] * 4,
        tokens[0, 0],
        out_grad[0, 0],
        top_ids[0, 0].T,
        route_probs[0, 0].T,
        scratch=[
            pltpu.VMEM((rows, width), BF16),
            pltpu.VMEM((rows, width), BF16),
            pltpu.VMEM((top, rows), jnp.int32),
            pltpu.VMEM((top, rows), F32),
            pltpu.SemaphoreType.DMA((4,)),
        ],
        space=HBM,
    )
    arrived = [packed[0]] + [swap(packed[s], "et", s) for s in (1, 2, 3)]
    weights = call(
        stage_kernel,
        [like((hidden, width))] * 3,
        w_gate[0],
        w_up[0],
        w_down[0],
        scratch=[pltpu.SemaphoreType.DMA((9,))],
        space=HBM,
    )
    arrived, weights = lax.optimization_barrier((arrived, weights))
    slot_block, pick = call(
        compact_kernel,
        [like((cap, 2 * piece)), like((cap, FLAG))],
        *arrived,
        scratch=[pltpu.VMEM((4 * rows, 2 * piece + FLAG), BF16)],
    )
    diag = swap(slot_block, "dp", 3)
    near = swap(slot_block, "dp", 1)
    far = swap(slot_block, "dp", 2)
    own = [diag, near, far, slot_block]
    chip = [swap(block, "et", 2) for block in own]
    core = [swap(block, "et", 1) for block in own]
    both = [swap(block, "et", 1) for block in chip]
    wide, sums = [like((slots, width))] * 2, [like((slots, hidden), F32)] * 3
    state = call(first_kernel, wide + sums, *own, *core, *chip, *weights, vmem=32)
    x, dz, act, gate_grad, up_grad, grads, away = call(
        third_kernel,
        wide + [like((slots, hidden))] * 3 + [like((2 * slots, hidden)), like((slots, half))],
        *both,
        *weights,
        *state,
        vmem=32,
        aliases={7: 0, 8: 1},
    )
    theirs = swap(away, "et", 1)
    (own_terms,) = call(
        own_terms_kernel,
        [like((slots, half), F32)],
        grads,
        *weights[:2],
        flops=4 * slots * hidden * half,
        vmem=32,
    )
    to_last, to_near, to_far, home, first = call(
        pair_kernel,
        [like((cap, half))] * 3 + [like((cap, half + FLAG)), like((8, 128), F32)],
        own_terms,
        theirs,
        pick,
    )
    from_last = swap(to_last, "dp", 1)
    home = hand(home, pipe_size, 0)
    x, dz, act, gate_grad, up_grad, first = lax.optimization_barrier(
        (x, dz, act, gate_grad, up_grad, first)
    )
    grad_down = contract(act, dz, 0, 0).astype(BF16)
    from_last, grad_down = lax.optimization_barrier((from_last, grad_down))
    to_far, to_near, ready = call(
        add_kernel,
        [like((cap, half))] * 2 + [like((8, 128), F32)],
        to_far,
        from_last,
        to_near,
        first,
    )
    x, dz, act, gate_grad, up_grad, ready = lax.optimization_barrier(
        (x, dz, act, gate_grad, up_grad, ready)
    )
    grad_gate = contract(gate_grad, x, 0, 0).astype(BF16)
    from_far = hand(to_far, pipe_size, 2)
    from_near = hand(to_near, pipe_size, 1)
    from_far, grad_gate = lax.optimization_barrier((from_far, grad_gate))
    by_token = call(
        expand_kernel,
        [like((rows, half))] * 4,
        home,
        ready,
        from_far,
        from_near,
        scratch=[pltpu.VMEM((FLAG, half), BF16)],
    )
    back = [by_token[0]] + [swap(by_token[s], "et", s) for s in (1, 2, 3)]
    (handed,) = call(finish_kernel, [like((rows, width))], *back)
    grad_up = contract(up_grad, x, 0, 0).astype(BF16)
    return (handed[None, None], grad_gate[None], grad_up[None], grad_down[None])


def solution(mesh):
    placed = (
        P("pipe", "dp", "et", None),
        P("pipe", "dp", "et", None),
        P("pipe", "dp", "et", None),
        P("pipe", "dp", "et", None),
        P("pipe", ("dp", "et"), None),
        P("pipe", ("dp", "et"), None),
        P("pipe", ("dp", "et"), None),
    )
    four = mesh.shape["et"] == 4 and mesh.shape["dp"] == 4
    return jax.shard_map(
        on_device_four if four else on_device_any,
        mesh=mesh,
        in_specs=placed,
        out_specs=(
            P("pipe", "dp", "et", None),
            P("pipe", ("dp", "et"), None),
            P("pipe", ("dp", "et"), None),
            P("pipe", ("dp", "et"), None),
        ),
        check_vma=False,
    )
```

```python
import functools

import jax
import jax.numpy as jnp
from jax import lax
from jax.experimental import pallas as pl
from jax.experimental.pallas import tpu as pltpu
from jax.sharding import PartitionSpec as P

FLAG = 128
BF16 = jnp.bfloat16
F32 = jnp.float32
VMEM = pl.BlockSpec(memory_space=pltpu.VMEM)
HBM = pl.BlockSpec(memory_space=pltpu.HBM)


def from_behind(value, axis, steps):
    count = lax.axis_size(axis)
    pairs = [(source, (source + steps) % count) for source in range(count)]
    return lax.ppermute(value, axis, pairs)


def slot_layout(routed, capacity):
    flags = routed.astype(jnp.int32)
    position = jnp.cumsum(flags, axis=-1, dtype=jnp.int32) - 1
    slot_ids = jnp.arange(capacity, dtype=jnp.int32)
    matches = (position[:, None, :] == slot_ids[None, :, None]) & routed[:, None, :]
    token_ids = jnp.arange(routed.shape[-1], dtype=jnp.int32)
    source = jnp.sum(jnp.where(matches, token_ids[None, None, :], 0), axis=-1)
    filled = jnp.any(matches, axis=-1)
    return (source, filled, position)


def gather_slots(rows, source, filled):
    picked = jnp.take_along_axis(rows, source[:, :, None], axis=1)
    return jnp.where(filled[:, :, None], picked, jnp.zeros_like(picked))


def contract(left, right, left_dim, right_dim):
    return lax.dot_general(
        left, right, (((left_dim,), (right_dim,)), ((), ())), preferred_element_type=F32
    )


def on_device_any(tokens, out_grad, top_ids, route_probs, w_gate, w_up, w_down):
    tok_dev = tokens.shape[2]
    model_width = tokens.shape[3]
    et_size = lax.axis_size("et")
    dp_size = lax.axis_size("dp")
    group_tokens = tok_dev * et_size
    capacity = group_tokens // 2
    token_rows = tokens[0, 0]
    chosen = top_ids[0, 0] == 0
    routed_flag = jnp.any(chosen, axis=-1).astype(BF16)
    route_weight = jnp.sum(jnp.where(chosen, route_probs[0, 0], F32(0.0)), axis=-1)
    scaled_rows = (route_weight[:, None] * out_grad[0, 0].astype(F32)).astype(BF16)
    group_x, group_dz, group_flag = (
        lax.all_gather(token_rows, "et", axis=0, tiled=True),
        lax.all_gather(scaled_rows, "et", axis=0, tiled=True),
        lax.all_gather(routed_flag, "et", axis=0, tiled=True),
    )
    routed = group_flag[None, :] > 0
    source, filled, position = slot_layout(routed, capacity)
    own_x = gather_slots(group_x[None], source, filled)
    own_dz = gather_slots(group_dz[None], source, filled)
    all_x, all_dz = (
        lax.all_gather(own_x, "dp", axis=0, tiled=True),
        lax.all_gather(own_dz, "dp", axis=0, tiled=True),
    )
    own_position = position[0]
    own_routed = routed[0]
    slot_x = all_x.reshape(dp_size * capacity, model_width)
    slot_dz = all_dz.reshape(dp_size * capacity, model_width)
    gate_rows = w_gate[0]
    up_rows = w_up[0]
    down_rows = w_down[0]
    gate = contract(slot_x, gate_rows, 1, 1)
    upper = contract(slot_x, up_rows, 1, 1)
    sigmoid_gate = jax.nn.sigmoid(gate)
    silu_gate = gate * sigmoid_gate
    act = (silu_gate * upper).astype(BF16)
    act_grad = contract(slot_dz, down_rows, 1, 1)
    gate_grad = (act_grad * upper * sigmoid_gate * (1.0 + gate * (1.0 - sigmoid_gate))).astype(BF16)
    up_grad = (act_grad * silu_gate).astype(BF16)
    grad_down = contract(act, slot_dz, 0, 0).astype(BF16)
    grad_gate = contract(gate_grad, slot_x, 0, 0).astype(BF16)
    grad_up = contract(up_grad, slot_x, 0, 0).astype(BF16)
    hidden_terms = contract(gate_grad, gate_rows, 1, 0) + contract(up_grad, up_rows, 1, 0)
    rounded = hidden_terms.astype(BF16).reshape(dp_size, capacity, model_width)
    hidden_sum = lax.psum_scatter(rounded, "et", scatter_dimension=1, tiled=True)
    slot_share = lax.psum_scatter(hidden_sum, "dp", scatter_dimension=0, tiled=True)
    slot_grad = lax.all_gather(slot_share, "et", axis=1, tiled=True)[0]
    start = lax.axis_index("et") * tok_dev
    my_position = lax.dynamic_slice_in_dim(own_position, start, tok_dev)
    my_routed = lax.dynamic_slice_in_dim(own_routed, start, tok_dev)
    picked = jnp.take(slot_grad, jnp.maximum(my_position, 0), axis=0)
    input_grad = jnp.where(my_routed[:, None], picked, jnp.zeros_like(picked))
    handed = from_behind(input_grad[None, None], "pipe", -1)
    return (handed, grad_gate[None], grad_up[None], grad_down[None])


def call(kernel, outs, *args, scratch=(), flops=0, vmem=16, space=VMEM, aliases=None):
    moved = 0
    if space is HBM or flops:
        moved = sum(a.size * a.dtype.itemsize for a in args)
        moved += sum(o.size * o.dtype.itemsize for o in outs)
    if space is HBM:
        args = [pltpu.with_memory_space_constraint(a, pltpu.HBM) for a in args]
    return pl.pallas_call(
        kernel,
        out_shape=outs,
        in_specs=[space] * len(args),
        out_specs=[VMEM] * len(outs),
        scratch_shapes=list(scratch),
        input_output_aliases=aliases or {},
        compiler_params=pltpu.CompilerParams(vmem_limit_bytes=vmem * 2**20),
        cost_estimate=pl.CostEstimate(flops=flops, bytes_accessed=moved, transcendentals=0),
    )(*args)


def like(shape, dtype=BF16):
    return jax.ShapeDtypeStruct(shape, dtype)


def spread(steps):
    return [(e, e ^ steps) for e in range(4)]


def bring(sources, targets, sems):
    copies = [
        pltpu.make_async_copy(source, target, sems.at[i])
        for i, (source, target) in enumerate(zip(sources, targets))
    ]
    for copy in copies:
        copy.start()
    return copies


def stage_kernel(*refs):
    weights, outs, sems = refs[:3], refs[3:6], refs[6]
    third = weights[0].shape[0] // 3
    sources, targets = [], []
    for weight, out in zip(weights, outs):
        for part in range(3):
            rows = pl.ds(part * third, third)
            sources.append(weight.at[rows, :])
            targets.append(out.at[rows, :])
    for copy in bring(sources, targets, sems):
        copy.wait()


def pack_kernel(*refs):
    outs, (x_ref, dz_ref, ids_ref, probs_ref, sems) = refs[4:8], refs[8:]
    for copy in bring(refs[:4], refs[8:12], sems):
        copy.wait()
    rows, width = x_ref.shape
    piece = width // 4
    e = lax.axis_index("et")
    chosen = ids_ref[...] == 0
    weight_row = jnp.sum(jnp.where(chosen, probs_ref[...], 0.0), axis=0, keepdims=True)
    flag_row = jnp.max(jnp.where(chosen, 1.0, 0.0), axis=0, keepdims=True)
    on_diagonal = lax.broadcasted_iota(jnp.int32, (rows, rows), 0) == lax.broadcasted_iota(
        jnp.int32, (rows, rows), 1
    )
    weight = jnp.sum(jnp.where(on_diagonal, weight_row, 0.0), axis=1, keepdims=True)
    flag = jnp.sum(jnp.where(on_diagonal, flag_row, 0.0), axis=1, keepdims=True)
    for steps, out in enumerate(outs):
        start = pl.multiple_of((e ^ steps) * piece, 128)
        out[:, :piece] = x_ref[:, pl.ds(start, piece)]
        out[:, piece : 2 * piece] = (weight * dz_ref[:, pl.ds(start, piece)].astype(F32)).astype(BF16)
        out[:, 2 * piece :] = jnp.broadcast_to(flag, (rows, FLAG)).astype(BF16)


def compact_kernel(*refs):
    parts, (slots_ref, pick_ref, all_rows) = refs[:4], refs[4:]
    rows, wide = parts[0].shape
    tokens = 4 * rows
    data = wide - FLAG
    cap = slots_ref.shape[0]
    e = lax.axis_index("et")
    for steps, part in enumerate(parts):
        all_rows[pl.ds(pl.multiple_of((e ^ steps) * rows, 16), rows), :] = part[...]
    flags = all_rows[:, data:]
    before = lax.broadcasted_iota(jnp.int32, (tokens, tokens), 0)
    after = lax.broadcasted_iota(jnp.int32, (tokens, tokens), 1)
    count = contract(flags, (before <= after).astype(F32).astype(BF16), 0, 0)[:cap]
    here = contract(flags, (before == after).astype(F32).astype(BF16), 0, 0)[:cap]
    slot = lax.broadcasted_iota(jnp.int32, (cap, tokens), 0).astype(F32)
    pick = jnp.where((count - 1.0 == slot) & (here > 0.5), 1.0, 0.0).astype(BF16)
    slots_ref[...] = jnp.dot(pick, all_rows[:, :data], preferred_element_type=F32).astype(BF16)
    pick_ref[...] = jnp.zeros_like(pick_ref)
    pick_ref[:, :tokens] = pick


def add_quarter(steps, blocks, x_ref, dz_ref, weights):
    piece = blocks[0].shape[1] // 2
    columns = pl.ds(pl.multiple_of((lax.axis_index("et") ^ steps) * piece, 128), piece)
    start = 0
    for block in blocks:
        rows = pl.ds(start, block.shape[0])
        x_ref[rows, columns] = block[:, :piece]
        dz_ref[rows, columns] = block[:, piece:]
        start += block.shape[0]
    wg_ref, wu_ref, wd_ref = weights
    x, dz = x_ref[:, columns], dz_ref[:, columns]
    return (
        contract(x, wg_ref[:, columns], 1, 1),
        contract(x, wu_ref[:, columns], 1, 1),
        contract(dz, wd_ref[:, columns], 1, 1),
    )


def first_kernel(*refs):
    own, weights, (x_ref, dz_ref, *sums) = refs[:4], refs[4:7], refs[7:]
    for out, part in zip(sums, add_quarter(0, own, x_ref, dz_ref, weights)):
        out[...] = part


def second_kernel(*refs):
    core, chip, weights, olds = refs[:4], refs[4:8], refs[8:11], refs[13:16]
    x_ref, dz_ref, *sums = refs[16:]
    parts = add_quarter(1, core, x_ref, dz_ref, weights)
    more = add_quarter(2, chip, x_ref, dz_ref, weights)
    for out, old, part, other in zip(sums, olds, parts, more):
        out[...] = old[...] + part + other


def half_terms(other, gate_grad, up_grad, weights, half):
    side = lax.axis_index("et") % 2 ^ other
    columns = pl.ds(pl.multiple_of(side * half, 128), half)
    terms = contract(gate_grad, weights[0][:, columns], 1, 0)
    return terms + contract(up_grad, weights[1][:, columns], 1, 0)


def third_kernel(*refs):
    both, weights, olds, outs = refs[:4], refs[4:7], refs[9:12], refs[12:]
    x_ref, dz_ref, act_ref, gg_ref, ug_ref, grads_ref, away_ref = outs
    slots = x_ref.shape[0]
    parts = add_quarter(3, both, x_ref, dz_ref, weights)
    gate, upper, act_grad = (old[...] + part for old, part in zip(olds, parts))
    sigmoid_gate = jax.nn.sigmoid(gate)
    silu_gate = gate * sigmoid_gate
    gate_grad = (act_grad * upper * sigmoid_gate * (1.0 + gate * (1.0 - sigmoid_gate))).astype(BF16)
    up_grad = (act_grad * silu_gate).astype(BF16)
    gg_ref[...] = gate_grad
    ug_ref[...] = up_grad
    act_ref[...] = (silu_gate * upper).astype(BF16)
    grads_ref[:slots, :] = gate_grad
    grads_ref[slots:, :] = up_grad
    away_ref[...] = half_terms(1, gate_grad, up_grad, weights, away_ref.shape[1]).astype(BF16)


def own_terms_kernel(grads_ref, wg_ref, wu_ref, out_ref):
    slots, half = out_ref.shape
    grads = grads_ref[:slots, :], grads_ref[slots:, :]
    out_ref[...] = half_terms(0, *grads, (wg_ref, wu_ref), half)


def pair_kernel(own_ref, other_ref, pick_ref, *refs):
    outs, ready_ref = refs[:4], refs[4]
    cap, half = outs[0].shape
    for k, out in enumerate(outs):
        rows = pl.ds(k * cap, cap)
        out[:, :half] = (own_ref[rows, :] + other_ref[rows, :].astype(F32)).astype(BF16)
    outs[3][:, half:] = pick_ref[...]
    ready_ref[...] = jnp.zeros_like(ready_ref)


def add_kernel(left_ref, right_ref, near_ref, first_ref, out_ref, pass_ref, ready_ref):
    out_ref[...] = (left_ref[...].astype(F32) + right_ref[...].astype(F32)).astype(BF16)
    pass_ref[...] = near_ref[...]
    ready_ref[...] = first_ref[...]


def expand_kernel(own_ref, ready_ref, *refs):
    others, outs, tokens_ref = refs[:2], refs[2:6], refs[6]
    rows, half = outs[0].shape
    e = lax.axis_index("et")
    total = own_ref[:, :half].astype(F32)
    for other in others:
        total += other[...].astype(F32)
    tokens_ref[...] = contract(own_ref[:, half:], total.astype(BF16), 0, 0).astype(BF16)
    for steps, out in enumerate(outs):
        out[...] = tokens_ref[pl.ds(pl.multiple_of((e ^ steps) * rows, 16), rows), :]


def finish_kernel(own_ref, core_ref, chip_ref, both_ref, out_ref):
    half = own_ref.shape[1]
    core = lax.axis_index("et") % 2
    mine = own_ref[...].astype(F32) + chip_ref[...].astype(F32)
    out_ref[:, pl.ds(pl.multiple_of(core * half, 128), half)] = mine.astype(BF16)
    theirs = core_ref[...].astype(F32) + both_ref[...].astype(F32)
    out_ref[:, pl.ds(pl.multiple_of((1 - core) * half, 128), half)] = theirs.astype(BF16)


def swap(value, axis, steps):
    return lax.ppermute(value, axis, spread(steps))


def hand(value, pipe_size, steps):
    pairs = [
        (4 * p + z, 4 * ((p - 1) % pipe_size) + (z ^ steps)) for p in range(pipe_size) for z in range(4)
    ]
    return lax.ppermute(value, ("pipe", "dp"), pairs)


def on_device_four(tokens, out_grad, top_ids, route_probs, w_gate, w_up, w_down):
    rows, width = tokens.shape[2:]
    hidden = w_gate.shape[1]
    top = top_ids.shape[3]
    pipe_size = lax.axis_size("pipe")
    cap = 2 * rows
    slots = 4 * cap
    piece, half = width // 4, width // 2

    packed = call(
        pack_kernel,
        [like((rows, 2 * piece + FLAG))] * 4,
        tokens[0, 0],
        out_grad[0, 0],
        top_ids[0, 0].T,
        route_probs[0, 0].T,
        scratch=[
            pltpu.VMEM((rows, width), BF16),
            pltpu.VMEM((rows, width), BF16),
            pltpu.VMEM((top, rows), jnp.int32),
            pltpu.VMEM((top, rows), F32),
            pltpu.SemaphoreType.DMA((4,)),
        ],
        space=HBM,
    )
    arrived = [packed[0]] + [swap(packed[s], "et", s) for s in (1, 2, 3)]
    weights = call(
        stage_kernel,
        [like((hidden, width))] * 3,
        w_gate[0],
        w_up[0],
        w_down[0],
        scratch=[pltpu.SemaphoreType.DMA((9,))],
        space=HBM,
    )
    arrived, weights = lax.optimization_barrier((arrived, weights))
    slot_block, pick = call(
        compact_kernel,
        [like((cap, 2 * piece)), like((cap, FLAG))],
        *arrived,
        scratch=[pltpu.VMEM((4 * rows, 2 * piece + FLAG), BF16)],
    )
    diag = swap(slot_block, "dp", 3)
    near = swap(slot_block, "dp", 1)
    far = swap(slot_block, "dp", 2)
    own = [far, diag, near, slot_block]
    chip = [swap(block, "et", 2) for block in own]
    core = [swap(block, "et", 1) for block in own]
    wide, sums = [like((slots, width))] * 2, [like((slots, hidden), F32)] * 3
    state = call(first_kernel, wide + sums, *own, *weights, vmem=32)
    chip[0], state = lax.optimization_barrier((chip[0], state))
    both = [swap(block, "et", 1) for block in chip]
    state = call(
        second_kernel,
        wide + sums,
        *core,
        *chip,
        *weights,
        *state,
        vmem=32,
        aliases={11 + i: i for i in range(5)},
    )
    x, dz, act, gate_grad, up_grad, grads, away = call(
        third_kernel,
        wide + [like((slots, hidden))] * 3 + [like((2 * slots, hidden)), like((slots, half))],
        *both,
        *weights,
        *state,
        vmem=32,
        aliases={7: 0, 8: 1},
    )
    theirs = swap(away, "et", 1)
    (own_terms,) = call(
        own_terms_kernel,
        [like((slots, half), F32)],
        grads,
        *weights[:2],
        flops=4 * slots * hidden * half,
        vmem=32,
    )
    to_far, to_last, to_near, home, first = call(
        pair_kernel,
        [like((cap, half))] * 3 + [like((cap, half + FLAG)), like((8, 128), F32)],
        own_terms,
        theirs,
        pick,
    )
    from_last = swap(to_last, "dp", 1)
    home = hand(home, pipe_size, 0)
    x, dz, act, gate_grad, up_grad, first = lax.optimization_barrier(
        (x, dz, act, gate_grad, up_grad, first)
    )
    grad_down = contract(act, dz, 0, 0).astype(BF16)
    from_last, grad_down = lax.optimization_barrier((from_last, grad_down))
    to_far, to_near, ready = call(
        add_kernel,
        [like((cap, half))] * 2 + [like((8, 128), F32)],
        to_far,
        from_last,
        to_near,
        first,
    )
    x, dz, act, gate_grad, up_grad, ready = lax.optimization_barrier(
        (x, dz, act, gate_grad, up_grad, ready)
    )
    grad_gate = contract(gate_grad, x, 0, 0).astype(BF16)
    from_far = hand(to_far, pipe_size, 2)
    from_near = hand(to_near, pipe_size, 1)
    from_far, grad_gate = lax.optimization_barrier((from_far, grad_gate))
    by_token = call(
        expand_kernel,
        [like((rows, half))] * 4,
        home,
        ready,
        from_far,
        from_near,
        scratch=[pltpu.VMEM((FLAG, half), BF16)],
    )
    back = [by_token[0]] + [swap(by_token[s], "et", s) for s in (1, 2, 3)]
    (handed,) = call(finish_kernel, [like((rows, width))], *back)
    grad_up = contract(up_grad, x, 0, 0).astype(BF16)
    return (handed[None, None], grad_gate[None], grad_up[None], grad_down[None])


def solution(mesh):
    placed = (
        P("pipe", "dp", "et", None),
        P("pipe", "dp", "et", None),
        P("pipe", "dp", "et", None),
        P("pipe", "dp", "et", None),
        P("pipe", ("dp", "et"), None),
        P("pipe", ("dp", "et"), None),
        P("pipe", ("dp", "et"), None),
    )
    four = mesh.shape["et"] == 4 and mesh.shape["dp"] == 4
    return jax.shard_map(
        on_device_four if four else on_device_any,
        mesh=mesh,
        in_specs=placed,
        out_specs=(
            P("pipe", "dp", "et", None),
            P("pipe", ("dp", "et"), None),
            P("pipe", ("dp", "et"), None),
            P("pipe", ("dp", "et"), None),
        ),
        check_vma=False,
    )
```

```python
import functools

import jax
import jax.numpy as jnp
from jax import lax
from jax.experimental import pallas as pl
from jax.experimental.pallas import tpu as pltpu
from jax.sharding import PartitionSpec as P

FLAG = 128
BF16 = jnp.bfloat16
F32 = jnp.float32
VMEM = pl.BlockSpec(memory_space=pltpu.VMEM)
HBM = pl.BlockSpec(memory_space=pltpu.HBM)


def from_behind(value, axis, steps):
    count = lax.axis_size(axis)
    pairs = [(source, (source + steps) % count) for source in range(count)]
    return lax.ppermute(value, axis, pairs)


def slot_layout(routed, capacity):
    flags = routed.astype(jnp.int32)
    position = jnp.cumsum(flags, axis=-1, dtype=jnp.int32) - 1
    slot_ids = jnp.arange(capacity, dtype=jnp.int32)
    matches = (position[:, None, :] == slot_ids[None, :, None]) & routed[:, None, :]
    token_ids = jnp.arange(routed.shape[-1], dtype=jnp.int32)
    source = jnp.sum(jnp.where(matches, token_ids[None, None, :], 0), axis=-1)
    filled = jnp.any(matches, axis=-1)
    return (source, filled, position)


def gather_slots(rows, source, filled):
    picked = jnp.take_along_axis(rows, source[:, :, None], axis=1)
    return jnp.where(filled[:, :, None], picked, jnp.zeros_like(picked))


def contract(left, right, left_dim, right_dim):
    return lax.dot_general(
        left, right, (((left_dim,), (right_dim,)), ((), ())), preferred_element_type=F32
    )


def on_device_any(tokens, out_grad, top_ids, route_probs, w_gate, w_up, w_down):
    tok_dev = tokens.shape[2]
    model_width = tokens.shape[3]
    et_size = lax.axis_size("et")
    dp_size = lax.axis_size("dp")
    group_tokens = tok_dev * et_size
    capacity = group_tokens // 2
    token_rows = tokens[0, 0]
    chosen = top_ids[0, 0] == 0
    routed_flag = jnp.any(chosen, axis=-1).astype(BF16)
    route_weight = jnp.sum(jnp.where(chosen, route_probs[0, 0], F32(0.0)), axis=-1)
    scaled_rows = (route_weight[:, None] * out_grad[0, 0].astype(F32)).astype(BF16)
    group_x, group_dz, group_flag = (
        lax.all_gather(token_rows, "et", axis=0, tiled=True),
        lax.all_gather(scaled_rows, "et", axis=0, tiled=True),
        lax.all_gather(routed_flag, "et", axis=0, tiled=True),
    )
    routed = group_flag[None, :] > 0
    source, filled, position = slot_layout(routed, capacity)
    own_x = gather_slots(group_x[None], source, filled)
    own_dz = gather_slots(group_dz[None], source, filled)
    all_x, all_dz = (
        lax.all_gather(own_x, "dp", axis=0, tiled=True),
        lax.all_gather(own_dz, "dp", axis=0, tiled=True),
    )
    own_position = position[0]
    own_routed = routed[0]
    slot_x = all_x.reshape(dp_size * capacity, model_width)
    slot_dz = all_dz.reshape(dp_size * capacity, model_width)
    gate_rows = w_gate[0]
    up_rows = w_up[0]
    down_rows = w_down[0]
    gate = contract(slot_x, gate_rows, 1, 1)
    upper = contract(slot_x, up_rows, 1, 1)
    sigmoid_gate = jax.nn.sigmoid(gate)
    silu_gate = gate * sigmoid_gate
    act = (silu_gate * upper).astype(BF16)
    act_grad = contract(slot_dz, down_rows, 1, 1)
    gate_grad = (act_grad * upper * sigmoid_gate * (1.0 + gate * (1.0 - sigmoid_gate))).astype(BF16)
    up_grad = (act_grad * silu_gate).astype(BF16)
    grad_down = contract(act, slot_dz, 0, 0).astype(BF16)
    grad_gate = contract(gate_grad, slot_x, 0, 0).astype(BF16)
    grad_up = contract(up_grad, slot_x, 0, 0).astype(BF16)
    hidden_terms = contract(gate_grad, gate_rows, 1, 0) + contract(up_grad, up_rows, 1, 0)
    rounded = hidden_terms.astype(BF16).reshape(dp_size, capacity, model_width)
    hidden_sum = lax.psum_scatter(rounded, "et", scatter_dimension=1, tiled=True)
    slot_share = lax.psum_scatter(hidden_sum, "dp", scatter_dimension=0, tiled=True)
    slot_grad = lax.all_gather(slot_share, "et", axis=1, tiled=True)[0]
    start = lax.axis_index("et") * tok_dev
    my_position = lax.dynamic_slice_in_dim(own_position, start, tok_dev)
    my_routed = lax.dynamic_slice_in_dim(own_routed, start, tok_dev)
    picked = jnp.take(slot_grad, jnp.maximum(my_position, 0), axis=0)
    input_grad = jnp.where(my_routed[:, None], picked, jnp.zeros_like(picked))
    handed = from_behind(input_grad[None, None], "pipe", -1)
    return (handed, grad_gate[None], grad_up[None], grad_down[None])


def call(kernel, outs, *args, scratch=(), flops=0, vmem=16, space=VMEM, aliases=None):
    moved = 0
    if space is HBM or flops:
        moved = sum(a.size * a.dtype.itemsize for a in args)
        moved += sum(o.size * o.dtype.itemsize for o in outs)
    if space is HBM:
        args = [pltpu.with_memory_space_constraint(a, pltpu.HBM) for a in args]
    return pl.pallas_call(
        kernel,
        out_shape=outs,
        in_specs=[space] * len(args),
        out_specs=[VMEM] * len(outs),
        scratch_shapes=list(scratch),
        input_output_aliases=aliases or {},
        compiler_params=pltpu.CompilerParams(vmem_limit_bytes=vmem * 2**20),
        cost_estimate=pl.CostEstimate(flops=flops, bytes_accessed=moved, transcendentals=0),
    )(*args)


def like(shape, dtype=BF16):
    return jax.ShapeDtypeStruct(shape, dtype)


def spread(steps):
    return [(e, e ^ steps) for e in range(4)]


def bring(sources, targets, sems):
    copies = [
        pltpu.make_async_copy(source, target, sems.at[i])
        for i, (source, target) in enumerate(zip(sources, targets))
    ]
    for copy in copies:
        copy.start()
    return copies


def stage_kernel(*refs):
    weights, outs, sems = refs[:3], refs[3:6], refs[6]
    third = weights[0].shape[0] // 3
    sources, targets = [], []
    for weight, out in zip(weights, outs):
        for part in range(3):
            rows = pl.ds(part * third, third)
            sources.append(weight.at[rows, :])
            targets.append(out.at[rows, :])
    for copy in bring(sources, targets, sems):
        copy.wait()


def pack_kernel(*refs):
    outs, (x_ref, dz_ref, ids_ref, probs_ref, sems) = refs[4:8], refs[8:]
    for copy in bring(refs[:4], refs[8:12], sems):
        copy.wait()
    rows, width = x_ref.shape
    piece = width // 4
    e = lax.axis_index("et")
    chosen = ids_ref[...] == 0
    weight_row = jnp.sum(jnp.where(chosen, probs_ref[...], 0.0), axis=0, keepdims=True)
    flag_row = jnp.max(jnp.where(chosen, 1.0, 0.0), axis=0, keepdims=True)
    on_diagonal = lax.broadcasted_iota(jnp.int32, (rows, rows), 0) == lax.broadcasted_iota(
        jnp.int32, (rows, rows), 1
    )
    weight = jnp.sum(jnp.where(on_diagonal, weight_row, 0.0), axis=1, keepdims=True)
    flag = jnp.sum(jnp.where(on_diagonal, flag_row, 0.0), axis=1, keepdims=True)
    for steps, out in enumerate(outs):
        start = pl.multiple_of((e ^ steps) * piece, 128)
        out[:, :piece] = x_ref[:, pl.ds(start, piece)]
        out[:, piece : 2 * piece] = (weight * dz_ref[:, pl.ds(start, piece)].astype(F32)).astype(BF16)
        out[:, 2 * piece :] = jnp.broadcast_to(flag, (rows, FLAG)).astype(BF16)


def compact_kernel(*refs):
    parts, (slots_ref, pick_ref, all_rows) = refs[:4], refs[4:]
    rows, wide = parts[0].shape
    tokens = 4 * rows
    data = wide - FLAG
    cap = slots_ref.shape[0]
    e = lax.axis_index("et")
    for steps, part in enumerate(parts):
        all_rows[pl.ds(pl.multiple_of((e ^ steps) * rows, 16), rows), :] = part[...]
    flags = all_rows[:, data:]
    before = lax.broadcasted_iota(jnp.int32, (tokens, tokens), 0)
    after = lax.broadcasted_iota(jnp.int32, (tokens, tokens), 1)
    count = contract(flags, (before <= after).astype(F32).astype(BF16), 0, 0)[:cap]
    here = contract(flags, (before == after).astype(F32).astype(BF16), 0, 0)[:cap]
    slot = lax.broadcasted_iota(jnp.int32, (cap, tokens), 0).astype(F32)
    pick = jnp.where((count - 1.0 == slot) & (here > 0.5), 1.0, 0.0).astype(BF16)
    slots_ref[...] = jnp.dot(pick, all_rows[:, :data], preferred_element_type=F32).astype(BF16)
    pick_ref[...] = jnp.zeros_like(pick_ref)
    pick_ref[:, :tokens] = pick


def add_quarter(steps, blocks, x_ref, dz_ref, weights):
    piece = blocks[0].shape[1] // 2
    columns = pl.ds(pl.multiple_of((lax.axis_index("et") ^ steps) * piece, 128), piece)
    start = 0
    for block in blocks:
        rows = pl.ds(start, block.shape[0])
        x_ref[rows, columns] = block[:, :piece]
        dz_ref[rows, columns] = block[:, piece:]
        start += block.shape[0]
    wg_ref, wu_ref, wd_ref = weights
    x, dz = x_ref[:, columns], dz_ref[:, columns]
    return (
        contract(x, wg_ref[:, columns], 1, 1),
        contract(x, wu_ref[:, columns], 1, 1),
        contract(dz, wd_ref[:, columns], 1, 1),
    )


def first_kernel(*refs):
    weights, (x_ref, dz_ref, *sums) = refs[12:15], refs[15:]
    for steps in range(3):
        parts = add_quarter(steps, refs[4 * steps : 4 * steps + 4], x_ref, dz_ref, weights)
        for out, part in zip(sums, parts):
            out[...] = out[...] + part if steps else part


def half_terms(other, gate_grad, up_grad, weights, half):
    side = lax.axis_index("et") % 2 ^ other
    columns = pl.ds(pl.multiple_of(side * half, 128), half)
    terms = contract(gate_grad, weights[0][:, columns], 1, 0)
    return terms + contract(up_grad, weights[1][:, columns], 1, 0)


def third_kernel(*refs):
    both, weights, olds, outs = refs[:4], refs[4:7], refs[9:12], refs[12:]
    x_ref, dz_ref, act_ref, gg_ref, ug_ref, grads_ref, away_ref = outs
    slots = x_ref.shape[0]
    parts = add_quarter(3, both, x_ref, dz_ref, weights)
    gate, upper, act_grad = (old[...] + part for old, part in zip(olds, parts))
    sigmoid_gate = jax.nn.sigmoid(gate)
    silu_gate = gate * sigmoid_gate
    gate_grad = (act_grad * upper * sigmoid_gate * (1.0 + gate * (1.0 - sigmoid_gate))).astype(BF16)
    up_grad = (act_grad * silu_gate).astype(BF16)
    gg_ref[...] = gate_grad
    ug_ref[...] = up_grad
    act_ref[...] = (silu_gate * upper).astype(BF16)
    grads_ref[:slots, :] = gate_grad
    grads_ref[slots:, :] = up_grad
    away_ref[...] = half_terms(1, gate_grad, up_grad, weights, away_ref.shape[1]).astype(BF16)


def own_terms_kernel(grads_ref, wg_ref, wu_ref, out_ref):
    slots, half = out_ref.shape
    grads = grads_ref[:slots, :], grads_ref[slots:, :]
    out_ref[...] = half_terms(0, *grads, (wg_ref, wu_ref), half)


def pair_kernel(own_ref, other_ref, pick_ref, *outs):
    cap, half = outs[0].shape
    for k, out in enumerate(outs):
        rows = pl.ds(k * cap, cap)
        out[:, :half] = (own_ref[rows, :] + other_ref[rows, :].astype(F32)).astype(BF16)
    outs[3][:, half:] = pick_ref[...]


def add_kernel(left_ref, right_ref, out_ref, ready_ref):
    out_ref[...] = (left_ref[...].astype(F32) + right_ref[...].astype(F32)).astype(BF16)
    ready_ref[...] = jnp.zeros_like(ready_ref)


def expand_kernel(own_ref, ready_ref, *refs):
    others, outs, tokens_ref = refs[:2], refs[2:6], refs[6]
    rows, half = outs[0].shape
    e = lax.axis_index("et")
    total = own_ref[:, :half].astype(F32)
    for other in others:
        total += other[...].astype(F32)
    tokens_ref[...] = contract(own_ref[:, half:], total.astype(BF16), 0, 0).astype(BF16)
    for steps, out in enumerate(outs):
        out[...] = tokens_ref[pl.ds(pl.multiple_of((e ^ steps) * rows, 16), rows), :]


def finish_kernel(own_ref, core_ref, chip_ref, both_ref, out_ref):
    half = own_ref.shape[1]
    core = lax.axis_index("et") % 2
    mine = own_ref[...].astype(F32) + chip_ref[...].astype(F32)
    out_ref[:, pl.ds(pl.multiple_of(core * half, 128), half)] = mine.astype(BF16)
    theirs = core_ref[...].astype(F32) + both_ref[...].astype(F32)
    out_ref[:, pl.ds(pl.multiple_of((1 - core) * half, 128), half)] = theirs.astype(BF16)


def swap(value, axis, steps):
    return lax.ppermute(value, axis, spread(steps))


def hand(value, pipe_size, steps):
    pairs = [
        (4 * p + z, 4 * ((p - 1) % pipe_size) + (z ^ steps)) for p in range(pipe_size) for z in range(4)
    ]
    return lax.ppermute(value, ("pipe", "dp"), pairs)


def on_device_four(tokens, out_grad, top_ids, route_probs, w_gate, w_up, w_down):
    rows, width = tokens.shape[2:]
    hidden = w_gate.shape[1]
    top = top_ids.shape[3]
    pipe_size = lax.axis_size("pipe")
    cap = 2 * rows
    slots = 4 * cap
    piece, half = width // 4, width // 2

    packed = call(
        pack_kernel,
        [like((rows, 2 * piece + FLAG))] * 4,
        tokens[0, 0],
        out_grad[0, 0],
        top_ids[0, 0].T,
        route_probs[0, 0].T,
        scratch=[
            pltpu.VMEM((rows, width), BF16),
            pltpu.VMEM((rows, width), BF16),
            pltpu.VMEM((top, rows), jnp.int32),
            pltpu.VMEM((top, rows), F32),
            pltpu.SemaphoreType.DMA((4,)),
        ],
        space=HBM,
    )
    arrived = [packed[0]] + [swap(packed[s], "et", s) for s in (1, 2, 3)]
    weights = call(
        stage_kernel,
        [like((hidden, width))] * 3,
        w_gate[0],
        w_up[0],
        w_down[0],
        scratch=[pltpu.SemaphoreType.DMA((9,))],
        space=HBM,
    )
    arrived, weights = lax.optimization_barrier((arrived, weights))
    slot_block, pick = call(
        compact_kernel,
        [like((cap, 2 * piece)), like((cap, FLAG))],
        *arrived,
        scratch=[pltpu.VMEM((4 * rows, 2 * piece + FLAG), BF16)],
    )
    diag = swap(slot_block, "dp", 3)
    near = swap(slot_block, "dp", 1)
    far = swap(slot_block, "dp", 2)
    own = [diag, near, far, slot_block]
    chip = [swap(block, "et", 2) for block in own]
    core = [swap(block, "et", 1) for block in own]
    both = [swap(block, "et", 1) for block in chip]
    wide, sums = [like((slots, width))] * 2, [like((slots, hidden), F32)] * 3
    state = call(first_kernel, wide + sums, *own, *core, *chip, *weights, vmem=32)
    x, dz, act, gate_grad, up_grad, grads, away = call(
        third_kernel,
        wide + [like((slots, hidden))] * 3 + [like((2 * slots, hidden)), like((slots, half))],
        *both,
        *weights,
        *state,
        vmem=32,
        aliases={7: 0, 8: 1},
    )
    theirs = swap(away, "et", 1)
    (own_terms,) = call(
        own_terms_kernel,
        [like((slots, half), F32)],
        grads,
        *weights[:2],
        flops=4 * slots * hidden * half,
        vmem=32,
    )
    to_last, to_near, to_far, home = call(
        pair_kernel,
        [like((cap, half))] * 3 + [like((cap, half + FLAG))],
        own_terms,
        theirs,
        pick,
    )
    from_last = swap(to_last, "dp", 1)
    home = hand(home, pipe_size, 0)
    from_near = hand(to_near, pipe_size, 1)
    to_far, ready = call(
        add_kernel, [like((cap, half)), like((8, 128), F32)], to_far, from_last
    )
    x, dz, act, gate_grad, up_grad, ready = lax.optimization_barrier(
        (x, dz, act, gate_grad, up_grad, ready)
    )
    grad_gate = contract(gate_grad, x, 0, 0).astype(BF16)
    grad_up = contract(up_grad, x, 0, 0).astype(BF16)
    from_far = hand(to_far, pipe_size, 2)
    from_far, grad_gate, grad_up = lax.optimization_barrier((from_far, grad_gate, grad_up))
    by_token = call(
        expand_kernel,
        [like((rows, half))] * 4,
        home,
        ready,
        from_far,
        from_near,
        scratch=[pltpu.VMEM((FLAG, half), BF16)],
    )
    back = [by_token[0]] + [swap(by_token[s], "et", s) for s in (1, 2, 3)]
    (handed,) = call(finish_kernel, [like((rows, width))], *back)
    grad_down = contract(act, dz, 0, 0).astype(BF16)
    return (handed[None, None], grad_gate[None], grad_up[None], grad_down[None])


def solution(mesh):
    placed = (
        P("pipe", "dp", "et", None),
        P("pipe", "dp", "et", None),
        P("pipe", "dp", "et", None),
        P("pipe", "dp", "et", None),
        P("pipe", ("dp", "et"), None),
        P("pipe", ("dp", "et"), None),
        P("pipe", ("dp", "et"), None),
    )
    four = mesh.shape["et"] == 4 and mesh.shape["dp"] == 4
    return jax.shard_map(
        on_device_four if four else on_device_any,
        mesh=mesh,
        in_specs=placed,
        out_specs=(
            P("pipe", "dp", "et", None),
            P("pipe", ("dp", "et"), None),
            P("pipe", ("dp", "et"), None),
            P("pipe", ("dp", "et"), None),
        ),
        check_vma=False,
    )
```

```python
import functools

import jax
import jax.numpy as jnp
from jax import lax
from jax.experimental import pallas as pl
from jax.experimental.pallas import tpu as pltpu
from jax.sharding import PartitionSpec as P

FLAG = 128
BF16 = jnp.bfloat16
F32 = jnp.float32
VMEM = pl.BlockSpec(memory_space=pltpu.VMEM)
HBM = pl.BlockSpec(memory_space=pltpu.HBM)


def from_behind(value, axis, steps):
    count = lax.axis_size(axis)
    pairs = [(source, (source + steps) % count) for source in range(count)]
    return lax.ppermute(value, axis, pairs)


def slot_layout(routed, capacity):
    flags = routed.astype(jnp.int32)
    position = jnp.cumsum(flags, axis=-1, dtype=jnp.int32) - 1
    slot_ids = jnp.arange(capacity, dtype=jnp.int32)
    matches = (position[:, None, :] == slot_ids[None, :, None]) & routed[:, None, :]
    token_ids = jnp.arange(routed.shape[-1], dtype=jnp.int32)
    source = jnp.sum(jnp.where(matches, token_ids[None, None, :], 0), axis=-1)
    filled = jnp.any(matches, axis=-1)
    return (source, filled, position)


def gather_slots(rows, source, filled):
    picked = jnp.take_along_axis(rows, source[:, :, None], axis=1)
    return jnp.where(filled[:, :, None], picked, jnp.zeros_like(picked))


def contract(left, right, left_dim, right_dim):
    return lax.dot_general(
        left, right, (((left_dim,), (right_dim,)), ((), ())), preferred_element_type=F32
    )


def on_device_any(tokens, out_grad, top_ids, route_probs, w_gate, w_up, w_down):
    tok_dev = tokens.shape[2]
    model_width = tokens.shape[3]
    et_size = lax.axis_size("et")
    dp_size = lax.axis_size("dp")
    group_tokens = tok_dev * et_size
    capacity = group_tokens // 2
    token_rows = tokens[0, 0]
    chosen = top_ids[0, 0] == 0
    routed_flag = jnp.any(chosen, axis=-1).astype(BF16)
    route_weight = jnp.sum(jnp.where(chosen, route_probs[0, 0], F32(0.0)), axis=-1)
    scaled_rows = (route_weight[:, None] * out_grad[0, 0].astype(F32)).astype(BF16)
    group_x, group_dz, group_flag = (
        lax.all_gather(token_rows, "et", axis=0, tiled=True),
        lax.all_gather(scaled_rows, "et", axis=0, tiled=True),
        lax.all_gather(routed_flag, "et", axis=0, tiled=True),
    )
    routed = group_flag[None, :] > 0
    source, filled, position = slot_layout(routed, capacity)
    own_x = gather_slots(group_x[None], source, filled)
    own_dz = gather_slots(group_dz[None], source, filled)
    all_x, all_dz = (
        lax.all_gather(own_x, "dp", axis=0, tiled=True),
        lax.all_gather(own_dz, "dp", axis=0, tiled=True),
    )
    own_position = position[0]
    own_routed = routed[0]
    slot_x = all_x.reshape(dp_size * capacity, model_width)
    slot_dz = all_dz.reshape(dp_size * capacity, model_width)
    gate_rows = w_gate[0]
    up_rows = w_up[0]
    down_rows = w_down[0]
    gate = contract(slot_x, gate_rows, 1, 1)
    upper = contract(slot_x, up_rows, 1, 1)
    sigmoid_gate = jax.nn.sigmoid(gate)
    silu_gate = gate * sigmoid_gate
    act = (silu_gate * upper).astype(BF16)
    act_grad = contract(slot_dz, down_rows, 1, 1)
    gate_grad = (act_grad * upper * sigmoid_gate * (1.0 + gate * (1.0 - sigmoid_gate))).astype(BF16)
    up_grad = (act_grad * silu_gate).astype(BF16)
    grad_down = contract(act, slot_dz, 0, 0).astype(BF16)
    grad_gate = contract(gate_grad, slot_x, 0, 0).astype(BF16)
    grad_up = contract(up_grad, slot_x, 0, 0).astype(BF16)
    hidden_terms = contract(gate_grad, gate_rows, 1, 0) + contract(up_grad, up_rows, 1, 0)
    rounded = hidden_terms.astype(BF16).reshape(dp_size, capacity, model_width)
    hidden_sum = lax.psum_scatter(rounded, "et", scatter_dimension=1, tiled=True)
    slot_share = lax.psum_scatter(hidden_sum, "dp", scatter_dimension=0, tiled=True)
    slot_grad = lax.all_gather(slot_share, "et", axis=1, tiled=True)[0]
    start = lax.axis_index("et") * tok_dev
    my_position = lax.dynamic_slice_in_dim(own_position, start, tok_dev)
    my_routed = lax.dynamic_slice_in_dim(own_routed, start, tok_dev)
    picked = jnp.take(slot_grad, jnp.maximum(my_position, 0), axis=0)
    input_grad = jnp.where(my_routed[:, None], picked, jnp.zeros_like(picked))
    handed = from_behind(input_grad[None, None], "pipe", -1)
    return (handed, grad_gate[None], grad_up[None], grad_down[None])


def call(kernel, outs, *args, scratch=(), flops=0, vmem=16, space=VMEM, aliases=None):
    moved = 0
    if space is HBM or flops:
        moved = sum(a.size * a.dtype.itemsize for a in args)
        moved += sum(o.size * o.dtype.itemsize for o in outs)
    if space is HBM:
        args = [pltpu.with_memory_space_constraint(a, pltpu.HBM) for a in args]
    return pl.pallas_call(
        kernel,
        out_shape=outs,
        in_specs=[space] * len(args),
        out_specs=[VMEM] * len(outs),
        scratch_shapes=list(scratch),
        input_output_aliases=aliases or {},
        compiler_params=pltpu.CompilerParams(vmem_limit_bytes=vmem * 2**20),
        cost_estimate=pl.CostEstimate(flops=flops, bytes_accessed=moved, transcendentals=0),
    )(*args)


def like(shape, dtype=BF16):
    return jax.ShapeDtypeStruct(shape, dtype)


def spread(steps):
    return [(e, e ^ steps) for e in range(4)]


def bring(sources, targets, sems):
    copies = [
        pltpu.make_async_copy(source, target, sems.at[i])
        for i, (source, target) in enumerate(zip(sources, targets))
    ]
    for copy in copies:
        copy.start()
    return copies


def stage_kernel(*refs):
    weights, outs, sems = refs[:3], refs[3:6], refs[6]
    third = weights[0].shape[0] // 3
    sources, targets = [], []
    for weight, out in zip(weights, outs):
        for part in range(3):
            rows = pl.ds(part * third, third)
            sources.append(weight.at[rows, :])
            targets.append(out.at[rows, :])
    for copy in bring(sources, targets, sems):
        copy.wait()


def pack_kernel(*refs):
    outs, (x_ref, dz_ref, ids_ref, probs_ref, sems) = refs[4:8], refs[8:]
    for copy in bring(refs[:4], refs[8:12], sems):
        copy.wait()
    rows, width = x_ref.shape
    piece = width // 4
    e = lax.axis_index("et")
    chosen = ids_ref[...] == 0
    weight_row = jnp.sum(jnp.where(chosen, probs_ref[...], 0.0), axis=0, keepdims=True)
    flag_row = jnp.max(jnp.where(chosen, 1.0, 0.0), axis=0, keepdims=True)
    on_diagonal = lax.broadcasted_iota(jnp.int32, (rows, rows), 0) == lax.broadcasted_iota(
        jnp.int32, (rows, rows), 1
    )
    weight = jnp.sum(jnp.where(on_diagonal, weight_row, 0.0), axis=1, keepdims=True)
    flag = jnp.sum(jnp.where(on_diagonal, flag_row, 0.0), axis=1, keepdims=True)
    for steps, out in enumerate(outs):
        start = pl.multiple_of((e ^ steps) * piece, 128)
        out[:, :piece] = x_ref[:, pl.ds(start, piece)]
        out[:, piece : 2 * piece] = (weight * dz_ref[:, pl.ds(start, piece)].astype(F32)).astype(BF16)
        out[:, 2 * piece :] = jnp.broadcast_to(flag, (rows, FLAG)).astype(BF16)


def compact_kernel(*refs):
    parts, (slots_ref, pick_ref, all_rows) = refs[:4], refs[4:]
    rows, wide = parts[0].shape
    tokens = 4 * rows
    data = wide - FLAG
    cap = slots_ref.shape[0]
    e = lax.axis_index("et")
    for steps, part in enumerate(parts):
        all_rows[pl.ds(pl.multiple_of((e ^ steps) * rows, 16), rows), :] = part[...]
    flags = all_rows[:, data:]
    before = lax.broadcasted_iota(jnp.int32, (tokens, tokens), 0)
    after = lax.broadcasted_iota(jnp.int32, (tokens, tokens), 1)
    count = contract(flags, (before <= after).astype(F32).astype(BF16), 0, 0)[:cap]
    here = contract(flags, (before == after).astype(F32).astype(BF16), 0, 0)[:cap]
    slot = lax.broadcasted_iota(jnp.int32, (cap, tokens), 0).astype(F32)
    pick = jnp.where((count - 1.0 == slot) & (here > 0.5), 1.0, 0.0).astype(BF16)
    slots_ref[...] = jnp.dot(pick, all_rows[:, :data], preferred_element_type=F32).astype(BF16)
    pick_ref[...] = jnp.zeros_like(pick_ref)
    pick_ref[:, :tokens] = pick


def add_quarter(steps, blocks, x_ref, dz_ref, weights):
    piece = blocks[0].shape[1] // 2
    columns = pl.ds(pl.multiple_of((lax.axis_index("et") ^ steps) * piece, 128), piece)
    start = 0
    for block in blocks:
        rows = pl.ds(start, block.shape[0])
        x_ref[rows, columns] = block[:, :piece]
        dz_ref[rows, columns] = block[:, piece:]
        start += block.shape[0]
    wg_ref, wu_ref, wd_ref = weights
    x, dz = x_ref[:, columns], dz_ref[:, columns]
    return (
        contract(x, wg_ref[:, columns], 1, 1),
        contract(x, wu_ref[:, columns], 1, 1),
        contract(dz, wd_ref[:, columns], 1, 1),
    )


def first_kernel(*refs):
    weights, (x_ref, dz_ref, *sums) = refs[12:15], refs[15:]
    for steps in range(3):
        parts = add_quarter(steps, refs[4 * steps : 4 * steps + 4], x_ref, dz_ref, weights)
        for out, part in zip(sums, parts):
            out[...] = out[...] + part if steps else part


def half_terms(other, gate_grad, up_grad, weights, half):
    side = lax.axis_index("et") % 2 ^ other
    columns = pl.ds(pl.multiple_of(side * half, 128), half)
    terms = contract(gate_grad, weights[0][:, columns], 1, 0)
    return terms + contract(up_grad, weights[1][:, columns], 1, 0)


def third_kernel(*refs):
    both, weights, olds, outs = refs[:4], refs[4:7], refs[9:12], refs[12:]
    x_ref, dz_ref, act_ref, gg_ref, ug_ref, grads_ref, away_ref = outs
    slots = x_ref.shape[0]
    parts = add_quarter(3, both, x_ref, dz_ref, weights)
    gate, upper, act_grad = (old[...] + part for old, part in zip(olds, parts))
    sigmoid_gate = jax.nn.sigmoid(gate)
    silu_gate = gate * sigmoid_gate
    gate_grad = (act_grad * upper * sigmoid_gate * (1.0 + gate * (1.0 - sigmoid_gate))).astype(BF16)
    up_grad = (act_grad * silu_gate).astype(BF16)
    gg_ref[...] = gate_grad
    ug_ref[...] = up_grad
    act_ref[...] = (silu_gate * upper).astype(BF16)
    grads_ref[:slots, :] = gate_grad
    grads_ref[slots:, :] = up_grad
    away_ref[...] = half_terms(1, gate_grad, up_grad, weights, away_ref.shape[1]).astype(BF16)


def own_terms_kernel(grads_ref, wg_ref, wu_ref, out_ref):
    slots, half = out_ref.shape
    grads = grads_ref[:slots, :], grads_ref[slots:, :]
    out_ref[...] = half_terms(0, *grads, (wg_ref, wu_ref), half)


def pair_kernel(own_ref, other_ref, pick_ref, *outs):
    cap, half = outs[0].shape
    for k, out in enumerate(outs):
        rows = pl.ds(k * cap, cap)
        out[:, :half] = (own_ref[rows, :] + other_ref[rows, :].astype(F32)).astype(BF16)
    outs[3][:, half:] = pick_ref[...]


def add_kernel(left_ref, right_ref, out_ref, ready_ref):
    out_ref[...] = (left_ref[...].astype(F32) + right_ref[...].astype(F32)).astype(BF16)
    ready_ref[...] = jnp.zeros_like(ready_ref)


def expand_kernel(own_ref, ready_ref, *refs):
    others, outs, tokens_ref = refs[:2], refs[2:6], refs[6]
    rows, half = outs[0].shape
    e = lax.axis_index("et")
    total = own_ref[:, :half].astype(F32)
    for other in others:
        total += other[...].astype(F32)
    tokens_ref[...] = contract(own_ref[:, half:], total.astype(BF16), 0, 0).astype(BF16)
    for steps, out in enumerate(outs):
        out[...] = tokens_ref[pl.ds(pl.multiple_of((e ^ steps) * rows, 16), rows), :]


def finish_kernel(own_ref, core_ref, chip_ref, both_ref, out_ref):
    half = own_ref.shape[1]
    core = lax.axis_index("et") % 2
    mine = own_ref[...].astype(F32) + chip_ref[...].astype(F32)
    out_ref[:, pl.ds(pl.multiple_of(core * half, 128), half)] = mine.astype(BF16)
    theirs = core_ref[...].astype(F32) + both_ref[...].astype(F32)
    out_ref[:, pl.ds(pl.multiple_of((1 - core) * half, 128), half)] = theirs.astype(BF16)


def swap(value, axis, steps):
    return lax.ppermute(value, axis, spread(steps))


def hand(value, pipe_size, steps):
    pairs = [
        (4 * p + z, 4 * ((p - 1) % pipe_size) + (z ^ steps)) for p in range(pipe_size) for z in range(4)
    ]
    return lax.ppermute(value, ("pipe", "dp"), pairs)


def on_device_four(tokens, out_grad, top_ids, route_probs, w_gate, w_up, w_down):
    rows, width = tokens.shape[2:]
    hidden = w_gate.shape[1]
    top = top_ids.shape[3]
    pipe_size = lax.axis_size("pipe")
    cap = 2 * rows
    slots = 4 * cap
    piece, half = width // 4, width // 2

    packed = call(
        pack_kernel,
        [like((rows, 2 * piece + FLAG))] * 4,
        tokens[0, 0],
        out_grad[0, 0],
        top_ids[0, 0].T,
        route_probs[0, 0].T,
        scratch=[
            pltpu.VMEM((rows, width), BF16),
            pltpu.VMEM((rows, width), BF16),
            pltpu.VMEM((top, rows), jnp.int32),
            pltpu.VMEM((top, rows), F32),
            pltpu.SemaphoreType.DMA((4,)),
        ],
        space=HBM,
    )
    arrived = [packed[0]] + [swap(packed[s], "et", s) for s in (1, 2, 3)]
    weights = call(
        stage_kernel,
        [like((hidden, width))] * 3,
        w_gate[0],
        w_up[0],
        w_down[0],
        scratch=[pltpu.SemaphoreType.DMA((9,))],
        space=HBM,
    )
    arrived, weights = lax.optimization_barrier((arrived, weights))
    slot_block, pick = call(
        compact_kernel,
        [like((cap, 2 * piece)), like((cap, FLAG))],
        *arrived,
        scratch=[pltpu.VMEM((4 * rows, 2 * piece + FLAG), BF16)],
    )
    diag = swap(slot_block, "dp", 3)
    near = swap(slot_block, "dp", 1)
    far = swap(slot_block, "dp", 2)
    own = [diag, far, near, slot_block]
    chip = [swap(block, "et", 2) for block in own]
    core = [swap(block, "et", 1) for block in own]
    both = [swap(block, "et", 1) for block in chip]
    wide, sums = [like((slots, width))] * 2, [like((slots, hidden), F32)] * 3
    state = call(first_kernel, wide + sums, *own, *core, *chip, *weights, vmem=32)
    x, dz, act, gate_grad, up_grad, grads, away = call(
        third_kernel,
        wide + [like((slots, hidden))] * 3 + [like((2 * slots, hidden)), like((slots, half))],
        *both,
        *weights,
        *state,
        vmem=32,
        aliases={7: 0, 8: 1},
    )
    theirs = swap(away, "et", 1)
    (own_terms,) = call(
        own_terms_kernel,
        [like((slots, half), F32)],
        grads,
        *weights[:2],
        flops=4 * slots * hidden * half,
        vmem=32,
    )
    to_last, to_far, to_near, home = call(
        pair_kernel,
        [like((cap, half))] * 3 + [like((cap, half + FLAG))],
        own_terms,
        theirs,
        pick,
    )
    from_last = swap(to_last, "dp", 1)
    home = hand(home, pipe_size, 0)
    from_near = hand(to_near, pipe_size, 1)
    to_far, ready = call(
        add_kernel, [like((cap, half)), like((8, 128), F32)], to_far, from_last
    )
    x, dz, act, gate_grad, up_grad, ready = lax.optimization_barrier(
        (x, dz, act, gate_grad, up_grad, ready)
    )
    grad_gate = contract(gate_grad, x, 0, 0).astype(BF16)
    grad_up = contract(up_grad, x, 0, 0).astype(BF16)
    from_far = hand(to_far, pipe_size, 2)
    from_far, grad_gate, grad_up = lax.optimization_barrier((from_far, grad_gate, grad_up))
    by_token = call(
        expand_kernel,
        [like((rows, half))] * 4,
        home,
        ready,
        from_far,
        from_near,
        scratch=[pltpu.VMEM((FLAG, half), BF16)],
    )
    back = [by_token[0]] + [swap(by_token[s], "et", s) for s in (1, 2, 3)]
    (handed,) = call(finish_kernel, [like((rows, width))], *back)
    grad_down = contract(act, dz, 0, 0).astype(BF16)
    return (handed[None, None], grad_gate[None], grad_up[None], grad_down[None])


def solution(mesh):
    placed = (
        P("pipe", "dp", "et", None),
        P("pipe", "dp", "et", None),
        P("pipe", "dp", "et", None),
        P("pipe", "dp", "et", None),
        P("pipe", ("dp", "et"), None),
        P("pipe", ("dp", "et"), None),
        P("pipe", ("dp", "et"), None),
    )
    four = mesh.shape["et"] == 4 and mesh.shape["dp"] == 4
    return jax.shard_map(
        on_device_four if four else on_device_any,
        mesh=mesh,
        in_specs=placed,
        out_specs=(
            P("pipe", "dp", "et", None),
            P("pipe", ("dp", "et"), None),
            P("pipe", ("dp", "et"), None),
            P("pipe", ("dp", "et"), None),
        ),
        check_vma=False,
    )
```

```python
import functools

import jax
import jax.numpy as jnp
from jax import lax
from jax.experimental import pallas as pl
from jax.experimental.pallas import tpu as pltpu
from jax.sharding import PartitionSpec as P

FLAG = 128
BF16 = jnp.bfloat16
F32 = jnp.float32
VMEM = pl.BlockSpec(memory_space=pltpu.VMEM)
HBM = pl.BlockSpec(memory_space=pltpu.HBM)


def from_behind(value, axis, steps):
    count = lax.axis_size(axis)
    pairs = [(source, (source + steps) % count) for source in range(count)]
    return lax.ppermute(value, axis, pairs)


def slot_layout(routed, capacity):
    flags = routed.astype(jnp.int32)
    position = jnp.cumsum(flags, axis=-1, dtype=jnp.int32) - 1
    slot_ids = jnp.arange(capacity, dtype=jnp.int32)
    matches = (position[:, None, :] == slot_ids[None, :, None]) & routed[:, None, :]
    token_ids = jnp.arange(routed.shape[-1], dtype=jnp.int32)
    source = jnp.sum(jnp.where(matches, token_ids[None, None, :], 0), axis=-1)
    filled = jnp.any(matches, axis=-1)
    return (source, filled, position)


def gather_slots(rows, source, filled):
    picked = jnp.take_along_axis(rows, source[:, :, None], axis=1)
    return jnp.where(filled[:, :, None], picked, jnp.zeros_like(picked))


def contract(left, right, left_dim, right_dim):
    return lax.dot_general(
        left, right, (((left_dim,), (right_dim,)), ((), ())), preferred_element_type=F32
    )


def on_device_any(tokens, out_grad, top_ids, route_probs, w_gate, w_up, w_down):
    tok_dev = tokens.shape[2]
    model_width = tokens.shape[3]
    et_size = lax.axis_size("et")
    dp_size = lax.axis_size("dp")
    group_tokens = tok_dev * et_size
    capacity = group_tokens // 2
    token_rows = tokens[0, 0]
    chosen = top_ids[0, 0] == 0
    routed_flag = jnp.any(chosen, axis=-1).astype(BF16)
    route_weight = jnp.sum(jnp.where(chosen, route_probs[0, 0], F32(0.0)), axis=-1)
    scaled_rows = (route_weight[:, None] * out_grad[0, 0].astype(F32)).astype(BF16)
    group_x, group_dz, group_flag = (
        lax.all_gather(token_rows, "et", axis=0, tiled=True),
        lax.all_gather(scaled_rows, "et", axis=0, tiled=True),
        lax.all_gather(routed_flag, "et", axis=0, tiled=True),
    )
    routed = group_flag[None, :] > 0
    source, filled, position = slot_layout(routed, capacity)
    own_x = gather_slots(group_x[None], source, filled)
    own_dz = gather_slots(group_dz[None], source, filled)
    all_x, all_dz = (
        lax.all_gather(own_x, "dp", axis=0, tiled=True),
        lax.all_gather(own_dz, "dp", axis=0, tiled=True),
    )
    own_position = position[0]
    own_routed = routed[0]
    slot_x = all_x.reshape(dp_size * capacity, model_width)
    slot_dz = all_dz.reshape(dp_size * capacity, model_width)
    gate_rows = w_gate[0]
    up_rows = w_up[0]
    down_rows = w_down[0]
    gate = contract(slot_x, gate_rows, 1, 1)
    upper = contract(slot_x, up_rows, 1, 1)
    sigmoid_gate = jax.nn.sigmoid(gate)
    silu_gate = gate * sigmoid_gate
    act = (silu_gate * upper).astype(BF16)
    act_grad = contract(slot_dz, down_rows, 1, 1)
    gate_grad = (act_grad * upper * sigmoid_gate * (1.0 + gate * (1.0 - sigmoid_gate))).astype(BF16)
    up_grad = (act_grad * silu_gate).astype(BF16)
    grad_down = contract(act, slot_dz, 0, 0).astype(BF16)
    grad_gate = contract(gate_grad, slot_x, 0, 0).astype(BF16)
    grad_up = contract(up_grad, slot_x, 0, 0).astype(BF16)
    hidden_terms = contract(gate_grad, gate_rows, 1, 0) + contract(up_grad, up_rows, 1, 0)
    rounded = hidden_terms.astype(BF16).reshape(dp_size, capacity, model_width)
    hidden_sum = lax.psum_scatter(rounded, "et", scatter_dimension=1, tiled=True)
    slot_share = lax.psum_scatter(hidden_sum, "dp", scatter_dimension=0, tiled=True)
    slot_grad = lax.all_gather(slot_share, "et", axis=1, tiled=True)[0]
    start = lax.axis_index("et") * tok_dev
    my_position = lax.dynamic_slice_in_dim(own_position, start, tok_dev)
    my_routed = lax.dynamic_slice_in_dim(own_routed, start, tok_dev)
    picked = jnp.take(slot_grad, jnp.maximum(my_position, 0), axis=0)
    input_grad = jnp.where(my_routed[:, None], picked, jnp.zeros_like(picked))
    handed = from_behind(input_grad[None, None], "pipe", -1)
    return (handed, grad_gate[None], grad_up[None], grad_down[None])


def call(kernel, outs, *args, scratch=(), flops=0, vmem=16, space=VMEM, aliases=None):
    moved = 0
    if space is HBM or flops:
        moved = sum(a.size * a.dtype.itemsize for a in args)
        moved += sum(o.size * o.dtype.itemsize for o in outs)
    if space is HBM:
        args = [pltpu.with_memory_space_constraint(a, pltpu.HBM) for a in args]
    return pl.pallas_call(
        kernel,
        out_shape=outs,
        in_specs=[space] * len(args),
        out_specs=[VMEM] * len(outs),
        scratch_shapes=list(scratch),
        input_output_aliases=aliases or {},
        compiler_params=pltpu.CompilerParams(vmem_limit_bytes=vmem * 2**20),
        cost_estimate=pl.CostEstimate(flops=flops, bytes_accessed=moved, transcendentals=0),
    )(*args)


def like(shape, dtype=BF16):
    return jax.ShapeDtypeStruct(shape, dtype)


def spread(steps):
    return [(e, e ^ steps) for e in range(4)]


def bring(sources, targets, sems):
    copies = [
        pltpu.make_async_copy(source, target, sems.at[i])
        for i, (source, target) in enumerate(zip(sources, targets))
    ]
    for copy in copies:
        copy.start()
    return copies


def stage_kernel(*refs):
    weights, outs, sems = refs[:3], refs[3:6], refs[6]
    third = weights[0].shape[0] // 3
    sources, targets = [], []
    for weight, out in zip(weights, outs):
        for part in range(3):
            rows = pl.ds(part * third, third)
            sources.append(weight.at[rows, :])
            targets.append(out.at[rows, :])
    for copy in bring(sources, targets, sems):
        copy.wait()


def pack_kernel(*refs):
    outs, (x_ref, dz_ref, ids_ref, probs_ref, sems) = refs[4:8], refs[8:]
    for copy in bring(refs[:4], refs[8:12], sems):
        copy.wait()
    rows, width = x_ref.shape
    piece = width // 4
    e = lax.axis_index("et")
    chosen = ids_ref[...] == 0
    weight_row = jnp.sum(jnp.where(chosen, probs_ref[...], 0.0), axis=0, keepdims=True)
    flag_row = jnp.max(jnp.where(chosen, 1.0, 0.0), axis=0, keepdims=True)
    on_diagonal = lax.broadcasted_iota(jnp.int32, (rows, rows), 0) == lax.broadcasted_iota(
        jnp.int32, (rows, rows), 1
    )
    weight = jnp.sum(jnp.where(on_diagonal, weight_row, 0.0), axis=1, keepdims=True)
    flag = jnp.sum(jnp.where(on_diagonal, flag_row, 0.0), axis=1, keepdims=True)
    for steps, out in enumerate(outs):
        start = pl.multiple_of((e ^ steps) * piece, 128)
        out[:, :piece] = x_ref[:, pl.ds(start, piece)]
        out[:, piece : 2 * piece] = (weight * dz_ref[:, pl.ds(start, piece)].astype(F32)).astype(BF16)
        out[:, 2 * piece :] = jnp.broadcast_to(flag, (rows, FLAG)).astype(BF16)


def compact_kernel(*refs):
    parts, (slots_ref, pick_ref, all_rows) = refs[:4], refs[4:]
    rows, wide = parts[0].shape
    tokens = 4 * rows
    data = wide - FLAG
    cap = slots_ref.shape[0]
    e = lax.axis_index("et")
    for steps, part in enumerate(parts):
        all_rows[pl.ds(pl.multiple_of((e ^ steps) * rows, 16), rows), :] = part[...]
    flags = all_rows[:, data:]
    before = lax.broadcasted_iota(jnp.int32, (tokens, tokens), 0)
    after = lax.broadcasted_iota(jnp.int32, (tokens, tokens), 1)
    count = contract(flags, (before <= after).astype(F32).astype(BF16), 0, 0)[:cap]
    here = contract(flags, (before == after).astype(F32).astype(BF16), 0, 0)[:cap]
    slot = lax.broadcasted_iota(jnp.int32, (cap, tokens), 0).astype(F32)
    pick = jnp.where((count - 1.0 == slot) & (here > 0.5), 1.0, 0.0).astype(BF16)
    slots_ref[...] = jnp.dot(pick, all_rows[:, :data], preferred_element_type=F32).astype(BF16)
    pick_ref[...] = jnp.zeros_like(pick_ref)
    pick_ref[:, :tokens] = pick


def add_quarter(steps, blocks, x_ref, dz_ref, weights):
    piece = blocks[0].shape[1] // 2
    columns = pl.ds(pl.multiple_of((lax.axis_index("et") ^ steps) * piece, 128), piece)
    start = 0
    for block in blocks:
        rows = pl.ds(start, block.shape[0])
        x_ref[rows, columns] = block[:, :piece]
        dz_ref[rows, columns] = block[:, piece:]
        start += block.shape[0]
    wg_ref, wu_ref, wd_ref = weights
    x, dz = x_ref[:, columns], dz_ref[:, columns]
    return (
        contract(x, wg_ref[:, columns], 1, 1),
        contract(x, wu_ref[:, columns], 1, 1),
        contract(dz, wd_ref[:, columns], 1, 1),
    )


def first_kernel(*refs):
    weights, (x_ref, dz_ref, *sums) = refs[12:15], refs[15:]
    for steps in range(3):
        parts = add_quarter(steps, refs[4 * steps : 4 * steps + 4], x_ref, dz_ref, weights)
        for out, part in zip(sums, parts):
            out[...] = out[...] + part if steps else part


def half_terms(other, gate_grad, up_grad, weights, half):
    side = lax.axis_index("et") % 2 ^ other
    columns = pl.ds(pl.multiple_of(side * half, 128), half)
    terms = contract(gate_grad, weights[0][:, columns], 1, 0)
    return terms + contract(up_grad, weights[1][:, columns], 1, 0)


def third_kernel(*refs):
    both, weights, olds, outs = refs[:4], refs[4:7], refs[9:12], refs[12:]
    x_ref, dz_ref, act_ref, gg_ref, ug_ref, grads_ref, away_ref = outs
    slots = x_ref.shape[0]
    parts = add_quarter(3, both, x_ref, dz_ref, weights)
    gate, upper, act_grad = (old[...] + part for old, part in zip(olds, parts))
    sigmoid_gate = jax.nn.sigmoid(gate)
    silu_gate = gate * sigmoid_gate
    gate_grad = (act_grad * upper * sigmoid_gate * (1.0 + gate * (1.0 - sigmoid_gate))).astype(BF16)
    up_grad = (act_grad * silu_gate).astype(BF16)
    gg_ref[...] = gate_grad
    ug_ref[...] = up_grad
    act_ref[...] = (silu_gate * upper).astype(BF16)
    grads_ref[:slots, :] = gate_grad
    grads_ref[slots:, :] = up_grad
    away_ref[...] = half_terms(1, gate_grad, up_grad, weights, away_ref.shape[1]).astype(BF16)


def own_terms_kernel(grads_ref, wg_ref, wu_ref, out_ref):
    slots, half = out_ref.shape
    grads = grads_ref[:slots, :], grads_ref[slots:, :]
    out_ref[...] = half_terms(0, *grads, (wg_ref, wu_ref), half)


def pair_kernel(own_ref, other_ref, pick_ref, *outs):
    cap, half = outs[0].shape
    for k, out in enumerate(outs):
        rows = pl.ds(k * cap, cap)
        out[:, :half] = (own_ref[rows, :] + other_ref[rows, :].astype(F32)).astype(BF16)
    outs[3][:, half:] = pick_ref[...]


def add_kernel(left_ref, right_ref, out_ref, ready_ref):
    out_ref[...] = (left_ref[...].astype(F32) + right_ref[...].astype(F32)).astype(BF16)
    ready_ref[...] = jnp.zeros_like(ready_ref)


def expand_kernel(own_ref, ready_ref, *refs):
    others, outs, tokens_ref = refs[:2], refs[2:6], refs[6]
    rows, half = outs[0].shape
    e = lax.axis_index("et")
    total = own_ref[:, :half].astype(F32)
    for other in others:
        total += other[...].astype(F32)
    tokens_ref[...] = contract(own_ref[:, half:], total.astype(BF16), 0, 0).astype(BF16)
    for steps, out in enumerate(outs):
        out[...] = tokens_ref[pl.ds(pl.multiple_of((e ^ steps) * rows, 16), rows), :]


def finish_kernel(own_ref, core_ref, chip_ref, both_ref, out_ref):
    half = own_ref.shape[1]
    core = lax.axis_index("et") % 2
    mine = own_ref[...].astype(F32) + chip_ref[...].astype(F32)
    out_ref[:, pl.ds(pl.multiple_of(core * half, 128), half)] = mine.astype(BF16)
    theirs = core_ref[...].astype(F32) + both_ref[...].astype(F32)
    out_ref[:, pl.ds(pl.multiple_of((1 - core) * half, 128), half)] = theirs.astype(BF16)


def swap(value, axis, steps):
    return lax.ppermute(value, axis, spread(steps))


def hand(value, pipe_size, steps):
    pairs = [
        (4 * p + z, 4 * ((p - 1) % pipe_size) + (z ^ steps)) for p in range(pipe_size) for z in range(4)
    ]
    return lax.ppermute(value, ("pipe", "dp"), pairs)


def on_device_four(tokens, out_grad, top_ids, route_probs, w_gate, w_up, w_down):
    rows, width = tokens.shape[2:]
    hidden = w_gate.shape[1]
    top = top_ids.shape[3]
    pipe_size = lax.axis_size("pipe")
    cap = 2 * rows
    slots = 4 * cap
    piece, half = width // 4, width // 2

    packed = call(
        pack_kernel,
        [like((rows, 2 * piece + FLAG))] * 4,
        tokens[0, 0],
        out_grad[0, 0],
        top_ids[0, 0].T,
        route_probs[0, 0].T,
        scratch=[
            pltpu.VMEM((rows, width), BF16),
            pltpu.VMEM((rows, width), BF16),
            pltpu.VMEM((top, rows), jnp.int32),
            pltpu.VMEM((top, rows), F32),
            pltpu.SemaphoreType.DMA((4,)),
        ],
        space=HBM,
    )
    arrived = [packed[0]] + [swap(packed[s], "et", s) for s in (1, 2, 3)]
    weights = call(
        stage_kernel,
        [like((hidden, width))] * 3,
        w_gate[0],
        w_up[0],
        w_down[0],
        scratch=[pltpu.SemaphoreType.DMA((9,))],
        space=HBM,
    )
    arrived, weights = lax.optimization_barrier((arrived, weights))
    slot_block, pick = call(
        compact_kernel,
        [like((cap, 2 * piece)), like((cap, FLAG))],
        *arrived,
        scratch=[pltpu.VMEM((4 * rows, 2 * piece + FLAG), BF16)],
    )
    near = swap(slot_block, "dp", 1)
    far = swap(slot_block, "dp", 2)
    last = swap(far, "dp", 1)
    own = [near, last, far, slot_block]
    chip = [swap(block, "et", 2) for block in own]
    core = [swap(block, "et", 1) for block in own]
    both = [swap(block, "et", 1) for block in chip]
    wide, sums = [like((slots, width))] * 2, [like((slots, hidden), F32)] * 3
    state = call(first_kernel, wide + sums, *own, *core, *chip, *weights, vmem=32)
    x, dz, act, gate_grad, up_grad, grads, away = call(
        third_kernel,
        wide + [like((slots, hidden))] * 3 + [like((2 * slots, hidden)), like((slots, half))],
        *both,
        *weights,
        *state,
        vmem=32,
        aliases={7: 0, 8: 1},
    )
    theirs = swap(away, "et", 1)
    (own_terms,) = call(
        own_terms_kernel,
        [like((slots, half), F32)],
        grads,
        *weights[:2],
        flops=4 * slots * hidden * half,
        vmem=32,
    )
    to_near, to_last, to_far, home = call(
        pair_kernel,
        [like((cap, half))] * 3 + [like((cap, half + FLAG))],
        own_terms,
        theirs,
        pick,
    )
    from_last = swap(to_last, "dp", 1)
    home = hand(home, pipe_size, 0)
    from_near = hand(to_near, pipe_size, 1)
    to_far, ready = call(
        add_kernel, [like((cap, half)), like((8, 128), F32)], to_far, from_last
    )
    x, dz, act, gate_grad, up_grad, ready = lax.optimization_barrier(
        (x, dz, act, gate_grad, up_grad, ready)
    )
    grad_gate = contract(gate_grad, x, 0, 0).astype(BF16)
    grad_up = contract(up_grad, x, 0, 0).astype(BF16)
    from_far = hand(to_far, pipe_size, 2)
    from_far, grad_gate, grad_up = lax.optimization_barrier((from_far, grad_gate, grad_up))
    by_token = call(
        expand_kernel,
        [like((rows, half))] * 4,
        home,
        ready,
        from_far,
        from_near,
        scratch=[pltpu.VMEM((FLAG, half), BF16)],
    )
    back = [by_token[0]] + [swap(by_token[s], "et", s) for s in (1, 2, 3)]
    (handed,) = call(finish_kernel, [like((rows, width))], *back)
    grad_down = contract(act, dz, 0, 0).astype(BF16)
    return (handed[None, None], grad_gate[None], grad_up[None], grad_down[None])


def solution(mesh):
    placed = (
        P("pipe", "dp", "et", None),
        P("pipe", "dp", "et", None),
        P("pipe", "dp", "et", None),
        P("pipe", "dp", "et", None),
        P("pipe", ("dp", "et"), None),
        P("pipe", ("dp", "et"), None),
        P("pipe", ("dp", "et"), None),
    )
    four = mesh.shape["et"] == 4 and mesh.shape["dp"] == 4
    return jax.shard_map(
        on_device_four if four else on_device_any,
        mesh=mesh,
        in_specs=placed,
        out_specs=(
            P("pipe", "dp", "et", None),
            P("pipe", ("dp", "et"), None),
            P("pipe", ("dp", "et"), None),
            P("pipe", ("dp", "et"), None),
        ),
        check_vma=False,
    )
```

```python
import functools

import jax
import jax.numpy as jnp
from jax import lax
from jax.experimental import pallas as pl
from jax.experimental.pallas import tpu as pltpu
from jax.sharding import PartitionSpec as P

FLAG = 128
BF16 = jnp.bfloat16
F32 = jnp.float32
VMEM = pl.BlockSpec(memory_space=pltpu.VMEM)
HBM = pl.BlockSpec(memory_space=pltpu.HBM)


def from_behind(value, axis, steps):
    count = lax.axis_size(axis)
    pairs = [(source, (source + steps) % count) for source in range(count)]
    return lax.ppermute(value, axis, pairs)


def slot_layout(routed, capacity):
    flags = routed.astype(jnp.int32)
    position = jnp.cumsum(flags, axis=-1, dtype=jnp.int32) - 1
    slot_ids = jnp.arange(capacity, dtype=jnp.int32)
    matches = (position[:, None, :] == slot_ids[None, :, None]) & routed[:, None, :]
    token_ids = jnp.arange(routed.shape[-1], dtype=jnp.int32)
    source = jnp.sum(jnp.where(matches, token_ids[None, None, :], 0), axis=-1)
    filled = jnp.any(matches, axis=-1)
    return (source, filled, position)


def gather_slots(rows, source, filled):
    picked = jnp.take_along_axis(rows, source[:, :, None], axis=1)
    return jnp.where(filled[:, :, None], picked, jnp.zeros_like(picked))


def contract(left, right, left_dim, right_dim):
    return lax.dot_general(
        left, right, (((left_dim,), (right_dim,)), ((), ())), preferred_element_type=F32
    )


def on_device_any(tokens, out_grad, top_ids, route_probs, w_gate, w_up, w_down):
    tok_dev = tokens.shape[2]
    model_width = tokens.shape[3]
    et_size = lax.axis_size("et")
    dp_size = lax.axis_size("dp")
    group_tokens = tok_dev * et_size
    capacity = group_tokens // 2
    token_rows = tokens[0, 0]
    chosen = top_ids[0, 0] == 0
    routed_flag = jnp.any(chosen, axis=-1).astype(BF16)
    route_weight = jnp.sum(jnp.where(chosen, route_probs[0, 0], F32(0.0)), axis=-1)
    scaled_rows = (route_weight[:, None] * out_grad[0, 0].astype(F32)).astype(BF16)
    group_x, group_dz, group_flag = (
        lax.all_gather(token_rows, "et", axis=0, tiled=True),
        lax.all_gather(scaled_rows, "et", axis=0, tiled=True),
        lax.all_gather(routed_flag, "et", axis=0, tiled=True),
    )
    routed = group_flag[None, :] > 0
    source, filled, position = slot_layout(routed, capacity)
    own_x = gather_slots(group_x[None], source, filled)
    own_dz = gather_slots(group_dz[None], source, filled)
    all_x, all_dz = (
        lax.all_gather(own_x, "dp", axis=0, tiled=True),
        lax.all_gather(own_dz, "dp", axis=0, tiled=True),
    )
    own_position = position[0]
    own_routed = routed[0]
    slot_x = all_x.reshape(dp_size * capacity, model_width)
    slot_dz = all_dz.reshape(dp_size * capacity, model_width)
    gate_rows = w_gate[0]
    up_rows = w_up[0]
    down_rows = w_down[0]
    gate = contract(slot_x, gate_rows, 1, 1)
    upper = contract(slot_x, up_rows, 1, 1)
    sigmoid_gate = jax.nn.sigmoid(gate)
    silu_gate = gate * sigmoid_gate
    act = (silu_gate * upper).astype(BF16)
    act_grad = contract(slot_dz, down_rows, 1, 1)
    gate_grad = (act_grad * upper * sigmoid_gate * (1.0 + gate * (1.0 - sigmoid_gate))).astype(BF16)
    up_grad = (act_grad * silu_gate).astype(BF16)
    grad_down = contract(act, slot_dz, 0, 0).astype(BF16)
    grad_gate = contract(gate_grad, slot_x, 0, 0).astype(BF16)
    grad_up = contract(up_grad, slot_x, 0, 0).astype(BF16)
    hidden_terms = contract(gate_grad, gate_rows, 1, 0) + contract(up_grad, up_rows, 1, 0)
    rounded = hidden_terms.astype(BF16).reshape(dp_size, capacity, model_width)
    hidden_sum = lax.psum_scatter(rounded, "et", scatter_dimension=1, tiled=True)
    slot_share = lax.psum_scatter(hidden_sum, "dp", scatter_dimension=0, tiled=True)
    slot_grad = lax.all_gather(slot_share, "et", axis=1, tiled=True)[0]
    start = lax.axis_index("et") * tok_dev
    my_position = lax.dynamic_slice_in_dim(own_position, start, tok_dev)
    my_routed = lax.dynamic_slice_in_dim(own_routed, start, tok_dev)
    picked = jnp.take(slot_grad, jnp.maximum(my_position, 0), axis=0)
    input_grad = jnp.where(my_routed[:, None], picked, jnp.zeros_like(picked))
    handed = from_behind(input_grad[None, None], "pipe", -1)
    return (handed, grad_gate[None], grad_up[None], grad_down[None])


def call(kernel, outs, *args, scratch=(), flops=0, vmem=16, space=VMEM, aliases=None):
    moved = 0
    if space is HBM or flops:
        moved = sum(a.size * a.dtype.itemsize for a in args)
        moved += sum(o.size * o.dtype.itemsize for o in outs)
    if space is HBM:
        args = [pltpu.with_memory_space_constraint(a, pltpu.HBM) for a in args]
    return pl.pallas_call(
        kernel,
        out_shape=outs,
        in_specs=[space] * len(args),
        out_specs=[VMEM] * len(outs),
        scratch_shapes=list(scratch),
        input_output_aliases=aliases or {},
        compiler_params=pltpu.CompilerParams(vmem_limit_bytes=vmem * 2**20),
        cost_estimate=pl.CostEstimate(flops=flops, bytes_accessed=moved, transcendentals=0),
    )(*args)


def like(shape, dtype=BF16):
    return jax.ShapeDtypeStruct(shape, dtype)


def spread(steps):
    return [(e, e ^ steps) for e in range(4)]


def bring(sources, targets, sems):
    copies = [
        pltpu.make_async_copy(source, target, sems.at[i])
        for i, (source, target) in enumerate(zip(sources, targets))
    ]
    for copy in copies:
        copy.start()
    return copies


def stage_kernel(*refs):
    weights, outs, sems = refs[:3], refs[3:6], refs[6]
    third = weights[0].shape[0] // 3
    sources, targets = [], []
    for weight, out in zip(weights, outs):
        for part in range(3):
            rows = pl.ds(part * third, third)
            sources.append(weight.at[rows, :])
            targets.append(out.at[rows, :])
    for copy in bring(sources, targets, sems):
        copy.wait()


def pack_kernel(*refs):
    outs, (x_ref, dz_ref, ids_ref, probs_ref, sems) = refs[4:8], refs[8:]
    for copy in bring(refs[:4], refs[8:12], sems):
        copy.wait()
    rows, width = x_ref.shape
    piece = width // 4
    e = lax.axis_index("et")
    chosen = ids_ref[...] == 0
    weight_row = jnp.sum(jnp.where(chosen, probs_ref[...], 0.0), axis=0, keepdims=True)
    flag_row = jnp.max(jnp.where(chosen, 1.0, 0.0), axis=0, keepdims=True)
    on_diagonal = lax.broadcasted_iota(jnp.int32, (rows, rows), 0) == lax.broadcasted_iota(
        jnp.int32, (rows, rows), 1
    )
    weight = jnp.sum(jnp.where(on_diagonal, weight_row, 0.0), axis=1, keepdims=True)
    flag = jnp.sum(jnp.where(on_diagonal, flag_row, 0.0), axis=1, keepdims=True)
    for steps, out in enumerate(outs):
        start = pl.multiple_of((e ^ steps) * piece, 128)
        out[:, :piece] = x_ref[:, pl.ds(start, piece)]
        out[:, piece : 2 * piece] = (weight * dz_ref[:, pl.ds(start, piece)].astype(F32)).astype(BF16)
        out[:, 2 * piece :] = jnp.broadcast_to(flag, (rows, FLAG)).astype(BF16)


def compact_kernel(*refs):
    parts, (slots_ref, pick_ref, all_rows) = refs[:4], refs[4:]
    rows, wide = parts[0].shape
    tokens = 4 * rows
    data = wide - FLAG
    cap = slots_ref.shape[0]
    e = lax.axis_index("et")
    for steps, part in zip((0, 2, 3, 1), parts):
        all_rows[pl.ds(pl.multiple_of((e ^ steps) * rows, 16), rows), :] = part[...]
    flags = all_rows[:, data:]
    before = lax.broadcasted_iota(jnp.int32, (tokens, tokens), 0)
    after = lax.broadcasted_iota(jnp.int32, (tokens, tokens), 1)
    count = contract(flags, (before <= after).astype(F32).astype(BF16), 0, 0)[:cap]
    here = contract(flags, (before == after).astype(F32).astype(BF16), 0, 0)[:cap]
    slot = lax.broadcasted_iota(jnp.int32, (cap, tokens), 0).astype(F32)
    pick = jnp.where((count - 1.0 == slot) & (here > 0.5), 1.0, 0.0).astype(BF16)
    slots_ref[...] = jnp.dot(pick, all_rows[:, :data], preferred_element_type=F32).astype(BF16)
    pick_ref[...] = jnp.zeros_like(pick_ref)
    pick_ref[:, :tokens] = pick


def add_quarter(steps, blocks, x_ref, dz_ref, weights):
    piece = blocks[0].shape[1] // 2
    columns = pl.ds(pl.multiple_of((lax.axis_index("et") ^ steps) * piece, 128), piece)
    start = 0
    for block in blocks:
        rows = pl.ds(start, block.shape[0])
        x_ref[rows, columns] = block[:, :piece]
        dz_ref[rows, columns] = block[:, piece:]
        start += block.shape[0]
    wg_ref, wu_ref, wd_ref = weights
    x, dz = x_ref[:, columns], dz_ref[:, columns]
    return (
        contract(x, wg_ref[:, columns], 1, 1),
        contract(x, wu_ref[:, columns], 1, 1),
        contract(dz, wd_ref[:, columns], 1, 1),
    )


def first_kernel(*refs):
    weights, (x_ref, dz_ref, *sums) = refs[12:15], refs[15:]
    for steps in range(3):
        parts = add_quarter(steps, refs[4 * steps : 4 * steps + 4], x_ref, dz_ref, weights)
        for out, part in zip(sums, parts):
            out[...] = out[...] + part if steps else part


def half_terms(other, gate_grad, up_grad, weights, half):
    side = lax.axis_index("et") % 2 ^ other
    columns = pl.ds(pl.multiple_of(side * half, 128), half)
    terms = contract(gate_grad, weights[0][:, columns], 1, 0)
    return terms + contract(up_grad, weights[1][:, columns], 1, 0)


def third_kernel(*refs):
    both, weights, olds, outs = refs[:4], refs[4:7], refs[9:12], refs[12:]
    x_ref, dz_ref, act_ref, gg_ref, ug_ref, grads_ref, away_ref = outs
    slots = x_ref.shape[0]
    parts = add_quarter(3, both, x_ref, dz_ref, weights)
    gate, upper, act_grad = (old[...] + part for old, part in zip(olds, parts))
    sigmoid_gate = jax.nn.sigmoid(gate)
    silu_gate = gate * sigmoid_gate
    gate_grad = (act_grad * upper * sigmoid_gate * (1.0 + gate * (1.0 - sigmoid_gate))).astype(BF16)
    up_grad = (act_grad * silu_gate).astype(BF16)
    gg_ref[...] = gate_grad
    ug_ref[...] = up_grad
    act_ref[...] = (silu_gate * upper).astype(BF16)
    grads_ref[:slots, :] = gate_grad
    grads_ref[slots:, :] = up_grad
    away_ref[...] = half_terms(1, gate_grad, up_grad, weights, away_ref.shape[1]).astype(BF16)


def own_terms_kernel(grads_ref, wg_ref, wu_ref, out_ref):
    slots, half = out_ref.shape
    grads = grads_ref[:slots, :], grads_ref[slots:, :]
    out_ref[...] = half_terms(0, *grads, (wg_ref, wu_ref), half)


def pair_kernel(own_ref, other_ref, pick_ref, *outs):
    cap, half = outs[0].shape
    for k, out in enumerate(outs):
        rows = pl.ds(k * cap, cap)
        out[:, :half] = (own_ref[rows, :] + other_ref[rows, :].astype(F32)).astype(BF16)
    for out in outs[1::2]:
        out[:, half:] = pick_ref[...]


def add_kernel(left_ref, right_ref, out_ref, ready_ref):
    out_ref[...] = (left_ref[...].astype(F32) + right_ref[...].astype(F32)).astype(BF16)
    ready_ref[...] = jnp.zeros_like(ready_ref)


def expand_kernel(own_ref, ready_ref, *refs):
    others, outs, tokens_ref = refs[:2], refs[2:6], refs[6]
    rows, half = outs[0].shape
    e = lax.axis_index("et")
    total = own_ref[:, :half].astype(F32)
    for other in others:
        total += other[:, :half].astype(F32)
    tokens_ref[...] = contract(own_ref[:, half:], total.astype(BF16), 0, 0).astype(BF16)
    for steps, out in enumerate(outs):
        out[...] = tokens_ref[pl.ds(pl.multiple_of((e ^ steps) * rows, 16), rows), :]


def finish_kernel(own_ref, core_ref, chip_ref, both_ref, out_ref):
    half = own_ref.shape[1]
    core = lax.axis_index("et") % 2
    mine = own_ref[...].astype(F32) + chip_ref[...].astype(F32)
    out_ref[:, pl.ds(pl.multiple_of(core * half, 128), half)] = mine.astype(BF16)
    theirs = core_ref[...].astype(F32) + both_ref[...].astype(F32)
    out_ref[:, pl.ds(pl.multiple_of((1 - core) * half, 128), half)] = theirs.astype(BF16)


def swap(value, axis, steps):
    return lax.ppermute(value, axis, spread(steps))


def hand(value, pipe_size, steps):
    pairs = [
        (4 * p + z, 4 * ((p - 1) % pipe_size) + (z ^ steps)) for p in range(pipe_size) for z in range(4)
    ]
    return lax.ppermute(value, ("pipe", "dp"), pairs)


def on_device_four(tokens, out_grad, top_ids, route_probs, w_gate, w_up, w_down):
    rows, width = tokens.shape[2:]
    hidden = w_gate.shape[1]
    top = top_ids.shape[3]
    pipe_size = lax.axis_size("pipe")
    cap = 2 * rows
    slots = 4 * cap
    piece, half = width // 4, width // 2

    packed = call(
        pack_kernel,
        [like((rows, 2 * piece + FLAG))] * 4,
        tokens[0, 0],
        out_grad[0, 0],
        top_ids[0, 0].T,
        route_probs[0, 0].T,
        scratch=[
            pltpu.VMEM((rows, width), BF16),
            pltpu.VMEM((rows, width), BF16),
            pltpu.VMEM((top, rows), jnp.int32),
            pltpu.VMEM((top, rows), F32),
            pltpu.SemaphoreType.DMA((4,)),
        ],
        space=HBM,
    )
    arrived = [packed[0]] + [swap(packed[s], "et", s) for s in (2, 3, 1)]
    weights = call(
        stage_kernel,
        [like((hidden, width))] * 3,
        w_gate[0],
        w_up[0],
        w_down[0],
        scratch=[pltpu.SemaphoreType.DMA((9,))],
        space=HBM,
    )
    arrived, weights = lax.optimization_barrier((arrived, weights))
    slot_block, pick = call(
        compact_kernel,
        [like((cap, 2 * piece)), like((cap, FLAG))],
        *arrived,
        scratch=[pltpu.VMEM((4 * rows, 2 * piece + FLAG), BF16)],
    )
    diag = swap(slot_block, "dp", 3)
    near = swap(slot_block, "dp", 1)
    far = swap(slot_block, "dp", 2)
    own = [diag, near, far, slot_block]
    chip = [swap(block, "et", 2) for block in own]
    core = [swap(block, "et", 1) for block in own]
    both = [swap(block, "et", 1) for block in chip]
    wide, sums = [like((slots, width))] * 2, [like((slots, hidden), F32)] * 3
    state = call(first_kernel, wide + sums, *own, *core, *chip, *weights, vmem=32)
    x, dz, act, gate_grad, up_grad, grads, away = call(
        third_kernel,
        wide + [like((slots, hidden))] * 3 + [like((2 * slots, hidden)), like((slots, half))],
        *both,
        *weights,
        *state,
        vmem=32,
        aliases={7: 0, 8: 1},
    )
    theirs = swap(away, "et", 1)
    (own_terms,) = call(
        own_terms_kernel,
        [like((slots, half), F32)],
        grads,
        *weights[:2],
        flops=4 * slots * hidden * half,
        vmem=32,
    )
    to_last, to_near, to_far, home = call(
        pair_kernel,
        [like((cap, half)), like((cap, half + FLAG)), like((cap, half)), like((cap, half + FLAG))],
        own_terms,
        theirs,
        pick,
    )
    from_last = swap(to_last, "dp", 1)
    home = hand(home, pipe_size, 0)
    from_near = hand(to_near, pipe_size, 1)
    to_far, ready = call(
        add_kernel, [like((cap, half)), like((8, 128), F32)], to_far, from_last
    )
    x, dz, act, gate_grad, up_grad, ready = lax.optimization_barrier(
        (x, dz, act, gate_grad, up_grad, ready)
    )
    grad_gate = contract(gate_grad, x, 0, 0).astype(BF16)
    grad_up = contract(up_grad, x, 0, 0).astype(BF16)
    from_far = hand(to_far, pipe_size, 2)
    from_far, grad_gate, grad_up = lax.optimization_barrier((from_far, grad_gate, grad_up))
    by_token = call(
        expand_kernel,
        [like((rows, half))] * 4,
        home,
        ready,
        from_far,
        from_near,
        scratch=[pltpu.VMEM((FLAG, half), BF16)],
    )
    back = [by_token[0]] + [swap(by_token[s], "et", s) for s in (1, 2, 3)]
    (handed,) = call(finish_kernel, [like((rows, width))], *back)
    grad_down = contract(act, dz, 0, 0).astype(BF16)
    return (handed[None, None], grad_gate[None], grad_up[None], grad_down[None])


def solution(mesh):
    placed = (
        P("pipe", "dp", "et", None),
        P("pipe", "dp", "et", None),
        P("pipe", "dp", "et", None),
        P("pipe", "dp", "et", None),
        P("pipe", ("dp", "et"), None),
        P("pipe", ("dp", "et"), None),
        P("pipe", ("dp", "et"), None),
    )
    four = mesh.shape["et"] == 4 and mesh.shape["dp"] == 4
    return jax.shard_map(
        on_device_four if four else on_device_any,
        mesh=mesh,
        in_specs=placed,
        out_specs=(
            P("pipe", "dp", "et", None),
            P("pipe", ("dp", "et"), None),
            P("pipe", ("dp", "et"), None),
            P("pipe", ("dp", "et"), None),
        ),
        check_vma=False,
    )
```

```python
import functools

import jax
import jax.numpy as jnp
from jax import lax
from jax.experimental import pallas as pl
from jax.experimental.pallas import tpu as pltpu
from jax.sharding import PartitionSpec as P

FLAG = 128
BF16 = jnp.bfloat16
F32 = jnp.float32
VMEM = pl.BlockSpec(memory_space=pltpu.VMEM)
HBM = pl.BlockSpec(memory_space=pltpu.HBM)


def from_behind(value, axis, steps):
    count = lax.axis_size(axis)
    pairs = [(source, (source + steps) % count) for source in range(count)]
    return lax.ppermute(value, axis, pairs)


def slot_layout(routed, capacity):
    flags = routed.astype(jnp.int32)
    position = jnp.cumsum(flags, axis=-1, dtype=jnp.int32) - 1
    slot_ids = jnp.arange(capacity, dtype=jnp.int32)
    matches = (position[:, None, :] == slot_ids[None, :, None]) & routed[:, None, :]
    token_ids = jnp.arange(routed.shape[-1], dtype=jnp.int32)
    source = jnp.sum(jnp.where(matches, token_ids[None, None, :], 0), axis=-1)
    filled = jnp.any(matches, axis=-1)
    return (source, filled, position)


def gather_slots(rows, source, filled):
    picked = jnp.take_along_axis(rows, source[:, :, None], axis=1)
    return jnp.where(filled[:, :, None], picked, jnp.zeros_like(picked))


def contract(left, right, left_dim, right_dim):
    return lax.dot_general(
        left, right, (((left_dim,), (right_dim,)), ((), ())), preferred_element_type=F32
    )


def on_device_any(tokens, out_grad, top_ids, route_probs, w_gate, w_up, w_down):
    tok_dev = tokens.shape[2]
    model_width = tokens.shape[3]
    et_size = lax.axis_size("et")
    dp_size = lax.axis_size("dp")
    group_tokens = tok_dev * et_size
    capacity = group_tokens // 2
    token_rows = tokens[0, 0]
    chosen = top_ids[0, 0] == 0
    routed_flag = jnp.any(chosen, axis=-1).astype(BF16)
    route_weight = jnp.sum(jnp.where(chosen, route_probs[0, 0], F32(0.0)), axis=-1)
    scaled_rows = (route_weight[:, None] * out_grad[0, 0].astype(F32)).astype(BF16)
    group_x, group_dz, group_flag = (
        lax.all_gather(token_rows, "et", axis=0, tiled=True),
        lax.all_gather(scaled_rows, "et", axis=0, tiled=True),
        lax.all_gather(routed_flag, "et", axis=0, tiled=True),
    )
    routed = group_flag[None, :] > 0
    source, filled, position = slot_layout(routed, capacity)
    own_x = gather_slots(group_x[None], source, filled)
    own_dz = gather_slots(group_dz[None], source, filled)
    all_x, all_dz = (
        lax.all_gather(own_x, "dp", axis=0, tiled=True),
        lax.all_gather(own_dz, "dp", axis=0, tiled=True),
    )
    own_position = position[0]
    own_routed = routed[0]
    slot_x = all_x.reshape(dp_size * capacity, model_width)
    slot_dz = all_dz.reshape(dp_size * capacity, model_width)
    gate_rows = w_gate[0]
    up_rows = w_up[0]
    down_rows = w_down[0]
    gate = contract(slot_x, gate_rows, 1, 1)
    upper = contract(slot_x, up_rows, 1, 1)
    sigmoid_gate = jax.nn.sigmoid(gate)
    silu_gate = gate * sigmoid_gate
    act = (silu_gate * upper).astype(BF16)
    act_grad = contract(slot_dz, down_rows, 1, 1)
    gate_grad = (act_grad * upper * sigmoid_gate * (1.0 + gate * (1.0 - sigmoid_gate))).astype(BF16)
    up_grad = (act_grad * silu_gate).astype(BF16)
    grad_down = contract(act, slot_dz, 0, 0).astype(BF16)
    grad_gate = contract(gate_grad, slot_x, 0, 0).astype(BF16)
    grad_up = contract(up_grad, slot_x, 0, 0).astype(BF16)
    hidden_terms = contract(gate_grad, gate_rows, 1, 0) + contract(up_grad, up_rows, 1, 0)
    rounded = hidden_terms.astype(BF16).reshape(dp_size, capacity, model_width)
    hidden_sum = lax.psum_scatter(rounded, "et", scatter_dimension=1, tiled=True)
    slot_share = lax.psum_scatter(hidden_sum, "dp", scatter_dimension=0, tiled=True)
    slot_grad = lax.all_gather(slot_share, "et", axis=1, tiled=True)[0]
    start = lax.axis_index("et") * tok_dev
    my_position = lax.dynamic_slice_in_dim(own_position, start, tok_dev)
    my_routed = lax.dynamic_slice_in_dim(own_routed, start, tok_dev)
    picked = jnp.take(slot_grad, jnp.maximum(my_position, 0), axis=0)
    input_grad = jnp.where(my_routed[:, None], picked, jnp.zeros_like(picked))
    handed = from_behind(input_grad[None, None], "pipe", -1)
    return (handed, grad_gate[None], grad_up[None], grad_down[None])


def call(kernel, outs, *args, scratch=(), flops=0, vmem=16, space=VMEM, aliases=None):
    moved = 0
    if space is HBM or flops:
        moved = sum(a.size * a.dtype.itemsize for a in args)
        moved += sum(o.size * o.dtype.itemsize for o in outs)
    if space is HBM:
        args = [pltpu.with_memory_space_constraint(a, pltpu.HBM) for a in args]
    return pl.pallas_call(
        kernel,
        out_shape=outs,
        in_specs=[space] * len(args),
        out_specs=[VMEM] * len(outs),
        scratch_shapes=list(scratch),
        input_output_aliases=aliases or {},
        compiler_params=pltpu.CompilerParams(vmem_limit_bytes=vmem * 2**20),
        cost_estimate=pl.CostEstimate(flops=flops, bytes_accessed=moved, transcendentals=0),
    )(*args)


def like(shape, dtype=BF16):
    return jax.ShapeDtypeStruct(shape, dtype)


def spread(steps):
    return [(e, e ^ steps) for e in range(4)]


def bring(sources, targets, sems):
    copies = [
        pltpu.make_async_copy(source, target, sems.at[i])
        for i, (source, target) in enumerate(zip(sources, targets))
    ]
    for copy in copies:
        copy.start()
    return copies


def stage_kernel(*refs):
    weights, (pair_ref, down_ref, sems) = refs[:3], refs[3:]
    hidden = down_ref.shape[0]
    padded = pair_ref.shape[0] // 2
    third = hidden // 3
    sources, targets = [], []
    for weight, out, start in zip(weights, (pair_ref, pair_ref, down_ref), (0, padded, 0)):
        for part in range(3):
            sources.append(weight.at[pl.ds(part * third, third), :])
            targets.append(out.at[pl.ds(start + part * third, third), :])
    copies = bring(sources, targets, sems)
    for start in (0, padded):
        rows = pl.ds(start + hidden, padded - hidden)
        pair_ref[rows, :] = jnp.zeros((padded - hidden, pair_ref.shape[1]), BF16)
    for copy in copies:
        copy.wait()


def pack_kernel(*refs):
    outs, (x_ref, dz_ref, ids_ref, probs_ref, sems) = refs[4:8], refs[8:]
    for copy in bring(refs[:4], refs[8:12], sems):
        copy.wait()
    rows, width = x_ref.shape
    piece = width // 4
    e = lax.axis_index("et")
    chosen = ids_ref[...] == 0
    weight_row = jnp.sum(jnp.where(chosen, probs_ref[...], 0.0), axis=0, keepdims=True)
    flag_row = jnp.max(jnp.where(chosen, 1.0, 0.0), axis=0, keepdims=True)
    on_diagonal = lax.broadcasted_iota(jnp.int32, (rows, rows), 0) == lax.broadcasted_iota(
        jnp.int32, (rows, rows), 1
    )
    weight = jnp.sum(jnp.where(on_diagonal, weight_row, 0.0), axis=1, keepdims=True)
    flag = jnp.sum(jnp.where(on_diagonal, flag_row, 0.0), axis=1, keepdims=True)
    for steps, out in enumerate(outs):
        start = pl.multiple_of((e ^ steps) * piece, 128)
        out[:, :piece] = x_ref[:, pl.ds(start, piece)]
        out[:, piece : 2 * piece] = (weight * dz_ref[:, pl.ds(start, piece)].astype(F32)).astype(BF16)
        out[:, 2 * piece :] = jnp.broadcast_to(flag, (rows, FLAG)).astype(BF16)


def compact_kernel(*refs):
    parts, (slots_ref, pick_ref, all_rows) = refs[:4], refs[4:]
    rows, wide = parts[0].shape
    tokens = 4 * rows
    data = wide - FLAG
    cap = slots_ref.shape[0]
    e = lax.axis_index("et")
    for steps, part in enumerate(parts):
        all_rows[pl.ds(pl.multiple_of((e ^ steps) * rows, 16), rows), :] = part[...]
    flags = all_rows[:, data:]
    before = lax.broadcasted_iota(jnp.int32, (tokens, tokens), 0)
    after = lax.broadcasted_iota(jnp.int32, (tokens, tokens), 1)
    count = contract(flags, (before <= after).astype(F32).astype(BF16), 0, 0)[:cap]
    here = contract(flags, (before == after).astype(F32).astype(BF16), 0, 0)[:cap]
    slot = lax.broadcasted_iota(jnp.int32, (cap, tokens), 0).astype(F32)
    pick = jnp.where((count - 1.0 == slot) & (here > 0.5), 1.0, 0.0).astype(BF16)
    slots_ref[...] = jnp.dot(pick, all_rows[:, :data], preferred_element_type=F32).astype(BF16)
    pick_ref[...] = jnp.zeros_like(pick_ref)
    pick_ref[:, :tokens] = pick


def place_quarter(steps, blocks, x_ref, dz_ref):
    cap, wide = blocks[0].shape
    piece = wide // 2
    columns = pl.ds(pl.multiple_of((lax.axis_index("et") ^ steps) * piece, 128), piece)
    for k, block in enumerate(blocks):
        rows = pl.ds(k * cap, cap)
        x_ref[rows, columns] = block[:, :piece]
        dz_ref[rows, columns] = block[:, piece:]
    return columns


def products(columns, x_ref, dz_ref, weights):
    pair_ref, down_ref = weights
    return (
        contract(x_ref[:, columns], pair_ref[:, columns], 1, 1),
        contract(dz_ref[:, columns], down_ref[:, columns], 1, 1),
    )


def first_kernel(*refs):
    own, core, chip, weights = refs[:4], refs[4:8], refs[8:12], refs[12:14]
    x_ref, dz_ref, *sums = refs[14:]
    place_quarter(0, own, x_ref, dz_ref)
    place_quarter(1, core, x_ref, dz_ref)
    quarter = place_quarter(2, chip, x_ref, dz_ref)
    half = x_ref.shape[1] // 2
    row = pl.ds(pl.multiple_of(lax.axis_index("et") // 2 * half, 128), half)
    parts = products(row, x_ref, dz_ref, weights)
    for out, part, other in zip(sums, parts, products(quarter, x_ref, dz_ref, weights)):
        out[...] = part + other


def half_terms(other, grads, pair_ref, half):
    side = lax.axis_index("et") % 2 ^ other
    return contract(grads, pair_ref[:, pl.ds(pl.multiple_of(side * half, 128), half)], 1, 0)


def third_kernel(*refs):
    both, weights, olds, outs = refs[:4], refs[4:6], refs[8:10], refs[10:]
    x_ref, dz_ref, act_ref, gg_ref, ug_ref, grads_ref, away_ref = outs
    hidden = gg_ref.shape[1]
    padded = grads_ref.shape[1] // 2
    columns = place_quarter(3, both, x_ref, dz_ref)
    pair, act_grad = (
        old[...] + part for old, part in zip(olds, products(columns, x_ref, dz_ref, weights))
    )
    gate, upper = pair[:, :hidden], pair[:, padded : padded + hidden]
    sigmoid_gate = jax.nn.sigmoid(gate)
    silu_gate = gate * sigmoid_gate
    gate_grad = (act_grad * upper * sigmoid_gate * (1.0 + gate * (1.0 - sigmoid_gate))).astype(BF16)
    up_grad = (act_grad * silu_gate).astype(BF16)
    grads_ref[...] = jnp.zeros_like(grads_ref)
    grads_ref[:, :hidden] = gate_grad
    grads_ref[:, padded : padded + hidden] = up_grad
    away_ref[...] = half_terms(1, grads_ref[...], weights[0], away_ref.shape[1]).astype(BF16)
    gg_ref[...] = gate_grad
    ug_ref[...] = up_grad
    act_ref[...] = (silu_gate * upper).astype(BF16)


def own_terms_kernel(grads_ref, pair_ref, out_ref):
    out_ref[...] = half_terms(0, grads_ref[...], pair_ref, out_ref.shape[1])


def pair_kernel(own_ref, other_ref, pick_ref, *outs):
    cap, half = outs[0].shape
    for k, out in enumerate(outs):
        rows = pl.ds(k * cap, cap)
        out[:, :half] = (own_ref[rows, :] + other_ref[rows, :].astype(F32)).astype(BF16)
    outs[3][:, half:] = pick_ref[...]


def add_kernel(left_ref, right_ref, out_ref, ready_ref):
    out_ref[...] = (left_ref[...].astype(F32) + right_ref[...].astype(F32)).astype(BF16)
    ready_ref[...] = jnp.zeros_like(ready_ref)


def expand_kernel(own_ref, ready_ref, *refs):
    others, outs, tokens_ref = refs[:2], refs[2:6], refs[6]
    rows, half = outs[0].shape
    e = lax.axis_index("et")
    total = own_ref[:, :half].astype(F32)
    for other in others:
        total += other[...].astype(F32)
    tokens_ref[...] = contract(own_ref[:, half:], total.astype(BF16), 0, 0).astype(BF16)
    for steps, out in enumerate(outs):
        out[...] = tokens_ref[pl.ds(pl.multiple_of((e ^ steps) * rows, 16), rows), :]


def finish_kernel(own_ref, core_ref, chip_ref, both_ref, out_ref):
    half = own_ref.shape[1]
    core = lax.axis_index("et") % 2
    mine = own_ref[...].astype(F32) + chip_ref[...].astype(F32)
    out_ref[:, pl.ds(pl.multiple_of(core * half, 128), half)] = mine.astype(BF16)
    theirs = core_ref[...].astype(F32) + both_ref[...].astype(F32)
    out_ref[:, pl.ds(pl.multiple_of((1 - core) * half, 128), half)] = theirs.astype(BF16)


def swap(value, axis, steps):
    return lax.ppermute(value, axis, spread(steps))


def hand(value, pipe_size, steps):
    pairs = [
        (4 * p + z, 4 * ((p - 1) % pipe_size) + (z ^ steps)) for p in range(pipe_size) for z in range(4)
    ]
    return lax.ppermute(value, ("pipe", "dp"), pairs)


def on_device_four(tokens, out_grad, top_ids, route_probs, w_gate, w_up, w_down):
    rows, width = tokens.shape[2:]
    hidden = w_gate.shape[1]
    top = top_ids.shape[3]
    pipe_size = lax.axis_size("pipe")
    cap = 2 * rows
    slots = 4 * cap
    piece, half = width // 4, width // 2
    padded = -(-hidden // 128) * 128

    packed = call(
        pack_kernel,
        [like((rows, 2 * piece + FLAG))] * 4,
        tokens[0, 0],
        out_grad[0, 0],
        top_ids[0, 0].T,
        route_probs[0, 0].T,
        scratch=[
            pltpu.VMEM((rows, width), BF16),
            pltpu.VMEM((rows, width), BF16),
            pltpu.VMEM((top, rows), jnp.int32),
            pltpu.VMEM((top, rows), F32),
            pltpu.SemaphoreType.DMA((4,)),
        ],
        space=HBM,
    )
    arrived = [packed[0]] + [swap(packed[s], "et", s) for s in (1, 2, 3)]
    weights = call(
        stage_kernel,
        [like((2 * padded, width)), like((hidden, width))],
        w_gate[0],
        w_up[0],
        w_down[0],
        scratch=[pltpu.SemaphoreType.DMA((9,))],
        space=HBM,
    )
    arrived, weights = lax.optimization_barrier((arrived, weights))
    slot_block, pick = call(
        compact_kernel,
        [like((cap, 2 * piece)), like((cap, FLAG))],
        *arrived,
        scratch=[pltpu.VMEM((4 * rows, 2 * piece + FLAG), BF16)],
    )
    diag = swap(slot_block, "dp", 3)
    near = swap(slot_block, "dp", 1)
    far = swap(slot_block, "dp", 2)
    own = [diag, near, far, slot_block]
    chip = [swap(block, "et", 2) for block in own]
    core = [swap(block, "et", 1) for block in own]
    both = [swap(block, "et", 1) for block in chip]
    wide = [like((slots, width))] * 2
    sums = [like((slots, 2 * padded), F32), like((slots, hidden), F32)]
    state = call(first_kernel, wide + sums, *own, *core, *chip, *weights, vmem=32)
    x, dz, act, gate_grad, up_grad, grads, away = call(
        third_kernel,
        wide + [like((slots, hidden))] * 3 + [like((slots, 2 * padded)), like((slots, half))],
        *both,
        *weights,
        *state,
        vmem=32,
        aliases={6: 0, 7: 1},
    )
    theirs = swap(away, "et", 1)
    (own_terms,) = call(
        own_terms_kernel,
        [like((slots, half), F32)],
        grads,
        weights[0],
        flops=4 * slots * hidden * half,
        vmem=32,
    )
    to_last, to_near, to_far, home = call(
        pair_kernel,
        [like((cap, half))] * 3 + [like((cap, half + FLAG))],
        own_terms,
        theirs,
        pick,
    )
    from_last = swap(to_last, "dp", 1)
    home = hand(home, pipe_size, 0)
    from_near = hand(to_near, pipe_size, 1)
    to_far, ready = call(
        add_kernel, [like((cap, half)), like((8, 128), F32)], to_far, from_last
    )
    x, dz, act, gate_grad, up_grad, ready = lax.optimization_barrier(
        (x, dz, act, gate_grad, up_grad, ready)
    )
    grad_gate = contract(gate_grad, x, 0, 0).astype(BF16)
    grad_up = contract(up_grad, x, 0, 0).astype(BF16)
    from_far = hand(to_far, pipe_size, 2)
    from_far, grad_gate, grad_up = lax.optimization_barrier((from_far, grad_gate, grad_up))
    by_token = call(
        expand_kernel,
        [like((rows, half))] * 4,
        home,
        ready,
        from_far,
        from_near,
        scratch=[pltpu.VMEM((FLAG, half), BF16)],
    )
    back = [by_token[0]] + [swap(by_token[s], "et", s) for s in (1, 2, 3)]
    (handed,) = call(finish_kernel, [like((rows, width))], *back)
    grad_down = contract(act, dz, 0, 0).astype(BF16)
    return (handed[None, None], grad_gate[None], grad_up[None], grad_down[None])


def solution(mesh):
    placed = (
        P("pipe", "dp", "et", None),
        P("pipe", "dp", "et", None),
        P("pipe", "dp", "et", None),
        P("pipe", "dp", "et", None),
        P("pipe", ("dp", "et"), None),
        P("pipe", ("dp", "et"), None),
        P("pipe", ("dp", "et"), None),
    )
    four = mesh.shape["et"] == 4 and mesh.shape["dp"] == 4
    return jax.shard_map(
        on_device_four if four else on_device_any,
        mesh=mesh,
        in_specs=placed,
        out_specs=(
            P("pipe", "dp", "et", None),
            P("pipe", ("dp", "et"), None),
            P("pipe", ("dp", "et"), None),
            P("pipe", ("dp", "et"), None),
        ),
        check_vma=False,
    )
```

```python
import functools

import jax
import jax.numpy as jnp
from jax import lax
from jax.experimental import pallas as pl
from jax.experimental.pallas import tpu as pltpu
from jax.sharding import PartitionSpec as P

FLAG = 128
BF16 = jnp.bfloat16
F32 = jnp.float32
VMEM = pl.BlockSpec(memory_space=pltpu.VMEM)
HBM = pl.BlockSpec(memory_space=pltpu.HBM)


def from_behind(value, axis, steps):
    count = lax.axis_size(axis)
    pairs = [(source, (source + steps) % count) for source in range(count)]
    return lax.ppermute(value, axis, pairs)


def slot_layout(routed, capacity):
    flags = routed.astype(jnp.int32)
    position = jnp.cumsum(flags, axis=-1, dtype=jnp.int32) - 1
    slot_ids = jnp.arange(capacity, dtype=jnp.int32)
    matches = (position[:, None, :] == slot_ids[None, :, None]) & routed[:, None, :]
    token_ids = jnp.arange(routed.shape[-1], dtype=jnp.int32)
    source = jnp.sum(jnp.where(matches, token_ids[None, None, :], 0), axis=-1)
    filled = jnp.any(matches, axis=-1)
    return (source, filled, position)


def gather_slots(rows, source, filled):
    picked = jnp.take_along_axis(rows, source[:, :, None], axis=1)
    return jnp.where(filled[:, :, None], picked, jnp.zeros_like(picked))


def contract(left, right, left_dim, right_dim):
    return lax.dot_general(
        left, right, (((left_dim,), (right_dim,)), ((), ())), preferred_element_type=F32
    )


def on_device_any(tokens, out_grad, top_ids, route_probs, w_gate, w_up, w_down):
    tok_dev = tokens.shape[2]
    model_width = tokens.shape[3]
    et_size = lax.axis_size("et")
    dp_size = lax.axis_size("dp")
    group_tokens = tok_dev * et_size
    capacity = group_tokens // 2
    token_rows = tokens[0, 0]
    chosen = top_ids[0, 0] == 0
    routed_flag = jnp.any(chosen, axis=-1).astype(BF16)
    route_weight = jnp.sum(jnp.where(chosen, route_probs[0, 0], F32(0.0)), axis=-1)
    scaled_rows = (route_weight[:, None] * out_grad[0, 0].astype(F32)).astype(BF16)
    group_x, group_dz, group_flag = (
        lax.all_gather(token_rows, "et", axis=0, tiled=True),
        lax.all_gather(scaled_rows, "et", axis=0, tiled=True),
        lax.all_gather(routed_flag, "et", axis=0, tiled=True),
    )
    routed = group_flag[None, :] > 0
    source, filled, position = slot_layout(routed, capacity)
    own_x = gather_slots(group_x[None], source, filled)
    own_dz = gather_slots(group_dz[None], source, filled)
    all_x, all_dz = (
        lax.all_gather(own_x, "dp", axis=0, tiled=True),
        lax.all_gather(own_dz, "dp", axis=0, tiled=True),
    )
    own_position = position[0]
    own_routed = routed[0]
    slot_x = all_x.reshape(dp_size * capacity, model_width)
    slot_dz = all_dz.reshape(dp_size * capacity, model_width)
    gate_rows = w_gate[0]
    up_rows = w_up[0]
    down_rows = w_down[0]
    gate = contract(slot_x, gate_rows, 1, 1)
    upper = contract(slot_x, up_rows, 1, 1)
    sigmoid_gate = jax.nn.sigmoid(gate)
    silu_gate = gate * sigmoid_gate
    act = (silu_gate * upper).astype(BF16)
    act_grad = contract(slot_dz, down_rows, 1, 1)
    gate_grad = (act_grad * upper * sigmoid_gate * (1.0 + gate * (1.0 - sigmoid_gate))).astype(BF16)
    up_grad = (act_grad * silu_gate).astype(BF16)
    grad_down = contract(act, slot_dz, 0, 0).astype(BF16)
    grad_gate = contract(gate_grad, slot_x, 0, 0).astype(BF16)
    grad_up = contract(up_grad, slot_x, 0, 0).astype(BF16)
    hidden_terms = contract(gate_grad, gate_rows, 1, 0) + contract(up_grad, up_rows, 1, 0)
    rounded = hidden_terms.astype(BF16).reshape(dp_size, capacity, model_width)
    hidden_sum = lax.psum_scatter(rounded, "et", scatter_dimension=1, tiled=True)
    slot_share = lax.psum_scatter(hidden_sum, "dp", scatter_dimension=0, tiled=True)
    slot_grad = lax.all_gather(slot_share, "et", axis=1, tiled=True)[0]
    start = lax.axis_index("et") * tok_dev
    my_position = lax.dynamic_slice_in_dim(own_position, start, tok_dev)
    my_routed = lax.dynamic_slice_in_dim(own_routed, start, tok_dev)
    picked = jnp.take(slot_grad, jnp.maximum(my_position, 0), axis=0)
    input_grad = jnp.where(my_routed[:, None], picked, jnp.zeros_like(picked))
    handed = from_behind(input_grad[None, None], "pipe", -1)
    return (handed, grad_gate[None], grad_up[None], grad_down[None])


def call(kernel, outs, *args, scratch=(), flops=0, vmem=16, space=VMEM, aliases=None):
    moved = 0
    if space is HBM or flops:
        moved = sum(a.size * a.dtype.itemsize for a in args)
        moved += sum(o.size * o.dtype.itemsize for o in outs)
    if space is HBM:
        args = [pltpu.with_memory_space_constraint(a, pltpu.HBM) for a in args]
    return pl.pallas_call(
        kernel,
        out_shape=outs,
        in_specs=[space] * len(args),
        out_specs=[VMEM] * len(outs),
        scratch_shapes=list(scratch),
        input_output_aliases=aliases or {},
        compiler_params=pltpu.CompilerParams(vmem_limit_bytes=vmem * 2**20),
        cost_estimate=pl.CostEstimate(flops=flops, bytes_accessed=moved, transcendentals=0),
    )(*args)


def like(shape, dtype=BF16):
    return jax.ShapeDtypeStruct(shape, dtype)


def spread(steps):
    return [(e, e ^ steps) for e in range(4)]


def bring(sources, targets, sems):
    copies = [
        pltpu.make_async_copy(source, target, sems.at[i])
        for i, (source, target) in enumerate(zip(sources, targets))
    ]
    for copy in copies:
        copy.start()
    return copies


def stage_kernel(*refs):
    weights, (pair_ref, down_ref, sems) = refs[:3], refs[3:]
    hidden = down_ref.shape[0]
    padded = pair_ref.shape[0] // 2
    third = hidden // 3
    sources, targets = [], []
    for weight, out, start in zip(weights, (pair_ref, pair_ref, down_ref), (0, padded, 0)):
        for part in range(3):
            sources.append(weight.at[pl.ds(part * third, third), :])
            targets.append(out.at[pl.ds(start + part * third, third), :])
    copies = bring(sources, targets, sems)
    for start in (0, padded):
        rows = pl.ds(start + hidden, padded - hidden)
        pair_ref[rows, :] = jnp.zeros((padded - hidden, pair_ref.shape[1]), BF16)
    for copy in copies:
        copy.wait()


def pack_kernel(*refs):
    outs, (x_ref, dz_ref, ids_ref, probs_ref, sems) = refs[4:8], refs[8:]
    for copy in bring(refs[:4], refs[8:12], sems):
        copy.wait()
    rows, width = x_ref.shape
    piece = width // 4
    e = lax.axis_index("et")
    chosen = ids_ref[...] == 0
    weight_row = jnp.sum(jnp.where(chosen, probs_ref[...], 0.0), axis=0, keepdims=True)
    flag_row = jnp.max(jnp.where(chosen, 1.0, 0.0), axis=0, keepdims=True)
    on_diagonal = lax.broadcasted_iota(jnp.int32, (rows, rows), 0) == lax.broadcasted_iota(
        jnp.int32, (rows, rows), 1
    )
    weight = jnp.sum(jnp.where(on_diagonal, weight_row, 0.0), axis=1, keepdims=True)
    flag = jnp.sum(jnp.where(on_diagonal, flag_row, 0.0), axis=1, keepdims=True)
    for steps, out in enumerate(outs):
        start = pl.multiple_of((e ^ steps) * piece, 128)
        out[:, :piece] = x_ref[:, pl.ds(start, piece)]
        out[:, piece : 2 * piece] = (weight * dz_ref[:, pl.ds(start, piece)].astype(F32)).astype(BF16)
        out[:, 2 * piece :] = jnp.broadcast_to(flag, (rows, FLAG)).astype(BF16)


def compact_kernel(*refs):
    parts, (slots_ref, pick_ref, all_rows) = refs[:4], refs[4:]
    rows, wide = parts[0].shape
    tokens = 4 * rows
    data = wide - FLAG
    cap = slots_ref.shape[0]
    e = lax.axis_index("et")
    for steps, part in enumerate(parts):
        all_rows[pl.ds(pl.multiple_of((e ^ steps) * rows, 16), rows), :] = part[...]
    flags = all_rows[:, data:]
    before = lax.broadcasted_iota(jnp.int32, (tokens, tokens), 0)
    after = lax.broadcasted_iota(jnp.int32, (tokens, tokens), 1)
    count = contract(flags, (before <= after).astype(F32).astype(BF16), 0, 0)[:cap]
    here = contract(flags, (before == after).astype(F32).astype(BF16), 0, 0)[:cap]
    slot = lax.broadcasted_iota(jnp.int32, (cap, tokens), 0).astype(F32)
    pick = jnp.where((count - 1.0 == slot) & (here > 0.5), 1.0, 0.0).astype(BF16)
    slots_ref[...] = jnp.dot(pick, all_rows[:, :data], preferred_element_type=F32).astype(BF16)
    pick_ref[...] = jnp.zeros_like(pick_ref)
    pick_ref[:, :tokens] = pick


def place_quarter(steps, blocks, x_ref, dz_ref):
    cap, wide = blocks[0].shape
    piece = wide // 2
    columns = pl.ds(pl.multiple_of((lax.axis_index("et") ^ steps) * piece, 128), piece)
    for k, block in enumerate(blocks):
        rows = pl.ds(k * cap, cap)
        x_ref[rows, columns] = block[:, :piece]
        dz_ref[rows, columns] = block[:, piece:]
    return columns


def products(columns, x_ref, dz_ref, weights):
    pair_ref, down_ref = weights
    return (
        contract(x_ref[:, columns], pair_ref[:, columns], 1, 1),
        contract(dz_ref[:, columns], down_ref[:, columns], 1, 1),
    )


def first_kernel(*refs):
    own, core, chip, weights = refs[:4], refs[4:8], refs[8:12], refs[12:14]
    x_ref, dz_ref, *sums = refs[14:]
    place_quarter(0, own, x_ref, dz_ref)
    place_quarter(1, core, x_ref, dz_ref)
    quarter = place_quarter(2, chip, x_ref, dz_ref)
    half = x_ref.shape[1] // 2
    row = pl.ds(pl.multiple_of(lax.axis_index("et") // 2 * half, 128), half)
    parts = products(row, x_ref, dz_ref, weights)
    for out, part, other in zip(sums, parts, products(quarter, x_ref, dz_ref, weights)):
        out[...] = part + other


def half_terms(other, grads, pair_ref, half):
    side = lax.axis_index("et") % 2 ^ other
    return contract(grads, pair_ref[:, pl.ds(pl.multiple_of(side * half, 128), half)], 1, 0)


def third_kernel(*refs):
    both, weights, olds, outs = refs[:4], refs[4:6], refs[8:10], refs[10:]
    x_ref, dz_ref, act_ref, gg_ref, ug_ref, grads_ref, last_ref, away_ref = outs
    hidden = gg_ref.shape[1]
    padded = grads_ref.shape[1] // 2
    columns = place_quarter(3, both, x_ref, dz_ref)
    pair, act_grad = (
        old[...] + part for old, part in zip(olds, products(columns, x_ref, dz_ref, weights))
    )
    gate, upper = pair[:, :hidden], pair[:, padded : padded + hidden]
    sigmoid_gate = jax.nn.sigmoid(gate)
    silu_gate = gate * sigmoid_gate
    gate_grad = (act_grad * upper * sigmoid_gate * (1.0 + gate * (1.0 - sigmoid_gate))).astype(BF16)
    up_grad = (act_grad * silu_gate).astype(BF16)
    grads_ref[...] = jnp.zeros_like(grads_ref)
    grads_ref[:, :hidden] = gate_grad
    grads_ref[:, padded : padded + hidden] = up_grad
    cap = last_ref.shape[0]
    away = half_terms(1, grads_ref[...], weights[0], away_ref.shape[1]).astype(BF16)
    last_ref[...] = away[:cap]
    away_ref[...] = away[cap:]
    gg_ref[...] = gate_grad
    ug_ref[...] = up_grad
    act_ref[...] = (silu_gate * upper).astype(BF16)


def own_terms_kernel(grads_ref, pair_ref, out_ref):
    out_ref[...] = half_terms(0, grads_ref[...], pair_ref, out_ref.shape[1])


def last_kernel(own_ref, other_ref, out_ref):
    own = own_ref[: out_ref.shape[0], :]
    out_ref[...] = (own + other_ref[...].astype(F32)).astype(BF16)


def pair_kernel(own_ref, other_ref, pick_ref, *refs):
    outs, ready_ref = refs[:3], refs[3]
    cap, half = outs[0].shape
    ready_ref[...] = jnp.zeros_like(ready_ref)
    for k, out in enumerate(outs):
        rows = pl.ds(k * cap, cap)
        own = own_ref[pl.ds((k + 1) * cap, cap), :]
        out[:, :half] = (own + other_ref[rows, :].astype(F32)).astype(BF16)
    outs[2][:, half:] = pick_ref[...]


def add_kernel(left_ref, right_ref, first_ref, out_ref, ready_ref):
    out_ref[...] = (left_ref[...].astype(F32) + right_ref[...].astype(F32)).astype(BF16)
    ready_ref[...] = first_ref[...]


def expand_kernel(own_ref, ready_ref, *refs):
    others, outs, tokens_ref = refs[:2], refs[2:6], refs[6]
    rows, half = outs[0].shape
    e = lax.axis_index("et")
    total = own_ref[:, :half].astype(F32)
    for other in others:
        total += other[...].astype(F32)
    tokens_ref[...] = contract(own_ref[:, half:], total.astype(BF16), 0, 0).astype(BF16)
    for steps, out in enumerate(outs):
        out[...] = tokens_ref[pl.ds(pl.multiple_of((e ^ steps) * rows, 16), rows), :]


def finish_kernel(own_ref, core_ref, chip_ref, both_ref, out_ref):
    half = own_ref.shape[1]
    core = lax.axis_index("et") % 2
    mine = own_ref[...].astype(F32) + chip_ref[...].astype(F32)
    out_ref[:, pl.ds(pl.multiple_of(core * half, 128), half)] = mine.astype(BF16)
    theirs = core_ref[...].astype(F32) + both_ref[...].astype(F32)
    out_ref[:, pl.ds(pl.multiple_of((1 - core) * half, 128), half)] = theirs.astype(BF16)


def swap(value, axis, steps):
    return lax.ppermute(value, axis, spread(steps))


def hand(value, pipe_size, steps):
    pairs = [
        (4 * p + z, 4 * ((p - 1) % pipe_size) + (z ^ steps)) for p in range(pipe_size) for z in range(4)
    ]
    return lax.ppermute(value, ("pipe", "dp"), pairs)


def on_device_four(tokens, out_grad, top_ids, route_probs, w_gate, w_up, w_down):
    rows, width = tokens.shape[2:]
    hidden = w_gate.shape[1]
    top = top_ids.shape[3]
    pipe_size = lax.axis_size("pipe")
    cap = 2 * rows
    slots = 4 * cap
    piece, half = width // 4, width // 2
    padded = -(-hidden // 128) * 128

    packed = call(
        pack_kernel,
        [like((rows, 2 * piece + FLAG))] * 4,
        tokens[0, 0],
        out_grad[0, 0],
        top_ids[0, 0].T,
        route_probs[0, 0].T,
        scratch=[
            pltpu.VMEM((rows, width), BF16),
            pltpu.VMEM((rows, width), BF16),
            pltpu.VMEM((top, rows), jnp.int32),
            pltpu.VMEM((top, rows), F32),
            pltpu.SemaphoreType.DMA((4,)),
        ],
        space=HBM,
    )
    arrived = [packed[0]] + [swap(packed[s], "et", s) for s in (1, 2, 3)]
    weights = call(
        stage_kernel,
        [like((2 * padded, width)), like((hidden, width))],
        w_gate[0],
        w_up[0],
        w_down[0],
        scratch=[pltpu.SemaphoreType.DMA((9,))],
        space=HBM,
    )
    arrived, weights = lax.optimization_barrier((arrived, weights))
    slot_block, pick = call(
        compact_kernel,
        [like((cap, 2 * piece)), like((cap, FLAG))],
        *arrived,
        scratch=[pltpu.VMEM((4 * rows, 2 * piece + FLAG), BF16)],
    )
    diag = swap(slot_block, "dp", 3)
    near = swap(slot_block, "dp", 1)
    far = swap(slot_block, "dp", 2)
    own = [diag, near, far, slot_block]
    chip = [swap(block, "et", 2) for block in own]
    core = [swap(block, "et", 1) for block in own]
    both = [swap(block, "et", 1) for block in chip]
    wide = [like((slots, width))] * 2
    sums = [like((slots, 2 * padded), F32), like((slots, hidden), F32)]
    state = call(first_kernel, wide + sums, *own, *core, *chip, *weights, vmem=32)
    x, dz, act, gate_grad, up_grad, grads, away_last, away = call(
        third_kernel,
        wide
        + [like((slots, hidden))] * 3
        + [like((slots, 2 * padded)), like((cap, half)), like((3 * cap, half))],
        *both,
        *weights,
        *state,
        vmem=32,
        aliases={6: 0, 7: 1},
    )
    their_last = swap(away_last, "et", 1)
    theirs = swap(away, "et", 1)
    (own_terms,) = call(
        own_terms_kernel,
        [like((slots, half), F32)],
        grads,
        weights[0],
        flops=4 * slots * hidden * half,
        vmem=32,
    )
    (to_last,) = call(last_kernel, [like((cap, half))], own_terms, their_last)
    to_near, to_far, home, first = call(
        pair_kernel,
        [like((cap, half))] * 2 + [like((cap, half + FLAG)), like((8, 128), F32)],
        own_terms,
        theirs,
        pick,
    )
    from_last = swap(to_last, "dp", 1)
    home = hand(home, pipe_size, 0)
    from_near = hand(to_near, pipe_size, 1)
    x, gate_grad, first = lax.optimization_barrier((x, gate_grad, first))
    grad_gate = contract(gate_grad, x, 0, 0).astype(BF16)
    from_last, grad_gate = lax.optimization_barrier((from_last, grad_gate))
    to_far, ready = call(
        add_kernel, [like((cap, half)), like((8, 128), F32)], to_far, from_last, first
    )
    x, dz, act, up_grad, ready = lax.optimization_barrier((x, dz, act, up_grad, ready))
    grad_up = contract(up_grad, x, 0, 0).astype(BF16)
    from_far = hand(to_far, pipe_size, 2)
    from_far, grad_up = lax.optimization_barrier((from_far, grad_up))
    by_token = call(
        expand_kernel,
        [like((rows, half))] * 4,
        home,
        ready,
        from_far,
        from_near,
        scratch=[pltpu.VMEM((FLAG, half), BF16)],
    )
    back = [by_token[0]] + [swap(by_token[s], "et", s) for s in (1, 2, 3)]
    (handed,) = call(finish_kernel, [like((rows, width))], *back)
    grad_down = contract(act, dz, 0, 0).astype(BF16)
    return (handed[None, None], grad_gate[None], grad_up[None], grad_down[None])


def solution(mesh):
    placed = (
        P("pipe", "dp", "et", None),
        P("pipe", "dp", "et", None),
        P("pipe", "dp", "et", None),
        P("pipe", "dp", "et", None),
        P("pipe", ("dp", "et"), None),
        P("pipe", ("dp", "et"), None),
        P("pipe", ("dp", "et"), None),
    )
    four = mesh.shape["et"] == 4 and mesh.shape["dp"] == 4
    return jax.shard_map(
        on_device_four if four else on_device_any,
        mesh=mesh,
        in_specs=placed,
        out_specs=(
            P("pipe", "dp", "et", None),
            P("pipe", ("dp", "et"), None),
            P("pipe", ("dp", "et"), None),
            P("pipe", ("dp", "et"), None),
        ),
        check_vma=False,
    )
```

```python
import functools

import jax
import jax.numpy as jnp
from jax import lax
from jax.experimental import pallas as pl
from jax.experimental.pallas import tpu as pltpu
from jax.sharding import PartitionSpec as P

FLAG = 128
BF16 = jnp.bfloat16
F32 = jnp.float32
VMEM = pl.BlockSpec(memory_space=pltpu.VMEM)
HBM = pl.BlockSpec(memory_space=pltpu.HBM)


def from_behind(value, axis, steps):
    count = lax.axis_size(axis)
    pairs = [(source, (source + steps) % count) for source in range(count)]
    return lax.ppermute(value, axis, pairs)


def slot_layout(routed, capacity):
    flags = routed.astype(jnp.int32)
    position = jnp.cumsum(flags, axis=-1, dtype=jnp.int32) - 1
    slot_ids = jnp.arange(capacity, dtype=jnp.int32)
    matches = (position[:, None, :] == slot_ids[None, :, None]) & routed[:, None, :]
    token_ids = jnp.arange(routed.shape[-1], dtype=jnp.int32)
    source = jnp.sum(jnp.where(matches, token_ids[None, None, :], 0), axis=-1)
    filled = jnp.any(matches, axis=-1)
    return (source, filled, position)


def gather_slots(rows, source, filled):
    picked = jnp.take_along_axis(rows, source[:, :, None], axis=1)
    return jnp.where(filled[:, :, None], picked, jnp.zeros_like(picked))


def contract(left, right, left_dim, right_dim):
    return lax.dot_general(
        left, right, (((left_dim,), (right_dim,)), ((), ())), preferred_element_type=F32
    )


def on_device_any(tokens, out_grad, top_ids, route_probs, w_gate, w_up, w_down):
    tok_dev = tokens.shape[2]
    model_width = tokens.shape[3]
    et_size = lax.axis_size("et")
    dp_size = lax.axis_size("dp")
    group_tokens = tok_dev * et_size
    capacity = group_tokens // 2
    token_rows = tokens[0, 0]
    chosen = top_ids[0, 0] == 0
    routed_flag = jnp.any(chosen, axis=-1).astype(BF16)
    route_weight = jnp.sum(jnp.where(chosen, route_probs[0, 0], F32(0.0)), axis=-1)
    scaled_rows = (route_weight[:, None] * out_grad[0, 0].astype(F32)).astype(BF16)
    group_x, group_dz, group_flag = (
        lax.all_gather(token_rows, "et", axis=0, tiled=True),
        lax.all_gather(scaled_rows, "et", axis=0, tiled=True),
        lax.all_gather(routed_flag, "et", axis=0, tiled=True),
    )
    routed = group_flag[None, :] > 0
    source, filled, position = slot_layout(routed, capacity)
    own_x = gather_slots(group_x[None], source, filled)
    own_dz = gather_slots(group_dz[None], source, filled)
    all_x, all_dz = (
        lax.all_gather(own_x, "dp", axis=0, tiled=True),
        lax.all_gather(own_dz, "dp", axis=0, tiled=True),
    )
    own_position = position[0]
    own_routed = routed[0]
    slot_x = all_x.reshape(dp_size * capacity, model_width)
    slot_dz = all_dz.reshape(dp_size * capacity, model_width)
    gate_rows = w_gate[0]
    up_rows = w_up[0]
    down_rows = w_down[0]
    gate = contract(slot_x, gate_rows, 1, 1)
    upper = contract(slot_x, up_rows, 1, 1)
    sigmoid_gate = jax.nn.sigmoid(gate)
    silu_gate = gate * sigmoid_gate
    act = (silu_gate * upper).astype(BF16)
    act_grad = contract(slot_dz, down_rows, 1, 1)
    gate_grad = (act_grad * upper * sigmoid_gate * (1.0 + gate * (1.0 - sigmoid_gate))).astype(BF16)
    up_grad = (act_grad * silu_gate).astype(BF16)
    grad_down = contract(act, slot_dz, 0, 0).astype(BF16)
    grad_gate = contract(gate_grad, slot_x, 0, 0).astype(BF16)
    grad_up = contract(up_grad, slot_x, 0, 0).astype(BF16)
    hidden_terms = contract(gate_grad, gate_rows, 1, 0) + contract(up_grad, up_rows, 1, 0)
    rounded = hidden_terms.astype(BF16).reshape(dp_size, capacity, model_width)
    hidden_sum = lax.psum_scatter(rounded, "et", scatter_dimension=1, tiled=True)
    slot_share = lax.psum_scatter(hidden_sum, "dp", scatter_dimension=0, tiled=True)
    slot_grad = lax.all_gather(slot_share, "et", axis=1, tiled=True)[0]
    start = lax.axis_index("et") * tok_dev
    my_position = lax.dynamic_slice_in_dim(own_position, start, tok_dev)
    my_routed = lax.dynamic_slice_in_dim(own_routed, start, tok_dev)
    picked = jnp.take(slot_grad, jnp.maximum(my_position, 0), axis=0)
    input_grad = jnp.where(my_routed[:, None], picked, jnp.zeros_like(picked))
    handed = from_behind(input_grad[None, None], "pipe", -1)
    return (handed, grad_gate[None], grad_up[None], grad_down[None])


def call(kernel, outs, *args, scratch=(), flops=0, vmem=16, space=VMEM, aliases=None):
    moved = 0
    if space is HBM or flops:
        moved = sum(a.size * a.dtype.itemsize for a in args)
        moved += sum(o.size * o.dtype.itemsize for o in outs)
    if space is HBM:
        args = [pltpu.with_memory_space_constraint(a, pltpu.HBM) for a in args]
    return pl.pallas_call(
        kernel,
        out_shape=outs,
        in_specs=[space] * len(args),
        out_specs=[VMEM] * len(outs),
        scratch_shapes=list(scratch),
        input_output_aliases=aliases or {},
        compiler_params=pltpu.CompilerParams(vmem_limit_bytes=vmem * 2**20),
        cost_estimate=pl.CostEstimate(flops=flops, bytes_accessed=moved, transcendentals=0),
    )(*args)


def like(shape, dtype=BF16):
    return jax.ShapeDtypeStruct(shape, dtype)


def spread(steps):
    return [(e, e ^ steps) for e in range(4)]


def bring(sources, targets, sems):
    copies = [
        pltpu.make_async_copy(source, target, sems.at[i])
        for i, (source, target) in enumerate(zip(sources, targets))
    ]
    for copy in copies:
        copy.start()
    return copies


def stage_kernel(*refs):
    weights, (pair_ref, down_ref, sems) = refs[:3], refs[3:]
    hidden = down_ref.shape[0]
    padded = pair_ref.shape[0] // 2
    third = hidden // 3
    sources, targets = [], []
    for weight, out, start in zip(weights, (pair_ref, pair_ref, down_ref), (0, padded, 0)):
        for part in range(3):
            sources.append(weight.at[pl.ds(part * third, third), :])
            targets.append(out.at[pl.ds(start + part * third, third), :])
    copies = bring(sources, targets, sems)
    for start in (0, padded):
        rows = pl.ds(start + hidden, padded - hidden)
        pair_ref[rows, :] = jnp.zeros((padded - hidden, pair_ref.shape[1]), BF16)
    for copy in copies:
        copy.wait()


def pack_kernel(*refs):
    outs, (x_ref, dz_ref, ids_ref, probs_ref, sems) = refs[4:8], refs[8:]
    for copy in bring(refs[:4], refs[8:12], sems):
        copy.wait()
    rows, width = x_ref.shape
    piece = width // 4
    e = lax.axis_index("et")
    chosen = ids_ref[...] == 0
    weight_row = jnp.sum(jnp.where(chosen, probs_ref[...], 0.0), axis=0, keepdims=True)
    flag_row = jnp.max(jnp.where(chosen, 1.0, 0.0), axis=0, keepdims=True)
    on_diagonal = lax.broadcasted_iota(jnp.int32, (rows, rows), 0) == lax.broadcasted_iota(
        jnp.int32, (rows, rows), 1
    )
    weight = jnp.sum(jnp.where(on_diagonal, weight_row, 0.0), axis=1, keepdims=True)
    flag = jnp.sum(jnp.where(on_diagonal, flag_row, 0.0), axis=1, keepdims=True)
    for steps, out in enumerate(outs):
        start = pl.multiple_of((e ^ steps) * piece, 128)
        out[:, :piece] = x_ref[:, pl.ds(start, piece)]
        out[:, piece : 2 * piece] = (weight * dz_ref[:, pl.ds(start, piece)].astype(F32)).astype(BF16)
        out[:, 2 * piece :] = jnp.broadcast_to(flag, (rows, FLAG)).astype(BF16)


def compact_kernel(*refs):
    parts, (slots_ref, pick_ref, all_rows) = refs[:4], refs[4:]
    rows, wide = parts[0].shape
    tokens = 4 * rows
    data = wide - FLAG
    cap = slots_ref.shape[0]
    e = lax.axis_index("et")
    for steps, part in enumerate(parts):
        all_rows[pl.ds(pl.multiple_of((e ^ steps) * rows, 16), rows), :] = part[...]
    flags = all_rows[:, data:]
    before = lax.broadcasted_iota(jnp.int32, (tokens, tokens), 0)
    after = lax.broadcasted_iota(jnp.int32, (tokens, tokens), 1)
    count = contract(flags, (before <= after).astype(F32).astype(BF16), 0, 0)[:cap]
    here = contract(flags, (before == after).astype(F32).astype(BF16), 0, 0)[:cap]
    slot = lax.broadcasted_iota(jnp.int32, (cap, tokens), 0).astype(F32)
    pick = jnp.where((count - 1.0 == slot) & (here > 0.5), 1.0, 0.0).astype(BF16)
    slots_ref[...] = jnp.dot(pick, all_rows[:, :data], preferred_element_type=F32).astype(BF16)
    pick_ref[...] = jnp.zeros_like(pick_ref)
    pick_ref[:, :tokens] = pick


def place_quarter(steps, blocks, x_ref, dz_ref):
    cap, wide = blocks[0].shape
    piece = wide // 2
    columns = pl.ds(pl.multiple_of((lax.axis_index("et") ^ steps) * piece, 128), piece)
    for k, block in enumerate(blocks):
        rows = pl.ds(k * cap, cap)
        x_ref[rows, columns] = block[:, :piece]
        dz_ref[rows, columns] = block[:, piece:]
    return columns


def products(columns, x_ref, dz_ref, weights):
    pair_ref, down_ref = weights
    return (
        contract(x_ref[:, columns], pair_ref[:, columns], 1, 1),
        contract(dz_ref[:, columns], down_ref[:, columns], 1, 1),
    )


def first_kernel(*refs):
    own, core, chip, weights = refs[:4], refs[4:8], refs[8:12], refs[12:14]
    x_ref, dz_ref, *sums = refs[14:]
    place_quarter(0, own, x_ref, dz_ref)
    place_quarter(1, core, x_ref, dz_ref)
    quarter = place_quarter(2, chip, x_ref, dz_ref)
    half = x_ref.shape[1] // 2
    row = pl.ds(pl.multiple_of(lax.axis_index("et") // 2 * half, 128), half)
    parts = products(row, x_ref, dz_ref, weights)
    for out, part, other in zip(sums, parts, products(quarter, x_ref, dz_ref, weights)):
        out[...] = part + other


def half_terms(other, grads, pair_ref, half):
    side = lax.axis_index("et") % 2 ^ other
    return contract(grads, pair_ref[:, pl.ds(pl.multiple_of(side * half, 128), half)], 1, 0)


def third_kernel(*refs):
    both, weights, olds, outs = refs[:4], refs[4:6], refs[8:10], refs[10:]
    x_ref, dz_ref, act_ref, gg_ref, ug_ref, grads_ref, away_ref = outs
    hidden = gg_ref.shape[1]
    padded = grads_ref.shape[1] // 2
    columns = place_quarter(3, both, x_ref, dz_ref)
    pair, act_grad = (
        old[...] + part for old, part in zip(olds, products(columns, x_ref, dz_ref, weights))
    )
    gate, upper = pair[:, :hidden], pair[:, padded : padded + hidden]
    sigmoid_gate = jax.nn.sigmoid(gate)
    silu_gate = gate * sigmoid_gate
    gate_grad = (act_grad * upper * sigmoid_gate * (1.0 + gate * (1.0 - sigmoid_gate))).astype(BF16)
    up_grad = (act_grad * silu_gate).astype(BF16)
    grads_ref[...] = jnp.zeros_like(grads_ref)
    grads_ref[:, :hidden] = gate_grad
    grads_ref[:, padded : padded + hidden] = up_grad
    away_ref[...] = half_terms(1, grads_ref[...], weights[0], away_ref.shape[1]).astype(BF16)
    gg_ref[...] = gate_grad
    ug_ref[...] = up_grad
    act_ref[...] = (silu_gate * upper).astype(BF16)


def own_terms_kernel(grads_ref, pair_ref, out_ref):
    out_ref[...] = half_terms(0, grads_ref[...], pair_ref, out_ref.shape[1])


def pair_kernel(own_ref, other_ref, pick_ref, *outs):
    cap, half = outs[0].shape
    for k, out in enumerate(outs):
        rows = pl.ds(k * cap, cap)
        out[:, :half] = (own_ref[rows, :] + other_ref[rows, :].astype(F32)).astype(BF16)
    outs[3][:, half:] = pick_ref[...]


def add_kernel(left_ref, right_ref, out_ref, ready_ref):
    out_ref[...] = (left_ref[...].astype(F32) + right_ref[...].astype(F32)).astype(BF16)
    ready_ref[...] = jnp.zeros_like(ready_ref)


def expand_kernel(own_ref, ready_ref, *refs):
    others, outs, tokens_ref = refs[:2], refs[2:6], refs[6]
    rows, half = outs[0].shape
    e = lax.axis_index("et")
    total = own_ref[:, :half].astype(F32)
    for other in others:
        total += other[...].astype(F32)
    tokens_ref[...] = contract(own_ref[:, half:], total.astype(BF16), 0, 0).astype(BF16)
    for steps, out in enumerate(outs):
        out[...] = tokens_ref[pl.ds(pl.multiple_of((e ^ steps) * rows, 16), rows), :]


def finish_kernel(own_ref, chip_ref, both_ref, core_ref, out_ref):
    half = own_ref.shape[1]
    core = lax.axis_index("et") % 2
    mine = own_ref[...].astype(F32) + chip_ref[...].astype(F32)
    out_ref[:, pl.ds(pl.multiple_of(core * half, 128), half)] = mine.astype(BF16)
    theirs = core_ref[...].astype(F32) + both_ref[...].astype(F32)
    out_ref[:, pl.ds(pl.multiple_of((1 - core) * half, 128), half)] = theirs.astype(BF16)


def swap(value, axis, steps):
    return lax.ppermute(value, axis, spread(steps))


def hand(value, pipe_size, steps):
    pairs = [
        (4 * p + z, 4 * ((p - 1) % pipe_size) + (z ^ steps)) for p in range(pipe_size) for z in range(4)
    ]
    return lax.ppermute(value, ("pipe", "dp"), pairs)


def on_device_four(tokens, out_grad, top_ids, route_probs, w_gate, w_up, w_down):
    rows, width = tokens.shape[2:]
    hidden = w_gate.shape[1]
    top = top_ids.shape[3]
    pipe_size = lax.axis_size("pipe")
    cap = 2 * rows
    slots = 4 * cap
    piece, half = width // 4, width // 2
    padded = -(-hidden // 128) * 128

    packed = call(
        pack_kernel,
        [like((rows, 2 * piece + FLAG))] * 4,
        tokens[0, 0],
        out_grad[0, 0],
        top_ids[0, 0].T,
        route_probs[0, 0].T,
        scratch=[
            pltpu.VMEM((rows, width), BF16),
            pltpu.VMEM((rows, width), BF16),
            pltpu.VMEM((top, rows), jnp.int32),
            pltpu.VMEM((top, rows), F32),
            pltpu.SemaphoreType.DMA((4,)),
        ],
        space=HBM,
    )
    arrived = [packed[0]] + [swap(packed[s], "et", s) for s in (1, 2, 3)]
    weights = call(
        stage_kernel,
        [like((2 * padded, width)), like((hidden, width))],
        w_gate[0],
        w_up[0],
        w_down[0],
        scratch=[pltpu.SemaphoreType.DMA((9,))],
        space=HBM,
    )
    arrived, weights = lax.optimization_barrier((arrived, weights))
    slot_block, pick = call(
        compact_kernel,
        [like((cap, 2 * piece)), like((cap, FLAG))],
        *arrived,
        scratch=[pltpu.VMEM((4 * rows, 2 * piece + FLAG), BF16)],
    )
    diag = swap(slot_block, "dp", 3)
    near = swap(slot_block, "dp", 1)
    far = swap(slot_block, "dp", 2)
    own = [diag, near, far, slot_block]
    chip = [swap(block, "et", 2) for block in own]
    core = [swap(block, "et", 1) for block in own]
    both = [swap(block, "et", 1) for block in chip]
    wide = [like((slots, width))] * 2
    sums = [like((slots, 2 * padded), F32), like((slots, hidden), F32)]
    state = call(first_kernel, wide + sums, *own, *core, *chip, *weights, vmem=32)
    x, dz, act, gate_grad, up_grad, grads, away = call(
        third_kernel,
        wide + [like((slots, hidden))] * 3 + [like((slots, 2 * padded)), like((slots, half))],
        *both,
        *weights,
        *state,
        vmem=32,
        aliases={6: 0, 7: 1},
    )
    theirs = swap(away, "et", 1)
    (own_terms,) = call(
        own_terms_kernel,
        [like((slots, half), F32)],
        grads,
        weights[0],
        flops=4 * slots * hidden * half,
        vmem=32,
    )
    to_last, to_near, to_far, home = call(
        pair_kernel,
        [like((cap, half))] * 3 + [like((cap, half + FLAG))],
        own_terms,
        theirs,
        pick,
    )
    from_last = swap(to_last, "dp", 1)
    home = hand(home, pipe_size, 0)
    from_near = hand(to_near, pipe_size, 1)
    to_far, ready = call(
        add_kernel, [like((cap, half)), like((8, 128), F32)], to_far, from_last
    )
    x, dz, act, gate_grad, up_grad, ready = lax.optimization_barrier(
        (x, dz, act, gate_grad, up_grad, ready)
    )
    grad_gate = contract(gate_grad, x, 0, 0).astype(BF16)
    grad_up = contract(up_grad, x, 0, 0).astype(BF16)
    from_far = hand(to_far, pipe_size, 2)
    from_far, grad_gate, grad_up = lax.optimization_barrier((from_far, grad_gate, grad_up))
    by_token = call(
        expand_kernel,
        [like((rows, half))] * 4,
        home,
        ready,
        from_far,
        from_near,
        scratch=[pltpu.VMEM((FLAG, half), BF16)],
    )
    back = [by_token[0]] + [swap(by_token[s], "et", s) for s in (2, 3, 1)]
    (handed,) = call(finish_kernel, [like((rows, width))], *back)
    grad_down = contract(act, dz, 0, 0).astype(BF16)
    return (handed[None, None], grad_gate[None], grad_up[None], grad_down[None])


def solution(mesh):
    placed = (
        P("pipe", "dp", "et", None),
        P("pipe", "dp", "et", None),
        P("pipe", "dp", "et", None),
        P("pipe", "dp", "et", None),
        P("pipe", ("dp", "et"), None),
        P("pipe", ("dp", "et"), None),
        P("pipe", ("dp", "et"), None),
    )
    four = mesh.shape["et"] == 4 and mesh.shape["dp"] == 4
    return jax.shard_map(
        on_device_four if four else on_device_any,
        mesh=mesh,
        in_specs=placed,
        out_specs=(
            P("pipe", "dp", "et", None),
            P("pipe", ("dp", "et"), None),
            P("pipe", ("dp", "et"), None),
            P("pipe", ("dp", "et"), None),
        ),
        check_vma=False,
    )
```
